32 devices in a mesh: dp: 8 (over z, x), seq: 4 (over y, core).
Axes of the slice: x: 2, y: 2, z: 4, core: 2. Of those that a mesh axis runs over, the one named last changes fastest.
Arguments:
- hidden_in: bfloat16 [64, 512, 768], P('dp', 'seq'), may hold values from -6 to 6
- segment_ids: int32 [64, 512], P('dp'), may hold values from 0 to 512, as said below
- row_lengths: int32 [64], P('dp'), may hold values from 256 to 512
- teacher_scores: bfloat16 [64, 12, 512, 512], P('dp', None, 'seq'), may hold values from -8 to 8
- teacher_hidden: bfloat16 [64, 512, 768], P('dp', 'seq'), may hold values from -6 to 6
- w_query: float32 [768, 768], P(None, 'dp'), may hold values from -0.625 to 0.625
- w_key: float32 [768, 768], P(None, 'dp'), may hold values from -0.625 to 0.625
- w_value: float32 [768, 768], P(None, 'dp'), may hold values from -0.21875 to 0.21875
- w_out: float32 [768, 768], P(None, 'dp'), may hold values from -0.875 to 0.875
- w_up: float32 [768, 3072], P(None, 'dp'), may hold values from -0.21875 to 0.21875
- w_down: float32 [3072, 768], P(None, 'dp'), may hold values from -0.109375 to 0.109375
- b_query: bfloat16 [768], P('dp'), may hold values from -2 to 2
- b_value: bfloat16 [768], P('dp'), may hold values from -2 to 2
- b_out: bfloat16 [768], P('dp'), may hold values from -2 to 2
- b_up: bfloat16 [3072], P('dp'), may hold values from -2 to 2
- b_down: bfloat16 [768], P('dp'), may hold values from -2 to 2
- norm1_gain: bfloat16 [768], P('dp'), may hold values from 0.5 to 1.5
- norm1_bias: bfloat16 [768], P('dp'), may hold values from -2 to 2
- norm2_gain: bfloat16 [768], P('dp'), may hold values from 0.5 to 1.5
- norm2_bias: bfloat16 [768], P('dp'), may hold values from -2 to 2
- clip_in: bfloat16 [768], P('dp'), may hold values from 1 to 3
- clip_ctx: bfloat16 [768], P('dp'), may hold values from 0.5 to 2
- clip_mid: bfloat16 [768], P('dp'), may hold values from 1 to 3
- clip_hid: bfloat16 [3072], P('dp'), may hold values from 0.5 to 2
Outputs:
- output: bfloat16 [64, 512, 768], P('dp', 'seq')
- loss: float32 [], replicated
- grad_input: float32 [64, 512, 768], P('dp', 'seq')
- grad_w_query: float32 [768, 768], P(None, 'dp')
- grad_w_key: float32 [768, 768], P(None, 'dp')
- grad_w_value: float32 [768, 768], P(None, 'dp')
- grad_w_out: float32 [768, 768], P(None, 'dp')
- grad_w_up: float32 [768, 3072], P(None, 'dp')
- grad_w_down: float32 [3072, 768], P(None, 'dp')
- grad_b_query: float32 [768], P('dp')
- grad_b_value: float32 [768], P('dp')
- grad_b_out: float32 [768], P('dp')
- grad_b_up: float32 [3072], P('dp')
- grad_b_down: float32 [768], P('dp')
- grad_norm1_gain: float32 [768], P('dp')
- grad_norm1_bias: float32 [768], P('dp')
- grad_norm2_gain: float32 [768], P('dp')
- grad_norm2_bias: float32 [768], P('dp')
- grad_clip_in: float32 [768], P('dp')
- grad_clip_ctx: float32 [768], P('dp')
- grad_clip_mid: float32 [768], P('dp')
- grad_clip_hid: float32 [3072], P('dp')
The draws below stay inside these ranges and needn't reach their ends.
Inputs may be any that keep to these rules, and one draw needn't show every extreme that they name: `segment_ids`: within each row, document numbers start at 0 and never fall; positions at or after the row's length hold 512.
All inputs are finite; a program needn't handle non-finite values.
Results may differ from the reference program's by a relative error of at most 0.012.
Values may be sent and summed in bfloat16 or wider, within the bound.
A program may use at most 256 MiB of HBM per device.

```python
import math
import jax
import jax.numpy as jnp
from jax import lax

D = 768
HEADS = 12
HEAD_DIM = 64
FF = 3072
SEQ = 512
ROWS_DEV = 8
ROWS = 64
TOKENS = 32768


def draw_layout(key):
    pick_key, length_key, start_key = jax.random.split(key, 3)
    groups = ROWS // ROWS_DEV
    spans = jax.random.randint(pick_key, (groups,), 0, ROWS_DEV)
    local = jnp.arange(ROWS, dtype=jnp.int32) % ROWS_DEV
    group_span = jnp.repeat(spans, ROWS_DEV)
    is_span = local == group_span
    is_short = local == (group_span + 1) % ROWS_DEV
    lengths = jax.random.randint(length_key, (ROWS,), SEQ // 2, SEQ + 1)
    lengths = jnp.where(is_span, SEQ, jnp.where(is_short, SEQ // 2, lengths))
    positions = jnp.arange(SEQ, dtype=jnp.int32)
    starts = jax.random.randint(start_key, (ROWS, SEQ), 0, SEQ // 8) == 0
    starts = starts & (positions[None, :] > 0) & jnp.logical_not(is_span)[:, None]
    numbers = jnp.cumsum(starts.astype(jnp.int32), axis=1)
    numbers = jnp.where(positions[None, :] < lengths[:, None], numbers, SEQ)
    return (numbers.astype(jnp.int32), lengths.astype(jnp.int32))


def draw_segment_ids(key, part):
    shared = draw_layout(key)
    return shared[0]


def draw_row_lengths(key, part):
    shared = draw_layout(key)
    return shared[1]


def shard_levels(stream_key, shape, cuts, low, largest):
    level = 1.0
    for position, parts in cuts:
        heights = jax.random.uniform(jax.random.fold_in(jax.random.fold_in(stream_key, 6), position), (parts,), jnp.float32, low / len(cuts), largest / len(cuts))
        level = level * jnp.repeat(jnp.exp(heights), shape[position] // parts).reshape((-1,) + (1,) * (len(shape) - 1 - position))
    return level


def gaussian(stream_key, dims, width, most, cuts=(), kind=jnp.bfloat16):
    result = width * jax.random.normal(stream_key, dims, jnp.float32)
    if cuts:
        result = result * shard_levels(stream_key, dims, cuts, -0.22, 0.18)
    return jnp.clip(result, -most, most).astype(kind)


def setup_inputs(seed: int = 0) -> dict:
    arg_keys = jax.random.split(jax.random.key(seed), 25)
    return {
        "hidden_in": gaussian(arg_keys[0], (ROWS, SEQ, D), 1.0, 6.0, ((0, 8), (1, 4))),
        "segment_ids": draw_segment_ids(jax.random.fold_in(arg_keys[24], 71), 0),
        "row_lengths": draw_row_lengths(jax.random.fold_in(arg_keys[24], 71), 0),
        "teacher_scores": gaussian(arg_keys[3], (ROWS, HEADS, SEQ, SEQ), 2.0, 8.0, ((0, 8), (2, 4))),
        "teacher_hidden": gaussian(arg_keys[4], (ROWS, SEQ, D), 1.0, 6.0, ((0, 8), (1, 4))),
        "w_query": gaussian(arg_keys[5], (D, D), (D // 8) ** -0.5, 0.625, ((1, 8),), jnp.float32),
        "w_key": gaussian(arg_keys[6], (D, D), (D // 8) ** -0.5, 0.625, ((1, 8),), jnp.float32),
        "w_value": gaussian(arg_keys[7], (D, D), D ** -0.5, 0.21875, ((1, 8),), jnp.float32),
        "w_out": gaussian(arg_keys[8], (D, D), (D // 16) ** -0.5, 0.875, ((1, 8),), jnp.float32),
        "w_up": gaussian(arg_keys[9], (D, FF), D ** -0.5, 0.21875, ((1, 8),), jnp.float32),
        "w_down": gaussian(arg_keys[10], (FF, D), FF ** -0.5, 0.109375, ((1, 8),), jnp.float32),
        "b_query": gaussian(arg_keys[11], (D,), 0.3, 2.0, ((0, 8),)),
        "b_value": gaussian(arg_keys[12], (D,), 0.3, 2.0, ((0, 8),)),
        "b_out": gaussian(arg_keys[13], (D,), 0.3, 2.0, ((0, 8),)),
        "b_up": gaussian(arg_keys[14], (FF,), 0.3, 2.0, ((0, 8),)),
        "b_down": gaussian(arg_keys[15], (D,), 0.3, 2.0, ((0, 8),)),
        "norm1_gain": jnp.clip(1.0 + 0.1 * jax.random.normal(arg_keys[16], (D,), jnp.float32), 0.5, 1.5).astype(jnp.bfloat16),
        "norm1_bias": gaussian(arg_keys[17], (D,), 0.3, 2.0, ((0, 8),)),
        "norm2_gain": jnp.clip(1.0 + 0.1 * jax.random.normal(arg_keys[18], (D,), jnp.float32), 0.5, 1.5).astype(jnp.bfloat16),
        "norm2_bias": gaussian(arg_keys[19], (D,), 0.3, 2.0, ((0, 8),)),
        "clip_in": jnp.clip(jnp.exp(math.log(3.0) - 1.0986123 * jax.random.uniform(arg_keys[20], (D,), jnp.float32) ** shard_levels(arg_keys[20], (D,), ((0, 8),), -0.2, 0.2)), 1.0, 3.0).astype(jnp.bfloat16),
        "clip_ctx": jnp.clip(jnp.exp(math.log(2.0) - 1.3862944 * jax.random.uniform(arg_keys[21], (D,), jnp.float32) ** shard_levels(arg_keys[21], (D,), ((0, 8),), -0.2, 0.2)), 0.5, 2.0).astype(jnp.bfloat16),
        "clip_mid": jnp.clip(jnp.exp(math.log(3.0) - 1.0986123 * jax.random.uniform(arg_keys[22], (D,), jnp.float32) ** shard_levels(arg_keys[22], (D,), ((0, 8),), -0.2, 0.2)), 1.0, 3.0).astype(jnp.bfloat16),
        "clip_hid": jnp.clip(jnp.exp(math.log(2.0) - 1.3862944 * jax.random.uniform(arg_keys[23], (FF,), jnp.float32) ** shard_levels(arg_keys[23], (FF,), ((0, 8),), -0.2, 0.2)), 0.5, 2.0).astype(jnp.bfloat16),
    }


@jax.custom_vjp
def low(v):
    return lax.optimization_barrier(v.astype(jnp.bfloat16)).astype(jnp.float32)

@jax.custom_vjp
def low_back(v):
    return v

def low_keep(v):
    return (low(v), None)

def low_pass(kept, grad):
    return (grad,)

def back_keep(v):
    return (v, None)

def back_low(kept, grad):
    return (low(grad),)
low.defvjp(low_keep, low_pass)
low_back.defvjp(back_keep, back_low)
eps_norm = 1e-05
score_weight = 0.0625
negative = -1e+30
highest = lax.Precision.HIGHEST

def matmul_high(left, right):
    return jnp.dot(left, right, precision=highest, preferred_element_type=jnp.float32)

def soft_clip(value, bound):
    return bound * jnp.tanh(value / bound)

def layer_norm(value, gain, shift):
    centre = value - lax.optimization_barrier(jnp.mean(value, axis=-1, keepdims=True))
    return centre * lax.rsqrt(lax.optimization_barrier(jnp.mean(centre * centre, axis=-1, keepdims=True)) + eps_norm) * gain + shift

def binarize(latent):
    scale = lax.optimization_barrier(jnp.mean(jnp.abs(latent), axis=0))
    return low(scale * jnp.sign(latent))

def group_pass(weights, block):
    bin_query, bin_key, bin_value, bin_out, bin_up, bin_down, b_query, b_value, b_out, b_up, b_down, norm1_gain, norm1_bias, norm2_gain, norm2_bias, clip_in, clip_ctx, clip_mid, clip_hid = weights
    inputs, segments, lengths, targets, hidden_targets = block
    count = inputs.shape[0]
    flat = inputs.reshape(count * SEQ, D)
    inputs_low = low(soft_clip(flat, clip_in))
    query = low(low_back(matmul_high(inputs_low, bin_query) + b_query))
    keys = low(low_back(matmul_high(inputs_low, bin_key)))
    values = low(low_back(matmul_high(inputs_low, bin_value) + b_value))
    query_heads = query.reshape(count, SEQ, HEADS, HEAD_DIM)
    key_heads = keys.reshape(count, SEQ, HEADS, HEAD_DIM)
    value_heads = values.reshape(count, SEQ, HEADS, HEAD_DIM)
    scores = low_back(jnp.einsum('gqhd,gkhd->ghqk', query_heads, key_heads, precision=highest) * HEAD_DIM ** (-0.5))
    positions = jnp.arange(SEQ, dtype=jnp.int32)
    live = positions[None, :] < lengths[:, None]
    same = (segments[:, :, None] == segments[:, None, :])[:, None]
    counted = same & live[:, None, :, None] & live[:, None, None, :]
    teacher = targets.astype(jnp.float32)
    distill = 0.5 * score_weight * jnp.sum(jnp.where(counted, (scores - teacher) ** 2, 0.0))
    top = lax.optimization_barrier(jnp.max(jnp.where(same, scores, negative), axis=-1, keepdims=True))
    expo = jnp.exp(jnp.where(same, scores - top, negative))
    total = lax.optimization_barrier(jnp.sum(expo, axis=-1))
    accum = low_back(jnp.einsum('ghqk,gkhd->gqhd', low(expo), value_heads, precision=highest))
    context = (accum / jnp.transpose(total, (0, 2, 1))[..., None]).reshape(count * SEQ, D)
    context_low = low(soft_clip(context, clip_ctx))
    attended = low_back(matmul_high(context_low, bin_out) + b_out)
    normed = layer_norm(flat + attended, norm1_gain, norm1_bias)
    normed_low = low(soft_clip(normed, clip_mid))
    up_pre = low_back(matmul_high(normed_low, bin_up) + b_up)
    hidden_low = low(soft_clip(jax.nn.gelu(up_pre, approximate=False), clip_hid))
    branch = low_back(matmul_high(hidden_low, bin_down) + b_down)
    final = layer_norm(normed + branch, norm2_gain, norm2_bias)
    errors = jnp.where(live.reshape(-1)[:, None], final - hidden_targets.reshape(count * SEQ, D), 0.0)
    return (0.5 * jnp.sum(errors * errors) + distill, final.reshape(count, SEQ, D))

def reference(hidden_in, segment_ids, row_lengths, teacher_scores, teacher_hidden, w_query, w_key, w_value, w_out, w_up, w_down, b_query, b_value, b_out, b_up, b_down, norm1_gain, norm1_bias, norm2_gain, norm2_bias, clip_in, clip_ctx, clip_mid, clip_hid):
    params = tuple((p.astype(jnp.float32) for p in (w_query, w_key, w_value, w_out, w_up, w_down, b_query, b_value, b_out, b_up, b_down, norm1_gain, norm1_bias, norm2_gain, norm2_bias, clip_in, clip_ctx, clip_mid, clip_hid)))
    inputs = hidden_in.astype(jnp.float32)
    group = math.gcd(ROWS, max(1, 4096 // SEQ))
    steps_count = ROWS // group
    blocks_int = (segment_ids.reshape(steps_count, group, SEQ), row_lengths.reshape(steps_count, group))
    teacher_blocks = (teacher_scores.astype(jnp.float32).reshape(steps_count, group, HEADS, SEQ, SEQ), teacher_hidden.astype(jnp.float32).reshape(steps_count, group, SEQ, D))

    def objective(params, inputs):
        binary = tuple((binarize(w) for w in params[:6]))
        weights = binary + tuple(params[6:])

        def step(carry, block):
            value, final = group_pass(weights, block)
            return (carry + value, final)
        xs = (inputs.reshape(steps_count, group, SEQ, D), blocks_int[0], blocks_int[1], teacher_blocks[0], teacher_blocks[1])
        total, finals = lax.scan(jax.checkpoint(step), jnp.zeros((), jnp.float32), xs)
        return (total, finals)
    total, pull, finals = jax.vjp(objective, params, inputs, has_aux=True)
    param_grads, input_grad = pull(jnp.ones_like(total))
    output = finals.reshape(ROWS, SEQ, D).astype(jnp.bfloat16)
    return (output, total / TOKENS, input_grad) + tuple(param_grads)
```

```python
import jax
import jax.numpy as jnp
from jax import lax
from jax.sharding import PartitionSpec as P

EPS = 1e-05
SCORE_WEIGHT = 0.0625
NEGATIVE = -1e30
F32 = jnp.float32
BF16 = jnp.bfloat16


def dot_nt(left, right):
    return lax.dot_general(left, right, (((1,), (1,)), ((), ())), preferred_element_type=F32)


def dot_nn(left, right):
    return lax.dot_general(left, right, (((1,), (0,)), ((), ())), preferred_element_type=F32)


def columns(value):
    return jnp.sum(value, axis=0, keepdims=True)


def clip_parts(value, bound):
    ratio = value / bound
    bent = jnp.tanh(ratio)
    slope = 1.0 - bent * bent
    return bound * bent, slope, bent - ratio * slope


def norm_parts(value, gain, shift):
    centre = value - jnp.mean(value, axis=-1, keepdims=True)
    inverse = lax.rsqrt(jnp.mean(centre * centre, axis=-1, keepdims=True) + EPS)
    unit = centre * inverse
    return unit * gain + shift, unit, inverse


def norm_back(grad, unit, inverse, gain):
    scaled = grad * gain
    return inverse * (
        scaled
        - jnp.mean(scaled, axis=-1, keepdims=True)
        - unit * jnp.mean(scaled * unit, axis=-1, keepdims=True)
    )


def signs_and_scale(latent):
    scale = jnp.mean(jnp.abs(latent), axis=0).astype(BF16)
    return jnp.sign(latent).astype(BF16).T, scale


def body(
    hidden_in,
    segment_ids,
    row_lengths,
    teacher_scores,
    teacher_hidden,
    w_query,
    w_key,
    w_value,
    w_out,
    w_up,
    w_down,
    b_query,
    b_value,
    b_out,
    b_up,
    b_down,
    norm1_gain,
    norm1_bias,
    norm2_gain,
    norm2_bias,
    clip_in,
    clip_ctx,
    clip_mid,
    clip_hid,
):
    rows, block, width = hidden_in.shape
    heads = teacher_scores.shape[1]
    head_dim = width // heads
    seq_len = segment_ids.shape[1]
    tokens = rows * block
    scale = head_dim ** (-0.5)
    place = lax.axis_index("seq")
    first = place * block

    shards = [signs_and_scale(w) for w in (w_query, w_key, w_value, w_out, w_up, w_down)]
    small = jnp.stack(
        [shards[0][1], shards[1][1], shards[2][1], shards[3][1], shards[5][1], b_query, b_value,
         b_out, b_down, norm1_gain, norm1_bias, norm2_gain, norm2_bias, clip_in, clip_ctx, clip_mid]
    )
    wide = jnp.stack([shards[4][1], b_up, clip_hid])
    small = lax.all_gather(small, "dp", axis=1, tiled=True).astype(F32)
    wide = lax.all_gather(wide, "dp", axis=1, tiled=True).astype(F32)
    (a_q, a_k, a_v, a_o, a_d, bias_q, bias_v, bias_o, bias_d, g1, s1, g2, s2, c_in, c_ctx, c_mid) = [
        small[i : i + 1] for i in range(16)
    ]
    a_u, bias_u, c_hid = [wide[i : i + 1] for i in range(3)]
    sq, sk, sv, so, su, sd = [
        lax.all_gather(s[0], "dp", axis=0, tiled=True) for s in shards
    ]

    core_swap = [(0, 1), (1, 0), (2, 3), (3, 2)]
    chip_swap = [(0, 2), (2, 0), (1, 3), (3, 1)]
    across = lax.ppermute(hidden_in, "seq", chip_swap)
    beside = lax.ppermute(jnp.stack([hidden_in, across]), "seq", core_swap)
    full = jnp.stack([hidden_in, beside[0], across, beside[1]], axis=1)
    order = jnp.stack([place, place ^ 1, place ^ 2, place ^ 3])
    segments = segment_ids.reshape(rows, 4, block)[:, order].reshape(rows, seq_len)
    positions = (order[:, None] * block + jnp.arange(block)[None, :]).reshape(-1)

    inputs = hidden_in.astype(F32).reshape(tokens, width)
    low_all = clip_parts(full.astype(F32).reshape(-1, width), c_in)[0].astype(BF16)
    low_own = low_all.reshape(rows, 4, block, width)[:, 0].reshape(tokens, width)
    s_query = dot_nt(low_own, sq)
    query = a_q * s_query + bias_q
    query_low = (query * (a_k * scale)).astype(BF16).reshape(rows, block, heads, head_dim)
    s_key = dot_nt(low_all, sk).astype(BF16).reshape(rows, seq_len, heads, head_dim)
    s_value = dot_nt(low_all, sv).astype(BF16).reshape(rows, seq_len, heads, head_dim)

    scores = jnp.einsum("rqhd,rkhd->rhqk", query_low, s_key, preferred_element_type=F32)
    live = positions[None, :] < row_lengths[:, None]
    query_live = live[:, :block]
    same = (segments[:, :block, None] == segments[:, None, :])[:, None]
    counted = same & query_live[:, None, :, None] & live[:, None, None, :]
    targets = teacher_scores.reshape(rows, heads, block, 4, block)[:, :, :, order].reshape(
        rows, heads, block, seq_len
    )
    gap = jnp.where(counted, scores - targets.astype(F32), 0.0)
    distill = jnp.sum(gap * gap)
    top = jnp.max(jnp.where(same, scores, NEGATIVE), axis=-1, keepdims=True)
    expo = jnp.exp(jnp.where(same, scores - top, NEGATIVE))
    total = jnp.sum(expo, axis=-1)
    accum = jnp.einsum("rhqk,rkhd->rqhd", expo.astype(BF16), s_value, preferred_element_type=F32)
    total_rows = jnp.transpose(total, (0, 2, 1))[..., None]
    s_context = (accum / total_rows).reshape(tokens, width)

    context = a_v * s_context + bias_v
    context_low, ctx_slope, ctx_bound = clip_parts(context, c_ctx)
    s_out = dot_nt(context_low.astype(BF16), so)
    normed, unit1, inverse1 = norm_parts(inputs + a_o * s_out + bias_o, g1, s1)
    normed_low, mid_slope, mid_bound = clip_parts(normed, c_mid)
    s_up = dot_nt(normed_low.astype(BF16), su)
    pre = a_u * s_up + bias_u
    phi = 0.5 * (1.0 + lax.erf(pre * (0.5**0.5)))
    act = pre * phi
    act_slope = phi + pre * jnp.exp(-0.5 * pre * pre) * 0.3989422804014327
    hidden_low, hid_slope, hid_bound = clip_parts(act, c_hid)
    s_down = dot_nt(hidden_low.astype(BF16), sd)
    final, unit2, inverse2 = norm_parts(normed + a_d * s_down + bias_d, g2, s2)
    errors = jnp.where(
        query_live.reshape(tokens, 1),
        final - teacher_hidden.astype(F32).reshape(tokens, width),
        0.0,
    )
    objective = 0.5 * jnp.sum(errors * errors) + 0.5 * SCORE_WEIGHT * distill

    grad_second = norm_back(errors, unit2, inverse2, g2)
    grad_hid = dot_nn((grad_second * a_d).astype(BF16), sd)
    up_grad = grad_hid * hid_slope * act_slope
    grad_mid = dot_nn((up_grad * a_u).astype(BF16), su)
    grad_normed = grad_second + grad_mid * mid_slope
    grad_first = norm_back(grad_normed, unit1, inverse1, g1)
    grad_ctx_low = dot_nn((grad_first * a_o).astype(BF16), so)
    grad_ctx = grad_ctx_low * ctx_slope

    pulled = (grad_ctx * a_v).reshape(rows, block, heads, head_dim)
    accum_grad = (pulled / total_rows).astype(BF16)
    delta = jnp.sum(pulled * s_context.reshape(pulled.shape), axis=-1, keepdims=True) / total_rows
    delta = jnp.transpose(delta[..., 0], (0, 2, 1))[..., None]
    prob_grad = jnp.einsum("rqhd,rkhd->rhqk", accum_grad, s_value, preferred_element_type=F32)
    score_grad = (expo * (prob_grad - delta) + SCORE_WEIGHT * gap).astype(BF16)
    back = jnp.einsum("rhqk,rkhd->rqhd", score_grad, s_key, preferred_element_type=F32).reshape(
        tokens, width
    ) * scale
    query_grad = back * a_k
    key_grad = jnp.einsum("rhqk,rqhd->rkhd", score_grad, query_low, preferred_element_type=F32)
    value_grad = jnp.einsum(
        "rhqk,rqhd->rkhd", expo.astype(BF16), accum_grad, preferred_element_type=F32
    )
    pulled_in = dot_nn(key_grad.astype(BF16).reshape(-1, width), sk) + dot_nn(
        value_grad.astype(BF16).reshape(-1, width), sv
    )
    pulled_in = pulled_in.reshape(rows, 4, block, width)
    own_in = dot_nn((query_grad * a_q).astype(BF16), sq).reshape(rows, block, width)
    sent = lax.ppermute(
        jnp.stack([pulled_in[:, 1], pulled_in[:, 3]]).astype(BF16), "seq", core_swap
    ).astype(F32)
    crossed = lax.ppermute((pulled_in[:, 2] + sent[1]).astype(BF16), "seq", chip_swap).astype(F32)
    grad_low = (pulled_in[:, 0] + own_in + sent[0] + crossed).reshape(tokens, width)
    unused, in_slope, in_bound = clip_parts(inputs, c_in)
    grad_input = grad_first + grad_low * in_slope

    sums = jnp.concatenate(
        [
            columns(query_grad * s_query),
            columns(query * back),
            columns(grad_ctx * s_context),
            columns(grad_first * s_out),
            columns(grad_second * s_down),
            columns(query_grad),
            columns(grad_ctx),
            columns(grad_first),
            columns(grad_second),
            columns(grad_normed * unit1),
            columns(grad_normed),
            columns(errors * unit2),
            columns(errors),
            columns(grad_low * in_bound),
            columns(grad_ctx_low * ctx_bound),
            columns(grad_mid * mid_bound),
        ]
    )
    wide_sums = jnp.concatenate(
        [columns(up_grad * s_up), columns(up_grad), columns(grad_hid * hid_bound)]
    )
    sums, wide_sums, objective = lax.psum((sums, wide_sums, objective), ("dp", "seq"))
    at = lax.axis_index("dp")
    narrow, broad = w_query.shape[1], w_up.shape[1]
    sums = lax.dynamic_slice_in_dim(sums, at * narrow, narrow, 1)
    wide_sums = lax.dynamic_slice_in_dim(wide_sums, at * broad, broad, 1)
    loss = objective / (lax.axis_size("dp") * rows * seq_len)
    grads = [
        jnp.sign(w) * (s / w.shape[0])
        for w, s in zip(
            (w_query, w_key, w_value, w_out, w_up, w_down),
            (sums[0], sums[1], sums[2], sums[3], wide_sums[0], sums[4]),
        )
    ]
    return (
        final.reshape(rows, block, width).astype(BF16),
        loss,
        grad_input.reshape(rows, block, width),
        *grads,
        sums[5],
        sums[6],
        sums[7],
        wide_sums[1],
        sums[8],
        sums[9],
        sums[10],
        sums[11],
        sums[12],
        sums[13],
        sums[14],
        sums[15],
        wide_sums[2],
    )


def solution(mesh):
    rows = P("dp", "seq", None)
    cols = P(None, "dp")
    vec = P("dp")
    return jax.shard_map(
        body,
        mesh=mesh,
        in_specs=(rows, P("dp", None), vec, P("dp", None, "seq", None), rows)
        + (cols,) * 6
        + (vec,) * 13,
        out_specs=(rows, P(), rows) + (cols,) * 6 + (vec,) * 13,
        check_vma=False,
    )
```

```python
import functools

import jax
import jax.numpy as jnp
from jax import lax
from jax.experimental import pallas as pl
from jax.experimental.pallas import tpu as pltpu
from jax.sharding import PartitionSpec as P

EPS = 1e-05
SCORE_WEIGHT = 0.0625
NEGATIVE = -1e30
F32 = jnp.float32
BF16 = jnp.bfloat16
PAIR = 128
A_Q, A_K, A_V, A_O, A_D, B_Q, B_V, B_O, B_D, G1, S1, G2, S2, C_IN, C_CTX, C_MID = range(16)
A_U, B_U, C_HID, VECTORS = 16, 20, 24, 32
G_Q, G_K, G_V, G_O, G_D, G_BQ, G_BV, G_BO, G_BD, G_G1, G_S1, G_G2, G_S2, G_CIN, G_CCTX, G_CMID = range(16)
G_U, G_BU, G_CHID, LOSS, SUMS = 16, 20, 24, 28, 29


def dot_nt(left, right):
    return lax.dot_general(left, right, (((1,), (1,)), ((), ())), preferred_element_type=F32)


def dot_nn(left, right):
    return lax.dot_general(left, right, (((1,), (0,)), ((), ())), preferred_element_type=F32)


def dot_tn(left, right):
    return lax.dot_general(left, right, (((0,), (0,)), ((), ())), preferred_element_type=F32)


def columns(value):
    return jnp.sum(value, axis=0, keepdims=True)


def clip_parts(value, bound):
    ratio = value / bound
    bent = jnp.tanh(ratio)
    slope = 1.0 - bent * bent
    return bound * bent, slope, bent - ratio * slope


def norm_parts(value, gain, shift):
    centre = value - jnp.mean(value, axis=-1, keepdims=True)
    inverse = lax.rsqrt(jnp.mean(centre * centre, axis=-1, keepdims=True) + EPS)
    unit = centre * inverse
    return unit * gain + shift, unit, inverse


def norm_back(grad, unit, inverse, gain):
    scaled = grad * gain
    return inverse * (
        scaled
        - jnp.mean(scaled, axis=-1, keepdims=True)
        - unit * jnp.mean(scaled * unit, axis=-1, keepdims=True)
    )


def halves(value):
    lane = lax.broadcasted_iota(jnp.int32, value.shape, 1)
    half = value.shape[1] // 2
    zero = jnp.zeros_like(value)
    return jnp.concatenate(
        [jnp.where(lane < half, value, zero), jnp.where(lane < half, zero, value)], axis=0
    )


def by_head(first, second):
    shape = jnp.broadcast_shapes(first.shape, second.shape)
    lane = lax.broadcasted_iota(jnp.int32, shape[:-1] + (PAIR,), 1)
    return jnp.where(lane < PAIR // 2, first, second)


def folded(value):
    return jnp.sum(value.reshape(value.shape[0] // 8, 8, value.shape[1]), axis=0)


def project_row(hidden, own_hidden, sq, sk, sv, small, s_query, s_key, s_value):
    c_in = small[C_IN : C_IN + 1]
    inverse_in = 1.0 / c_in
    low = (c_in * jnp.tanh(hidden[...].astype(F32) * inverse_in)).astype(BF16)
    s_key[...] = dot_nt(low, sk[...]).astype(BF16)
    s_value[...] = dot_nt(low, sv[...]).astype(BF16)
    low = (c_in * jnp.tanh(own_hidden[...].astype(F32) * inverse_in)).astype(BF16)
    s_query[...] = dot_nt(low, sq[...])


def attend_row(
    scale, small, query_seg, key_seg, teacher, s_query, s_key, s_value, s_context, spread, probs, gaps, distill,
):
    block, width = s_query.shape
    same = query_seg[:, 0:1] == key_seg[0:1, :]
    bias = jnp.where(same, 0.0, NEGATIVE)
    counted = jnp.where(query_seg[:, 1:2] == key_seg[1:2, :], 1.0, 0.0)

    def pair(index, carry):
        at = pl.ds(pl.multiple_of(index * PAIR, PAIR), PAIR)
        query = (
            (small[A_Q : A_Q + 1, at] * s_query[:, at] + small[B_Q : B_Q + 1, at])
            * (small[A_K : A_K + 1, at] * scale)
        ).astype(BF16)
        scores = dot_nt(halves(query), s_key[:, at])
        expos, inverses = [], []
        sums = jnp.zeros((8, scores.shape[1]), F32)
        for head in range(2):
            mine = scores[head * block : (head + 1) * block]
            gap = (mine - teacher[2 * index + head].astype(F32)) * counted
            sums = sums + folded(gap * gap)
            gaps[2 * index + head] = (gap * SCORE_WEIGHT).astype(BF16)
            masked = mine + bias
            expo = jnp.exp(masked - jnp.max(masked, axis=-1, keepdims=True))
            inverses.append(1.0 / jnp.sum(expo, axis=-1, keepdims=True))
            expo = expo.astype(BF16)
            probs[2 * index + head] = expo
            expos.append(expo)
        distill[...] += sums
        both = dot_nn(jnp.concatenate(expos, axis=0), s_value[:, at])
        inverse = by_head(inverses[0], inverses[1])
        s_context[:, at] = by_head(both[:block], both[block:]) * inverse
        spread[:, at] = inverse
        return carry

    lax.fori_loop(0, width // PAIR, pair, 0)


MESH = pl.DeviceIdType.MESH
UNITS = 12
STEPS = 10
SHARED = (6, 7)

def remote(source, target, send, recv, dp, seq):
    return pltpu.make_async_remote_copy(
        src_ref=source, dst_ref=target, send_sem=send, recv_sem=recv, device_id=(dp, seq), device_id_type=MESH
    )

class Streams:
    def __init__(self, lines, own, full, z_sems, x_sems, y_sems, c_sems, l_sems):
        self.lines, self.own, self.full = lines, own, full
        self.z_sems, self.x_sems, self.y_sems, self.c_sems, self.l_sems = z_sems, x_sems, y_sems, c_sems, l_sems
        self.dp, self.seq = lax.axis_index("dp"), lax.axis_index("seq")
        self.zi, self.xi = self.dp // 2, self.dp % 2
        self.yi, self.ci = self.seq // 2, self.seq % 2
        self.size = own.shape[1]
        self.half = self.size // 2

    def unit(self, t, partner=False):
        if t in SHARED:
            return SHARED[0] + 2 * (t - SHARED[0]) + (1 - self.yi if partner else self.yi)
        return t if t < SHARED[0] else t + 2

    def piece(self, u, dp):
        start = pl.multiple_of(dp * self.size + self.ci * self.half, self.half)
        return self.full.at[u, pl.ds(start, self.half)]

    def own_piece(self, u):
        return self.own.at[u, pl.ds(pl.multiple_of(self.ci * self.half, self.half), self.half)]

    def z_copy(self, u, src, to):
        place = self.piece(u, src * 2 + self.xi)
        return remote(self.own_piece(u) if src is self.zi else place, place,
                      self.z_sems.at[0, u, to + self.lines * src], self.z_sems.at[1, u, src], to * 2 + self.xi, self.seq)

    def x_copy(self, u, src):
        place = self.piece(u, src * 2 + self.xi)
        return remote(self.own_piece(u) if src is self.zi else place, place, self.x_sems.at[0, u, src], self.x_sems.at[1, u, src],
                      self.zi * 2 + 1 - self.xi, self.seq)

    def x_arrival(self, u, src):
        place = self.piece(u, src * 2 + 1 - self.xi)
        return remote(place, place, self.x_sems.at[0, u, src], self.x_sems.at[1, u, src], self.zi * 2 + 1 - self.xi, self.seq)

    def y_copy(self, u, dp):
        place = self.piece(u, dp)
        return remote(place, place, self.y_sems.at[0, u, dp], self.y_sems.at[1, u, dp], self.dp, (1 - self.yi) * 2 + self.ci)

    def c_copy(self, u, dp):
        place = self.piece(u, dp)
        return remote(place, place, self.c_sems.at[0, u, dp], self.c_sems.at[1, u, dp], self.dp, self.yi * 2 + 1 - self.ci)

    def local_copy(self, u):
        start = pl.multiple_of(self.dp * self.size, self.size)
        return pltpu.make_async_copy(self.own.at[u], self.full.at[u, pl.ds(start, self.size)], self.l_sems.at[u])

    def each_row(self, run):
        for k in range(1, self.lines):
            pl.when(self.zi >= k)(functools.partial(run, self.zi - k, True))
            pl.when(self.zi + k < self.lines)(functools.partial(run, self.zi + k, False))

    def neighbours(self, run):
        pl.when(self.zi > 0)(lambda: run(self.zi - 1))
        pl.when(self.zi < self.lines - 1)(lambda: run(self.zi + 1))

    def relay(self, src, below, run):
        if below:
            pl.when(self.zi < self.lines - 1)(lambda: run(self.zi + 1))
        else:
            pl.when(self.zi > 0)(lambda: run(self.zi - 1))

    def launch(self, t):
        u = self.unit(t)
        self.x_copy(u, self.zi).start()
        self.neighbours(lambda to: self.z_copy(u, self.zi, to).start())

    def along_z(self, t):
        u = self.unit(t)
        def run(src, below):
            self.z_copy(u, src, self.zi).wait_recv()
            self.relay(src, below, lambda to: self.z_copy(u, src, to).start())
            self.x_copy(u, src).start()
            self.spread(t, u, src * 2 + self.xi)
        self.each_row(run)

    def over_x(self, t):
        u = self.unit(t)
        def run(src, below):
            self.x_arrival(u, src).wait_recv()
            self.spread(t, u, src * 2 + 1 - self.xi)
        run(self.zi, None)
        self.each_row(run)

    def spread(self, t, u, dp):
        if t in SHARED:
            self.y_copy(u, dp).start()
        self.c_copy(u, dp).start()

    def others(self, run):
        self.each_row(lambda src, below: run(src * 2 + self.xi))
        run(self.zi * 2 + 1 - self.xi)
        self.each_row(lambda src, below: run(src * 2 + 1 - self.xi))

    def over_y(self, t):
        u = self.unit(t, True)
        def run(dp):
            self.y_copy(u, dp).wait_recv()
            self.c_copy(u, dp).start()
        self.others(run)

    def arrived(self, u):
        self.others(lambda dp: self.c_copy(u, dp).wait_recv())
        self.local_copy(u).wait()

    def finish(self):
        for t in range(STEPS):
            u = self.unit(t)
            self.x_copy(u, self.zi).wait_send()
            self.neighbours(lambda to: self.z_copy(u, self.zi, to).wait_send())
            def run(src, below):
                self.relay(src, below, lambda to: self.z_copy(u, src, to).wait_send())
                self.x_copy(u, src).wait_send()
            self.each_row(run)
            if t in SHARED:
                self.others(lambda dp: self.y_copy(u, dp).wait_send())
        for u in range(UNITS):
            self.others(lambda dp: self.c_copy(u, dp).wait_send())


def greet(dp_count):
    dp, seq = lax.axis_index("dp"), lax.axis_index("seq")
    barrier = pltpu.get_barrier_semaphore()
    for k in range(1, dp_count):
        pl.semaphore_signal(barrier, inc=1, device_id=(lax.rem(dp + k, dp_count), seq), device_id_type=MESH)
    pl.semaphore_signal(barrier, inc=1, device_id=(dp, seq // 2 * 2 + 1 - seq % 2), device_id_type=MESH)
    pl.semaphore_signal(barrier, inc=1, device_id=(dp, (1 - seq // 2) * 2 + seq % 2), device_id_type=MESH)
    pl.semaphore_wait(barrier, dp_count + 1)

AHEAD = 3
NEAR = 3


def first_kernel(
    scale, dp_count, own, own_vectors, hidden, own_hidden, query_seg, key_seg, teacher,
    full, table, s_query, s_key, s_value, s_context, spread, probs, gaps, distill,
    whole, vectors, weights, z_sems, x_sems, y_sems, c_sems, l_sems, h_sems, o_sems, v_sems, w_sems,
):
    step = pl.program_id(0)
    rows, block = hidden.shape[0], hidden.shape[1]
    s = Streams(dp_count // 2, own, full, z_sems, x_sems, y_sems, c_sems, l_sems)
    across, beside = (1 - s.yi) * 2 + s.ci, s.yi * 2 + 1 - s.ci

    def place(r, seq):
        return whole.at[r, pl.ds(pl.multiple_of(seq * block, block), block)]

    def to_chip(r):
        return remote(hidden.at[r], place(r, s.seq), h_sems.at[0, 0, r], h_sems.at[1, 0, r], s.dp, across)

    def to_core(r):
        return remote(hidden.at[r], place(r, s.seq), h_sems.at[0, 1, r], h_sems.at[1, 1, r], s.dp, beside)

    def passed_on(r):
        return remote(place(r, across), place(r, across), h_sems.at[0, 2, r], h_sems.at[1, 2, r], s.dp, beside)

    def kept(r):
        return pltpu.make_async_copy(hidden.at[r], place(r, s.seq), o_sems.at[r])

    def hidden_pump(r):
        to_chip(r).wait_recv()
        passed_on(r).start()
        if r + NEAR < rows:
            to_chip(r + NEAR).start()

    def vector_copy(k):
        mine = vectors.at[pl.ds(pl.multiple_of(s.dp * s.size, s.size), s.size)]
        return remote(own_vectors, mine, v_sems.at[0, k], v_sems.at[1, k], lax.rem(s.dp + k, dp_count), s.seq)

    def fetch(u):
        return pltpu.make_async_copy(full.at[u], weights.at[u], w_sems.at[u])

    def launch(t):
        if t < STEPS:
            s.launch(t)

    @pl.when(step == 0)
    def _():
        distill[...] = jnp.zeros_like(distill)
        greet(dp_count)
        for k in range(1, dp_count):
            vector_copy(k).start()
        launch(0)
        for r in range(NEAR):
            to_chip(r).start()
        launch(1)
        for u in range(UNITS):
            s.local_copy(u).start()
        launch(2)
        for r in range(rows):
            to_core(r).start()
            kept(r).start()
        mine = pl.ds(pl.multiple_of(s.dp * s.size, s.size), s.size)
        vectors[mine] = own_vectors[...]
        for t in range(3):
            s.along_z(t)
            launch(t + AHEAD)
            s.over_x(t)
            hidden_pump(t)
        for k in range(1, dp_count):
            vector_copy(k).wait()
        table[...] = jnp.transpose(vectors[...].astype(F32))[: table.shape[0]]
        for u in range(3):
            s.arrived(u)
            fetch(u).start()
        for u in range(3):
            fetch(u).wait()

    for r in range(rows):
        @pl.when(step == r)
        def _(r=r):
            if r + 3 < rows:
                hidden_pump(r + 3)
            if r + 3 < STEPS:
                s.along_z(r + 3)
                launch(r + 3 + AHEAD)
            kept(r).wait()
            to_core(r).wait_recv()
            passed_on(r).wait_recv()

    project_row(whole.at[step], own_hidden.at[0], weights.at[0], weights.at[1], weights.at[2], table,
                s_query.at[0], s_key.at[0], s_value.at[0])

    for r in range(rows):
        @pl.when(step == r)
        def _(r=r):
            if r + 3 < STEPS:
                s.over_x(r + 3)

    attend_row(scale, table, query_seg.at[0], key_seg.at[0], teacher.at[0], s_query.at[0], s_key.at[0], s_value.at[0],
               s_context.at[0], spread.at[0], probs.at[0], gaps.at[0], distill)

    @pl.when(step == rows - 1)
    def _():
        for t in range(rows + 3, STEPS):
            s.along_z(t)
            s.over_x(t)
        for t in SHARED:
            s.over_y(t)
        for u in range(3, UNITS):
            s.arrived(u)
        s.finish()
        for r in range(rows):
            to_chip(r).wait_send()
            to_core(r).wait_send()
            passed_on(r).wait_send()


def plain_kernel(
    scale, whole, own_hidden, weights, table, query_seg, key_seg, teacher,
    s_query, s_key, s_value, s_context, spread, probs, gaps, distill,
):
    @pl.when(pl.program_id(0) == 0)
    def _():
        distill[...] = jnp.zeros_like(distill)

    project_row(whole.at[0], own_hidden.at[0], weights.at[0], weights.at[1], weights.at[2], table,
                s_query.at[0], s_key.at[0], s_value.at[0])
    attend_row(scale, table, query_seg.at[0], key_seg.at[0], teacher.at[0], s_query.at[0], s_key.at[0], s_value.at[0],
               s_context.at[0], spread.at[0], probs.at[0], gaps.at[0], distill)


def chain(weights, small, hidden, teacher, live, s_context, sums, final_out, grad_first_out,
          grad_ctx_out, pres, slopes, bounds):
    def vec(i):
        return small[i : i + 1]

    def add(i, value):
        sums[i] += folded(value)

    width = hidden.shape[1]
    inputs = hidden.astype(F32)
    context = vec(A_V) * s_context + vec(B_V)
    context_low, ctx_slope, ctx_bound = clip_parts(context, vec(C_CTX))
    s_out = dot_nt(context_low.astype(BF16), weights[3])
    normed, unit1, inverse1 = norm_parts(inputs + vec(A_O) * s_out + vec(B_O), vec(G1), vec(S1))
    normed_low, mid_slope, mid_bound = clip_parts(normed, vec(C_MID))
    normed_low = normed_low.astype(BF16)
    s_down = jnp.zeros_like(inputs)
    for i in range(4):
        s_up = dot_nt(normed_low, weights[4 + 2 * i])
        pres[i] = s_up
        pre = vec(A_U + i) * s_up + vec(B_U + i)
        phi = 0.5 + 0.5 * lax.erf(pre * (0.5**0.5))
        act_slope = phi + pre * (jnp.exp(-0.5 * pre * pre) * 0.3989422804014327)
        hidden_low, slope, bound = clip_parts(pre * phi, vec(C_HID + i))
        slopes[i] = slope * act_slope
        bounds[i] = bound
        s_down = s_down + dot_nt(hidden_low.astype(BF16), weights[5 + 2 * i])
    final, unit2, inverse2 = norm_parts(normed + vec(A_D) * s_down + vec(B_D), vec(G2), vec(S2))
    final_out[...] = final.astype(BF16)
    errors = (final - teacher.astype(F32)) * live
    add(LOSS, errors * errors)
    add(G_G2, errors * unit2)
    add(G_S2, errors)
    grad_second = norm_back(errors, unit2, inverse2, vec(G2))
    add(G_D, grad_second * s_down)
    add(G_BD, grad_second)
    branch = (grad_second * vec(A_D)).astype(BF16)
    grad_mid = jnp.zeros_like(inputs)
    for i in range(4):
        grad_hid = dot_nn(branch, weights[5 + 2 * i])
        add(G_CHID + i, grad_hid * bounds[i])
        up_grad = grad_hid * slopes[i]
        add(G_BU + i, up_grad)
        add(G_U + i, up_grad * pres[i])
        grad_mid = grad_mid + dot_nn((up_grad * vec(A_U + i)).astype(BF16), weights[4 + 2 * i])
    add(G_CMID, grad_mid * mid_bound)
    grad_normed = grad_second + grad_mid * mid_slope
    add(G_G1, grad_normed * unit1)
    add(G_S1, grad_normed)
    grad_first = norm_back(grad_normed, unit1, inverse1, vec(G1))
    grad_first_out[...] = grad_first
    add(G_O, grad_first * s_out)
    add(G_BO, grad_first)
    grad_ctx_low = dot_nn((grad_first * vec(A_O)).astype(BF16), weights[3])
    add(G_CCTX, grad_ctx_low * ctx_bound)
    grad_ctx = grad_ctx_low * ctx_slope
    add(G_V, grad_ctx * s_context)
    add(G_BV, grad_ctx)
    grad_ctx_out[...] = grad_ctx


def attend_back_row(scale, small, s_query, s_key, s_value, s_context, spread, probs, gaps,
                    grad_ctx, key_grads, value_grads, query_grads):
    block, width = s_query.shape

    def pair(index, carry):
        at = pl.ds(pl.multiple_of(index * PAIR, PAIR), PAIR)
        raw = small[A_Q : A_Q + 1, at] * s_query[:, at] + small[B_Q : B_Q + 1, at]
        query = halves((raw * (small[A_K : A_K + 1, at] * scale)).astype(BF16))
        pulled = grad_ctx[:, at] * small[A_V : A_V + 1, at] * spread[:, at]
        product = pulled * s_context[:, at]
        lane = lax.broadcasted_iota(jnp.int32, product.shape, 1)
        left = jnp.sum(jnp.where(lane < PAIR // 2, product, 0.0), axis=-1, keepdims=True)
        right = jnp.sum(jnp.where(lane < PAIR // 2, 0.0, product), axis=-1, keepdims=True)
        accum_grad = halves(pulled.astype(BF16))
        prob_grad = dot_nt(accum_grad, s_value[:, at])
        score_grads, expos = [], []
        for head, delta in ((0, left), (1, right)):
            expo = probs[2 * index + head]
            expos.append(expo)
            mine = prob_grad[head * block : (head + 1) * block]
            score_grads.append(
                (expo.astype(F32) * (mine - delta) + gaps[2 * index + head].astype(F32)).astype(BF16)
            )
        score_grad = jnp.concatenate(score_grads, axis=0)
        both = dot_nn(score_grad, s_key[:, at])
        query_grads[:, at] = by_head(both[:block], both[block:]) * scale
        key_grads[:, at] = dot_tn(score_grad, query).astype(BF16)
        value_grads[:, at] = dot_tn(jnp.concatenate(expos, axis=0), accum_grad).astype(BF16)
        return carry

    lax.fori_loop(0, width // PAIR, pair, 0)


def chain_kernel(weights, small, hidden, teacher, live, s_context, final, grad_first, grad_ctx, sums_out,
                 sums, pres, slopes, bounds):
    step = pl.program_id(0)

    @pl.when(step == 0)
    def _():
        sums[...] = jnp.zeros_like(sums)

    rows, block, width = hidden.shape
    flat = (rows * block, width)
    chain(weights, small, hidden[...].reshape(flat), teacher[...].reshape(flat),
          live[...].reshape(rows * block, 1), s_context[...].reshape(flat), sums, final, grad_first,
          grad_ctx, pres, slopes, bounds)

    @pl.when(step == pl.num_programs(0) - 1)
    def _():
        sums_out[...] = sums[...]


def back_kernel(scale, weights, small, s_query, s_key, s_value, s_context, spread, probs, gaps, grad_ctx,
                pulled_in, own_in, sums, key_grads, value_grads, query_grads):
    step = pl.program_id(0)

    @pl.when(step == 0)
    def _():
        sums[...] = jnp.zeros_like(sums)

    attend_back_row(scale, small, s_query.at[0], s_key.at[0], s_value.at[0],
                    s_context.at[0], spread.at[0], probs.at[0], gaps.at[0],
                    grad_ctx, key_grads, value_grads, query_grads)
    back = query_grads[...]
    raw = small[A_Q : A_Q + 1] * s_query[0] + small[B_Q : B_Q + 1]
    sums[0] += folded(raw * back)
    query_grad = back * small[A_K : A_K + 1]
    sums[1] += folded(query_grad * s_query[0])
    sums[2] += folded(query_grad)
    own_in[...] = dot_nn((query_grad * small[A_Q : A_Q + 1]).astype(BF16), weights[0])
    pulled_in[0] = (dot_nn(key_grads[...], weights[1]) + dot_nn(value_grads[...], weights[2])).astype(BF16)


def signs_and_scale(latent):
    scale = jnp.mean(jnp.abs(latent), axis=0).astype(BF16)
    return jnp.sign(latent).astype(BF16).T, scale


def body(
    hidden_in,
    segment_ids,
    row_lengths,
    teacher_scores,
    teacher_hidden,
    w_query,
    w_key,
    w_value,
    w_out,
    w_up,
    w_down,
    b_query,
    b_value,
    b_out,
    b_up,
    b_down,
    norm1_gain,
    norm1_bias,
    norm2_gain,
    norm2_bias,
    clip_in,
    clip_ctx,
    clip_mid,
    clip_hid,
):
    rows, block, width = hidden_in.shape
    heads = teacher_scores.shape[1]
    head_dim = width // heads
    seq_len = segment_ids.shape[1]
    tokens = rows * block
    scale = head_dim ** (-0.5)
    place = lax.axis_index("seq")
    first = place * block

    dp_count = lax.axis_size("dp")
    size = w_query.shape[1]
    square = [signs_and_scale(w) for w in (w_query, w_key, w_value, w_out)]
    up_signs, up_scale = signs_and_scale(w_up)
    down = w_down.reshape(dp_count, 4, size, size)
    down_signs = jnp.sign(down).astype(BF16).transpose(1, 3, 0, 2).reshape(4, size, width)
    down_scale = jnp.mean(jnp.abs(w_down), axis=0).astype(BF16)
    pairs = jnp.stack([up_signs.reshape(4, size, width), down_signs], axis=1).reshape(8, size, width)
    own = jnp.concatenate([jnp.stack([s for s, _ in square]), pairs])
    own_vectors = jnp.concatenate(
        [jnp.stack([*(a for _, a in square), down_scale, b_query, b_value, b_out, b_down, norm1_gain, norm1_bias,
                    norm2_gain, norm2_bias, clip_in, clip_ctx, clip_mid]),
         up_scale.reshape(4, size), b_up.reshape(4, size), clip_hid.reshape(4, size)]
    )
    own_vectors = jnp.pad(own_vectors.T, ((0, 0), (0, PAIR - own_vectors.shape[0])))

    positions = jnp.arange(seq_len, dtype=jnp.int32)
    live = positions[None, :] < row_lengths[:, None]
    key_seg = jnp.stack([segment_ids, jnp.where(live, segment_ids, -1)], axis=1)
    own_seg = lax.dynamic_slice_in_dim(segment_ids, first, block, 1)
    query_live = lax.dynamic_slice_in_dim(live, first, block, 1)
    query_seg = jnp.stack([own_seg, jnp.where(query_live, own_seg, -2)], axis=2)

    def row_spec(*shape):
        return pl.BlockSpec((1,) + shape, lambda i: (i,) + (0,) * len(shape))

    def whole(array):
        return pl.BlockSpec(array.shape, lambda i: (0,) * array.ndim, pipeline_mode=pl.Buffered(1))

    three = pl.BlockSpec((3, width, width), lambda i: (0, 0, 0), pipeline_mode=pl.Buffered(1))
    attend_specs = [row_spec(block, width), row_spec(seq_len, width), row_spec(seq_len, width), row_spec(block, width),
                    row_spec(block, width), row_spec(heads, block, seq_len), row_spec(heads, block, seq_len),
                    pl.BlockSpec((8, seq_len), lambda i: (0, 0))]
    attend_shapes = [jax.ShapeDtypeStruct((rows, block, width), F32),
                     jax.ShapeDtypeStruct((rows, seq_len, width), BF16),
                     jax.ShapeDtypeStruct((rows, seq_len, width), BF16),
                     jax.ShapeDtypeStruct((rows, block, width), F32),
                     jax.ShapeDtypeStruct((rows, block, width), F32),
                     jax.ShapeDtypeStruct((rows, heads, block, seq_len), BF16),
                     jax.ShapeDtypeStruct((rows, heads, block, seq_len), BF16),
                     jax.ShapeDtypeStruct((8, seq_len), F32)]
    masks_specs = [row_spec(block, 2), row_spec(2, seq_len), row_spec(heads, block, seq_len)]
    anywhere = pl.BlockSpec(memory_space=pl.ANY)
    lines = dp_count // 2
    sems = pltpu.SemaphoreType.DMA
    if size % 32 == 0:
        full, table, s_query, s_key, s_value, s_context, spread, probs, gaps, distill = pl.pallas_call(
            functools.partial(first_kernel, scale, dp_count),
            grid=(rows,),
            in_specs=[anywhere, whole(own_vectors), anywhere, row_spec(block, width)] + masks_specs,
            out_specs=[anywhere, pl.BlockSpec((VECTORS, width), lambda i: (0, 0))] + attend_specs,
            out_shape=[jax.ShapeDtypeStruct((UNITS, width, width), BF16), jax.ShapeDtypeStruct((VECTORS, width), F32)]
            + attend_shapes,
            scratch_shapes=[
                pltpu.VMEM((rows, seq_len, width), BF16), pltpu.VMEM((width, PAIR), BF16), pltpu.VMEM((3, width, width), BF16),
                sems((2, UNITS, lines * lines)), sems((2, UNITS, lines)), sems((2, UNITS, dp_count)),
                sems((2, UNITS, dp_count)), sems((UNITS,)), sems((2, 3, rows)), sems((rows,)), sems((2, dp_count)), sems((3,)),
            ],
            compiler_params=pltpu.CompilerParams(collective_id=0, has_side_effects=True, vmem_limit_bytes=60 * 2**20),
        )(own, own_vectors, hidden_in, hidden_in, query_seg, key_seg, teacher_scores)
    else:
        full = lax.all_gather(own, "dp", axis=1, tiled=True)
        table = lax.all_gather(own_vectors, "dp", axis=0, tiled=True).astype(F32).T[:VECTORS]
        hidden_full = lax.all_gather(hidden_in, "seq", axis=1, tiled=True)
        s_query, s_key, s_value, s_context, spread, probs, gaps, distill = pl.pallas_call(
            functools.partial(plain_kernel, scale),
            grid=(rows,),
            in_specs=[row_spec(seq_len, width), row_spec(block, width), three, whole(table)] + masks_specs,
            out_specs=attend_specs,
            out_shape=attend_shapes,
            compiler_params=pltpu.CompilerParams(vmem_limit_bytes=60 * 2**20),
        )(hidden_full, hidden_in, full, table, query_seg, key_seg, teacher_scores)

    group = 2
    def group_spec(*shape):
        return pl.BlockSpec((group,) + shape, lambda i: (i,) + (0,) * len(shape))
    flat_spec = pl.BlockSpec((group * block, width), lambda i: (i, 0))
    live_column = query_live.astype(F32)[..., None]
    final, grad_first, grad_ctx, sums = pl.pallas_call(
        chain_kernel,
        grid=(rows // group,),
        in_specs=[whole(full), whole(table),
                  group_spec(block, width), group_spec(block, width), group_spec(block, 1), group_spec(block, width)],
        out_specs=[flat_spec, flat_spec, flat_spec,
                   pl.BlockSpec((SUMS, 8, width), lambda i: (0, 0, 0))],
        out_shape=[jax.ShapeDtypeStruct((tokens, width), BF16),
                   jax.ShapeDtypeStruct((tokens, width), F32),
                   jax.ShapeDtypeStruct((tokens, width), F32),
                   jax.ShapeDtypeStruct((SUMS, 8, width), F32)],
        scratch_shapes=[pltpu.VMEM((SUMS, 8, width), F32)]
        + [pltpu.VMEM((4, group * block, width), F32)] * 3,
        compiler_params=pltpu.CompilerParams(vmem_limit_bytes=60 * 2**20),
    )(full, table, hidden_in, teacher_hidden, live_column, s_context)
    one_spec = pl.BlockSpec((block, width), lambda i: (i, 0))
    pulled_in, own_in, more = pl.pallas_call(
        functools.partial(back_kernel, scale),
        grid=(rows,),
        in_specs=[three, whole(table),
                  row_spec(block, width), row_spec(seq_len, width), row_spec(seq_len, width), row_spec(block, width),
                  row_spec(block, width), row_spec(heads, block, seq_len), row_spec(heads, block, seq_len), one_spec],
        out_specs=[row_spec(seq_len, width), one_spec, pl.BlockSpec((3, 8, width), lambda i: (0, 0, 0))],
        out_shape=[jax.ShapeDtypeStruct((rows, seq_len, width), BF16),
                   jax.ShapeDtypeStruct((tokens, width), F32),
                   jax.ShapeDtypeStruct((3, 8, width), F32)],
        scratch_shapes=[pltpu.VMEM((seq_len, width), BF16), pltpu.VMEM((seq_len, width), BF16),
                        pltpu.VMEM((block, width), F32)],
        compiler_params=pltpu.CompilerParams(vmem_limit_bytes=60 * 2**20),
    )(full, table, s_query, s_key, s_value, s_context, spread, probs, gaps, grad_ctx)
    sums = sums.at[G_K].set(more[0]).at[G_Q].set(more[1]).at[G_BQ].set(more[2])
    objective = 0.5 * jnp.sum(sums[LOSS]) + 0.5 * SCORE_WEIGHT * jnp.sum(distill)

    crossed = lax.psum_scatter(pulled_in, "seq", scatter_dimension=1, tiled=True).astype(F32)
    grad_low = own_in + crossed.reshape(tokens, width)
    inputs = hidden_in.astype(F32).reshape(tokens, width)
    unused, in_slope, in_bound = clip_parts(inputs, table[C_IN : C_IN + 1])
    grad_input = grad_first + grad_low * in_slope
    sums = jnp.sum(sums, axis=1)
    wide_sums = sums[16:28]
    sums = sums[:16].at[G_CIN].set(columns(grad_low * in_bound)[0])
    sums, wide_sums, objective = lax.psum((sums, wide_sums, objective), ("dp", "seq"))
    at = lax.axis_index("dp")
    sums = lax.dynamic_slice_in_dim(sums, at * size, size, 1)
    wide_sums = lax.dynamic_slice_in_dim(wide_sums, at * size, size, 1).reshape(3, 4 * size)
    loss = objective / (lax.axis_size("dp") * rows * seq_len)
    grads = [
        jnp.sign(w) * (s / w.shape[0])
        for w, s in zip(
            (w_query, w_key, w_value, w_out, w_up, w_down),
            (sums[0], sums[1], sums[2], sums[3], wide_sums[0], sums[4]),
        )
    ]
    return (
        final.reshape(rows, block, width).astype(BF16),
        loss,
        grad_input.reshape(rows, block, width),
        *grads,
        sums[5],
        sums[6],
        sums[7],
        wide_sums[1],
        sums[8],
        sums[9],
        sums[10],
        sums[11],
        sums[12],
        sums[13],
        sums[14],
        sums[15],
        wide_sums[2],
    )


def solution(mesh):
    rows = P("dp", "seq", None)
    cols = P(None, "dp")
    vec = P("dp")
    return jax.shard_map(
        body,
        mesh=mesh,
        in_specs=(rows, P("dp", None), vec, P("dp", None, "seq", None), rows)
        + (cols,) * 6
        + (vec,) * 13,
        out_specs=(rows, P(), rows) + (cols,) * 6 + (vec,) * 13,
        check_vma=False,
    )
```

```python
import functools

import jax
import jax.numpy as jnp
from jax import lax
from jax.experimental import pallas as pl
from jax.experimental.pallas import tpu as pltpu
from jax.sharding import PartitionSpec as P

EPS = 1e-05
SCORE_WEIGHT = 0.0625
NEGATIVE = -1e30
F32 = jnp.float32
BF16 = jnp.bfloat16
PAIR = 128
A_Q, A_K, A_V, A_O, A_D, B_Q, B_V, B_O, B_D, G1, S1, G2, S2, C_IN, C_CTX, C_MID = range(16)
A_U, B_U, C_HID, VECTORS = 16, 20, 24, 32
G_Q, G_K, G_V, G_O, G_D, G_BQ, G_BV, G_BO, G_BD, G_G1, G_S1, G_G2, G_S2, G_CIN, G_CCTX, G_CMID = range(16)
G_U, G_BU, G_CHID, LOSS, SUMS = 16, 20, 24, 28, 29


def dot_nt(left, right):
    return lax.dot_general(left, right, (((1,), (1,)), ((), ())), preferred_element_type=F32)


def dot_nn(left, right):
    return lax.dot_general(left, right, (((1,), (0,)), ((), ())), preferred_element_type=F32)


def dot_tn(left, right):
    return lax.dot_general(left, right, (((0,), (0,)), ((), ())), preferred_element_type=F32)


def columns(value):
    return jnp.sum(value, axis=0, keepdims=True)


def clip_parts(value, bound):
    ratio = value / bound
    bent = jnp.tanh(ratio)
    slope = 1.0 - bent * bent
    return bound * bent, slope, bent - ratio * slope


def norm_parts(value, gain, shift):
    centre = value - jnp.mean(value, axis=-1, keepdims=True)
    inverse = lax.rsqrt(jnp.mean(centre * centre, axis=-1, keepdims=True) + EPS)
    unit = centre * inverse
    return unit * gain + shift, unit, inverse


def norm_back(grad, unit, inverse, gain):
    scaled = grad * gain
    return inverse * (
        scaled
        - jnp.mean(scaled, axis=-1, keepdims=True)
        - unit * jnp.mean(scaled * unit, axis=-1, keepdims=True)
    )


def halves(value):
    lane = lax.broadcasted_iota(jnp.int32, value.shape, 1)
    half = value.shape[1] // 2
    zero = jnp.zeros_like(value)
    return jnp.concatenate(
        [jnp.where(lane < half, value, zero), jnp.where(lane < half, zero, value)], axis=0
    )


def by_head(first, second):
    shape = jnp.broadcast_shapes(first.shape, second.shape)
    lane = lax.broadcasted_iota(jnp.int32, shape[:-1] + (PAIR,), 1)
    return jnp.where(lane < PAIR // 2, first, second)


def folded(value):
    return jnp.sum(value.reshape(value.shape[0] // 8, 8, value.shape[1]), axis=0)


def project_row(hidden, own_hidden, sq, sk, sv, small, s_query, s_key, s_value):
    c_in = small[C_IN : C_IN + 1]
    inverse_in = 1.0 / c_in
    low = (c_in * jnp.tanh(hidden[...].astype(F32) * inverse_in)).astype(BF16)
    s_key[...] = dot_nt(low, sk[...]).astype(BF16)
    s_value[...] = dot_nt(low, sv[...]).astype(BF16)
    low = (c_in * jnp.tanh(own_hidden[...].astype(F32) * inverse_in)).astype(BF16)
    s_query[...] = dot_nt(low, sq[...])


def attend_row(
    scale, small, query_seg, key_seg, teacher, s_query, s_key, s_value, s_context, spread, probs, gaps, distill, bias, counted,
    first, last,
):
    block, width = s_query.shape
    if first == 0:
        bias[...] = jnp.where(query_seg[:, 0:1] == key_seg[0:1, :], 0.0, NEGATIVE)
        counted[...] = jnp.where(query_seg[:, 1:2] == key_seg[1:2, :], 1.0, 0.0)

    def pair(index, carry):
        at = pl.ds(pl.multiple_of(index * PAIR, PAIR), PAIR)
        query = (
            (small[A_Q : A_Q + 1, at] * s_query[:, at] + small[B_Q : B_Q + 1, at])
            * (small[A_K : A_K + 1, at] * scale)
        ).astype(BF16)
        scores = dot_nt(halves(query), s_key[:, at])
        expos, inverses = [], []
        sums = jnp.zeros((8, scores.shape[1]), F32)
        for head in range(2):
            mine = scores[head * block : (head + 1) * block]
            gap = (mine - teacher[2 * index + head].astype(F32)) * counted[...]
            sums = sums + folded(gap * gap)
            gaps[2 * index + head] = (gap * SCORE_WEIGHT).astype(BF16)
            masked = mine + bias[...]
            expo = jnp.exp(masked - jnp.max(masked, axis=-1, keepdims=True))
            inverses.append(1.0 / jnp.sum(expo, axis=-1, keepdims=True))
            expo = expo.astype(BF16)
            probs[2 * index + head] = expo
            expos.append(expo)
        distill[...] += sums
        both = dot_nn(jnp.concatenate(expos, axis=0), s_value[:, at])
        inverse = by_head(inverses[0], inverses[1])
        s_context[:, at] = by_head(both[:block], both[block:]) * inverse
        spread[:, at] = inverse
        return carry

    lax.fori_loop(first, last, pair, 0)


MESH = pl.DeviceIdType.MESH
UNITS = 12
STEPS = 10
SHARED = (6, 7)

def remote(source, target, send, recv, dp, seq):
    return pltpu.make_async_remote_copy(
        src_ref=source, dst_ref=target, send_sem=send, recv_sem=recv, device_id=(dp, seq), device_id_type=MESH
    )

class Streams:
    def __init__(self, lines, own, full, z_sems, x_sems, y_sems, c_sems, l_sems):
        self.lines, self.own, self.full = lines, own, full
        self.z_sems, self.x_sems, self.y_sems, self.c_sems, self.l_sems = z_sems, x_sems, y_sems, c_sems, l_sems
        self.dp, self.seq = lax.axis_index("dp"), lax.axis_index("seq")
        self.zi, self.xi = self.dp // 2, self.dp % 2
        self.yi, self.ci = self.seq // 2, self.seq % 2
        self.size = own.shape[1]
        self.half = self.size // 2

    def unit(self, t, partner=False):
        if t in SHARED:
            return SHARED[0] + 2 * (t - SHARED[0]) + (1 - self.yi if partner else self.yi)
        return t if t < SHARED[0] else t + 2

    def piece(self, u, dp):
        start = pl.multiple_of(dp * self.size + self.ci * self.half, self.half)
        return self.full.at[u, pl.ds(start, self.half)]

    def own_piece(self, u):
        return self.own.at[u, pl.ds(pl.multiple_of(self.ci * self.half, self.half), self.half)]

    def z_copy(self, u, src, to):
        place = self.piece(u, src * 2 + self.xi)
        return remote(self.own_piece(u) if src is self.zi else place, place,
                      self.z_sems.at[0, u, to + self.lines * src], self.z_sems.at[1, u, src], to * 2 + self.xi, self.seq)

    def x_copy(self, u, src):
        place = self.piece(u, src * 2 + self.xi)
        return remote(self.own_piece(u) if src is self.zi else place, place, self.x_sems.at[0, u, src], self.x_sems.at[1, u, src],
                      self.zi * 2 + 1 - self.xi, self.seq)

    def x_arrival(self, u, src):
        place = self.piece(u, src * 2 + 1 - self.xi)
        return remote(place, place, self.x_sems.at[0, u, src], self.x_sems.at[1, u, src], self.zi * 2 + 1 - self.xi, self.seq)

    def y_copy(self, u, dp):
        place = self.piece(u, dp)
        return remote(place, place, self.y_sems.at[0, u, dp], self.y_sems.at[1, u, dp], self.dp, (1 - self.yi) * 2 + self.ci)

    def c_copy(self, u, dp):
        place = self.piece(u, dp)
        return remote(place, place, self.c_sems.at[0, u, dp], self.c_sems.at[1, u, dp], self.dp, self.yi * 2 + 1 - self.ci)

    def local_copy(self, u):
        start = pl.multiple_of(self.dp * self.size, self.size)
        return pltpu.make_async_copy(self.own.at[u], self.full.at[u, pl.ds(start, self.size)], self.l_sems.at[u])

    def each_row(self, run):
        for k in range(1, self.lines):
            pl.when(self.zi >= k)(functools.partial(run, self.zi - k, True))
            pl.when(self.zi + k < self.lines)(functools.partial(run, self.zi + k, False))

    def neighbours(self, run):
        pl.when(self.zi > 0)(lambda: run(self.zi - 1))
        pl.when(self.zi < self.lines - 1)(lambda: run(self.zi + 1))

    def relay(self, src, below, run):
        if below:
            pl.when(self.zi < self.lines - 1)(lambda: run(self.zi + 1))
        else:
            pl.when(self.zi > 0)(lambda: run(self.zi - 1))

    def launch(self, t):
        u = self.unit(t)
        self.x_copy(u, self.zi).start()
        self.neighbours(lambda to: self.z_copy(u, self.zi, to).start())

    def at_distance(self, k, run):
        if k == 0:
            run(self.zi, None)
        else:
            pl.when(self.zi >= k)(functools.partial(run, self.zi - k, True))
            pl.when(self.zi + k < self.lines)(functools.partial(run, self.zi + k, False))

    def along_z(self, t, k):
        u = self.unit(t)
        def run(src, below):
            self.z_copy(u, src, self.zi).wait_recv()
            self.relay(src, below, lambda to: self.z_copy(u, src, to).start())
            self.x_copy(u, src).start()
            self.spread(t, u, src * 2 + self.xi)
        self.at_distance(k, run)

    def over_x(self, t, k):
        u = self.unit(t)
        def run(src, below):
            self.x_arrival(u, src).wait_recv()
            self.spread(t, u, src * 2 + 1 - self.xi)
        self.at_distance(k, run)

    def spread(self, t, u, dp):
        if t in SHARED:
            self.y_copy(u, dp).start()
        self.c_copy(u, dp).start()

    def others(self, run):
        self.each_row(lambda src, below: run(src * 2 + self.xi))
        run(self.zi * 2 + 1 - self.xi)
        self.each_row(lambda src, below: run(src * 2 + 1 - self.xi))

    def over_y(self, t):
        u = self.unit(t, True)
        def run(dp):
            self.y_copy(u, dp).wait_recv()
            self.c_copy(u, dp).start()
        self.others(run)

    def arrived(self, u):
        self.others(lambda dp: self.c_copy(u, dp).wait_recv())
        self.local_copy(u).wait()

    def finish(self):
        for t in range(STEPS):
            u = self.unit(t)
            self.x_copy(u, self.zi).wait_send()
            self.neighbours(lambda to: self.z_copy(u, self.zi, to).wait_send())
            def run(src, below):
                self.relay(src, below, lambda to: self.z_copy(u, src, to).wait_send())
                self.x_copy(u, src).wait_send()
            self.each_row(run)
            if t in SHARED:
                self.others(lambda dp: self.y_copy(u, dp).wait_send())
        for u in range(UNITS):
            self.others(lambda dp: self.c_copy(u, dp).wait_send())


def greet(dp_count):
    dp, seq = lax.axis_index("dp"), lax.axis_index("seq")
    barrier = pltpu.get_barrier_semaphore()
    for k in range(1, dp_count):
        pl.semaphore_signal(barrier, inc=1, device_id=(lax.rem(dp + k, dp_count), seq), device_id_type=MESH)
    pl.semaphore_signal(barrier, inc=1, device_id=(dp, seq // 2 * 2 + 1 - seq % 2), device_id_type=MESH)
    pl.semaphore_signal(barrier, inc=1, device_id=(dp, (1 - seq // 2) * 2 + seq % 2), device_id_type=MESH)
    pl.semaphore_wait(barrier, dp_count + 1)

NEAR = 3


def first_kernel(
    scale, dp_count, own, own_vectors, hidden, own_hidden, query_seg, key_seg, teacher,
    full, table, s_query, s_key, s_value, s_context, spread, probs, gaps, distill,
    whole, vectors, weights, z_sems, x_sems, y_sems, c_sems, l_sems, h_sems, o_sems, v_sems, w_sems, bias, counted,
):
    step = pl.program_id(0)
    rows, block = hidden.shape[0], hidden.shape[1]
    s = Streams(dp_count // 2, own, full, z_sems, x_sems, y_sems, c_sems, l_sems)
    across, beside = (1 - s.yi) * 2 + s.ci, s.yi * 2 + 1 - s.ci

    def place(r, seq):
        return whole.at[r, pl.ds(pl.multiple_of(seq * block, block), block)]

    def to_chip(r):
        return remote(hidden.at[r], place(r, s.seq), h_sems.at[0, 0, r], h_sems.at[1, 0, r], s.dp, across)

    def to_core(r):
        return remote(hidden.at[r], place(r, s.seq), h_sems.at[0, 1, r], h_sems.at[1, 1, r], s.dp, beside)

    def passed_on(r):
        return remote(place(r, across), place(r, across), h_sems.at[0, 2, r], h_sems.at[1, 2, r], s.dp, beside)

    def kept(r):
        return pltpu.make_async_copy(hidden.at[r], place(r, s.seq), o_sems.at[r])

    def hidden_pump(r):
        to_chip(r).wait_recv()
        passed_on(r).start()
        if r + NEAR < rows:
            to_chip(r + NEAR).start()

    def vector_copy(k):
        mine = vectors.at[pl.ds(pl.multiple_of(s.dp * s.size, s.size), s.size)]
        return remote(own_vectors, mine, v_sems.at[0, k], v_sems.at[1, k], lax.rem(s.dp + k, dp_count), s.seq)

    def fetch(u):
        return pltpu.make_async_copy(full.at[u], weights.at[u], w_sems.at[u])

    def point(r, j):
        if j == 0 and r + 3 < rows:
            hidden_pump(r + 3)
        for t in range(3, STEPS):
            at = 4 * r + j - 3 * (t - 3)
            if at == 0 and t + 2 < STEPS:
                s.launch(t + 2)
            if at in (0, 3, 6):
                s.along_z(t, at // 3 + 1)
            if at in (1, 4, 7, 10):
                s.over_x(t, at // 3)
            if t in SHARED and at == 13:
                s.over_y(t)

    def points(j):
        for r in range(rows):
            pl.when(step == r)(functools.partial(point, r, j))

    @pl.when(step == 0)
    def _():
        distill[...] = jnp.zeros_like(distill)
        greet(dp_count)
        for k in range(1, dp_count):
            vector_copy(k).start()
        for t in range(3):
            s.launch(t)
        for r in range(NEAR):
            to_chip(r).start()
        for u in range(UNITS):
            s.local_copy(u).start()
        for r in range(rows):
            to_core(r).start()
            kept(r).start()
        mine = pl.ds(pl.multiple_of(s.dp * s.size, s.size), s.size)
        vectors[mine] = own_vectors[...]
        for k in range(1, s.lines):
            for t in range(3):
                s.along_z(t, k)
                s.over_x(t, k - 1)
            hidden_pump(k - 1)
        s.launch(3)
        for t in range(3):
            s.over_x(t, s.lines - 1)
        s.launch(4)
        for k in range(1, dp_count):
            vector_copy(k).wait()
        table[...] = jnp.transpose(vectors[...].astype(F32))[: table.shape[0]]
        for u in range(3):
            s.arrived(u)
            fetch(u).start()
        for u in range(3):
            fetch(u).wait()

    points(0)
    for r in range(rows):
        @pl.when(step == r)
        def _(r=r):
            kept(r).wait()
            to_core(r).wait_recv()
            passed_on(r).wait_recv()

    project_row(whole.at[step], own_hidden.at[0], weights.at[0], weights.at[1], weights.at[2], table,
                s_query.at[0], s_key.at[0], s_value.at[0])
    count = s_query.shape[2] // PAIR
    for j in range(3):
        points(j + 1)
        attend_row(scale, table, query_seg.at[0], key_seg.at[0], teacher.at[0], s_query.at[0], s_key.at[0], s_value.at[0],
                   s_context.at[0], spread.at[0], probs.at[0], gaps.at[0], distill, bias, counted,
                   count * j // 3, count * (j + 1) // 3)

    @pl.when(step == rows - 1)
    def _():
        for u in range(3, UNITS):
            s.arrived(u)
        s.finish()
        for r in range(rows):
            to_chip(r).wait_send()
            to_core(r).wait_send()
            passed_on(r).wait_send()


def plain_kernel(
    scale, whole, own_hidden, weights, table, query_seg, key_seg, teacher,
    s_query, s_key, s_value, s_context, spread, probs, gaps, distill, bias, counted,
):
    @pl.when(pl.program_id(0) == 0)
    def _():
        distill[...] = jnp.zeros_like(distill)

    project_row(whole.at[0], own_hidden.at[0], weights.at[0], weights.at[1], weights.at[2], table,
                s_query.at[0], s_key.at[0], s_value.at[0])
    attend_row(scale, table, query_seg.at[0], key_seg.at[0], teacher.at[0], s_query.at[0], s_key.at[0], s_value.at[0],
               s_context.at[0], spread.at[0], probs.at[0], gaps.at[0], distill, bias, counted, 0, s_query.shape[2] // PAIR)


def chain(weights, small, hidden, teacher, live, s_context, sums, final_out, grad_first_out,
          grad_ctx_out, pres, slopes, bounds):
    def vec(i):
        return small[i : i + 1]

    def add(i, value):
        sums[i] += folded(value)

    width = hidden.shape[1]
    inputs = hidden.astype(F32)
    context = vec(A_V) * s_context + vec(B_V)
    context_low, ctx_slope, ctx_bound = clip_parts(context, vec(C_CTX))
    s_out = dot_nt(context_low.astype(BF16), weights[3])
    normed, unit1, inverse1 = norm_parts(inputs + vec(A_O) * s_out + vec(B_O), vec(G1), vec(S1))
    normed_low, mid_slope, mid_bound = clip_parts(normed, vec(C_MID))
    normed_low = normed_low.astype(BF16)
    s_down = jnp.zeros_like(inputs)
    for i in range(4):
        s_up = dot_nt(normed_low, weights[4 + 2 * i])
        pres[i] = s_up
        pre = vec(A_U + i) * s_up + vec(B_U + i)
        phi = 0.5 + 0.5 * lax.erf(pre * (0.5**0.5))
        act_slope = phi + pre * (jnp.exp(-0.5 * pre * pre) * 0.3989422804014327)
        hidden_low, slope, bound = clip_parts(pre * phi, vec(C_HID + i))
        slopes[i] = slope * act_slope
        bounds[i] = bound
        s_down = s_down + dot_nt(hidden_low.astype(BF16), weights[5 + 2 * i])
    final, unit2, inverse2 = norm_parts(normed + vec(A_D) * s_down + vec(B_D), vec(G2), vec(S2))
    final_out[...] = final.astype(BF16)
    errors = (final - teacher.astype(F32)) * live
    add(LOSS, errors * errors)
    add(G_G2, errors * unit2)
    add(G_S2, errors)
    grad_second = norm_back(errors, unit2, inverse2, vec(G2))
    add(G_D, grad_second * s_down)
    add(G_BD, grad_second)
    branch = (grad_second * vec(A_D)).astype(BF16)
    grad_mid = jnp.zeros_like(inputs)
    for i in range(4):
        grad_hid = dot_nn(branch, weights[5 + 2 * i])
        add(G_CHID + i, grad_hid * bounds[i])
        up_grad = grad_hid * slopes[i]
        add(G_BU + i, up_grad)
        add(G_U + i, up_grad * pres[i])
        grad_mid = grad_mid + dot_nn((up_grad * vec(A_U + i)).astype(BF16), weights[4 + 2 * i])
    add(G_CMID, grad_mid * mid_bound)
    grad_normed = grad_second + grad_mid * mid_slope
    add(G_G1, grad_normed * unit1)
    add(G_S1, grad_normed)
    grad_first = norm_back(grad_normed, unit1, inverse1, vec(G1))
    grad_first_out[...] = grad_first
    add(G_O, grad_first * s_out)
    add(G_BO, grad_first)
    grad_ctx_low = dot_nn((grad_first * vec(A_O)).astype(BF16), weights[3])
    add(G_CCTX, grad_ctx_low * ctx_bound)
    grad_ctx = grad_ctx_low * ctx_slope
    add(G_V, grad_ctx * s_context)
    add(G_BV, grad_ctx)
    grad_ctx_out[...] = grad_ctx


def attend_back_row(scale, small, s_query, s_key, s_value, s_context, spread, probs, gaps,
                    grad_ctx, key_grads, value_grads, query_grads):
    block, width = s_query.shape

    def pair(index, carry):
        at = pl.ds(pl.multiple_of(index * PAIR, PAIR), PAIR)
        raw = small[A_Q : A_Q + 1, at] * s_query[:, at] + small[B_Q : B_Q + 1, at]
        query = halves((raw * (small[A_K : A_K + 1, at] * scale)).astype(BF16))
        pulled = grad_ctx[:, at] * small[A_V : A_V + 1, at] * spread[:, at]
        product = pulled * s_context[:, at]
        lane = lax.broadcasted_iota(jnp.int32, product.shape, 1)
        left = jnp.sum(jnp.where(lane < PAIR // 2, product, 0.0), axis=-1, keepdims=True)
        right = jnp.sum(jnp.where(lane < PAIR // 2, 0.0, product), axis=-1, keepdims=True)
        accum_grad = halves(pulled.astype(BF16))
        prob_grad = dot_nt(accum_grad, s_value[:, at])
        score_grads, expos = [], []
        for head, delta in ((0, left), (1, right)):
            expo = probs[2 * index + head]
            expos.append(expo)
            mine = prob_grad[head * block : (head + 1) * block]
            score_grads.append(
                (expo.astype(F32) * (mine - delta) + gaps[2 * index + head].astype(F32)).astype(BF16)
            )
        score_grad = jnp.concatenate(score_grads, axis=0)
        both = dot_nn(score_grad, s_key[:, at])
        query_grads[:, at] = by_head(both[:block], both[block:]) * scale
        key_grads[:, at] = dot_tn(score_grad, query).astype(BF16)
        value_grads[:, at] = dot_tn(jnp.concatenate(expos, axis=0), accum_grad).astype(BF16)
        return carry

    lax.fori_loop(0, width // PAIR, pair, 0)


def chain_kernel(weights, small, hidden, teacher, live, s_context, final, grad_first, grad_ctx, sums_out,
                 sums, pres, slopes, bounds):
    step = pl.program_id(0)

    @pl.when(step == 0)
    def _():
        sums[...] = jnp.zeros_like(sums)

    rows, block, width = hidden.shape
    flat = (rows * block, width)
    chain(weights, small, hidden[...].reshape(flat), teacher[...].reshape(flat),
          live[...].reshape(rows * block, 1), s_context[...].reshape(flat), sums, final, grad_first,
          grad_ctx, pres, slopes, bounds)

    @pl.when(step == pl.num_programs(0) - 1)
    def _():
        sums_out[...] = sums[...]


def back_kernel(scale, weights, small, s_query, s_key, s_value, s_context, spread, probs, gaps, grad_ctx,
                pulled_in, own_in, sums, key_grads, value_grads, query_grads):
    step = pl.program_id(0)

    @pl.when(step == 0)
    def _():
        sums[...] = jnp.zeros_like(sums)

    attend_back_row(scale, small, s_query.at[0], s_key.at[0], s_value.at[0],
                    s_context.at[0], spread.at[0], probs.at[0], gaps.at[0],
                    grad_ctx, key_grads, value_grads, query_grads)
    back = query_grads[...]
    raw = small[A_Q : A_Q + 1] * s_query[0] + small[B_Q : B_Q + 1]
    sums[0] += folded(raw * back)
    query_grad = back * small[A_K : A_K + 1]
    sums[1] += folded(query_grad * s_query[0])
    sums[2] += folded(query_grad)
    own_in[...] = dot_nn((query_grad * small[A_Q : A_Q + 1]).astype(BF16), weights[0])
    pulled_in[0] = (dot_nn(key_grads[...], weights[1]) + dot_nn(value_grads[...], weights[2])).astype(BF16)


def last_kernel(
    scale, dp_count, weights, table, s_query, s_key, s_value, s_context, spread, probs, gaps, grad_ctx,
    hidden, grad_first, chain_sums, distill,
    grad_input, early, late,
    key_grads, value_grads, query_grads, partial, kept, near, sent, far, sums,
    mine_a, slices_a, mine_b, slices_b, pieces,
    near_sems, far_sems, a_sems, b_sems,
):
    step = pl.program_id(0)
    rows = partial.shape[0]
    block, width = s_query.shape[1], s_query.shape[2]
    size = width // dp_count
    dp, seq = lax.axis_index("dp"), lax.axis_index("seq")
    yi, ci = seq // 2, seq % 2
    across, beside = (1 - yi) * 2 + ci, yi * 2 + 1 - ci
    corner = (1 - yi) * 2 + 1 - ci
    peers = (across, beside, corner)

    def positions(place):
        return pl.ds(pl.multiple_of(place * block, block), block)

    def near_copy(r, which):
        place = beside if which == 0 else corner
        return remote(partial.at[r, positions(place)], near.at[r, which], near_sems.at[0, r, which], near_sems.at[1, r, which],
                      dp, beside)

    def far_copy(r):
        return remote(sent.at[r], far.at[r], far_sems.at[0, r], far_sems.at[1, r], dp, across)

    def scatter(mine, slices, sems, k):
        to = lax.rem(dp + k, dp_count)
        return remote(mine.at[pl.ds(pl.multiple_of(to * size, size), size)], slices.at[k], sems.at[0, k], sems.at[1, k], to, seq)

    def scatter_done(mine, slices, sems):
        total = mine[pl.ds(pl.multiple_of(dp * size, size), size)]
        for k in range(1, dp_count):
            scatter(mine, slices, sems, k).wait()
            total = total + slices[k]
        return total

    def swap(which, pieces, sems, k):
        return remote(pieces.at[which, 0], pieces.at[which, k], sems.at[0, dp_count + k - 1], sems.at[1, dp_count + k - 1], dp, peers[k - 1])

    def swap_done(which, pieces, sems):
        total = pieces[which, 0]
        for k in range(1, 4):
            swap(which, pieces, sems, k).wait()
            total = total + pieces[which, k]
        return total

    @pl.when(step == 0)
    def _():
        sums[...] = jnp.zeros_like(sums)
        barrier = pltpu.get_barrier_semaphore()
        for k in range(1, dp_count):
            pl.semaphore_signal(barrier, inc=1, device_id=(lax.rem(dp + k, dp_count), seq), device_id_type=MESH)
        for peer in peers:
            pl.semaphore_signal(barrier, inc=1, device_id=(dp, peer), device_id_type=MESH)
        pl.semaphore_wait(barrier, dp_count + 2)
        columns_of = [jnp.sum(chain_sums[i], axis=0, keepdims=True) for i in range(LOSS)]
        objective = 0.5 * jnp.sum(chain_sums[LOSS]) + 0.5 * SCORE_WEIGHT * jnp.sum(distill[...])
        columns_of.append(jnp.full((1, width), objective, F32))
        columns_of.append(jnp.zeros((PAIR - len(columns_of), width), F32))
        mine_a[...] = jnp.transpose(jnp.concatenate(columns_of, axis=0))
        for k in range(1, dp_count):
            scatter(mine_a, slices_a, a_sems, k).start()

    @pl.when(step == 2)
    def _():
        pieces[0, 0] = scatter_done(mine_a, slices_a, a_sems)
        for k in range(1, 4):
            swap(0, pieces, a_sems, k).start()

    @pl.when(step == 4)
    def _():
        early[...] = swap_done(0, pieces, a_sems)

    def hand_over(r):
        near_copy(r, 1).wait_recv()
        sent[r] = (partial[r, positions(across)].astype(F32) + near[r, 1].astype(F32)).astype(BF16)
        far_copy(r).start()

    def settle(r):
        near_copy(r, 0).wait_recv()
        far_copy(r).wait_recv()
        grad_low = kept[r] + near[r, 0].astype(F32) + far[r].astype(F32)
        unused, slope, bound = clip_parts(hidden[0].astype(F32), table[C_IN : C_IN + 1])
        grad_input[0] = grad_first[...] + grad_low * slope
        sums[3] += folded(grad_low * bound)

    @pl.when(step < rows)
    def _():
        attend_back_row(scale, table, s_query.at[0], s_key.at[0], s_value.at[0],
                        s_context.at[0], spread.at[0], probs.at[0], gaps.at[0],
                        grad_ctx, key_grads, value_grads, query_grads)

    @pl.when((step > 0) & (step <= rows))
    def _():
        hand_over(step - 1)

    @pl.when(step < rows)
    def _():
        back = query_grads[...]
        raw = table[A_Q : A_Q + 1] * s_query[0] + table[B_Q : B_Q + 1]
        sums[0] += folded(raw * back)
        query_grad = back * table[A_K : A_K + 1]
        sums[1] += folded(query_grad * s_query[0])
        sums[2] += folded(query_grad)
        pulled = dot_nn(key_grads[...], weights[1]) + dot_nn(value_grads[...], weights[2])
        partial[step] = pulled.astype(BF16)
        near_copy(step, 1).start()
        near_copy(step, 0).start()
        kept[step] = partial[step, positions(seq)].astype(F32) + dot_nn(
            (query_grad * table[A_Q : A_Q + 1]).astype(BF16), weights[0]
        )

    @pl.when(step > 1)
    def _():
        settle(step - 2)

    @pl.when(step == pl.num_programs(0) - 1)
    def _():
        columns_of = [jnp.sum(sums[i], axis=0, keepdims=True) for i in range(4)]
        columns_of.append(jnp.zeros((PAIR - len(columns_of), width), F32))
        mine_b[...] = jnp.transpose(jnp.concatenate(columns_of, axis=0))
        for k in range(1, dp_count):
            scatter(mine_b, slices_b, b_sems, k).start()
        for r in range(rows):
            near_copy(r, 0).wait_send()
            near_copy(r, 1).wait_send()
            far_copy(r).wait_send()
        pieces[1, 0] = scatter_done(mine_b, slices_b, b_sems)
        for k in range(1, 4):
            swap(1, pieces, b_sems, k).start()
        late[...] = swap_done(1, pieces, b_sems)


def signs_and_scale(latent):
    scale = jnp.mean(jnp.abs(latent), axis=0).astype(BF16)
    return jnp.sign(latent).astype(BF16).T, scale


def body(
    hidden_in,
    segment_ids,
    row_lengths,
    teacher_scores,
    teacher_hidden,
    w_query,
    w_key,
    w_value,
    w_out,
    w_up,
    w_down,
    b_query,
    b_value,
    b_out,
    b_up,
    b_down,
    norm1_gain,
    norm1_bias,
    norm2_gain,
    norm2_bias,
    clip_in,
    clip_ctx,
    clip_mid,
    clip_hid,
):
    rows, block, width = hidden_in.shape
    heads = teacher_scores.shape[1]
    head_dim = width // heads
    seq_len = segment_ids.shape[1]
    tokens = rows * block
    scale = head_dim ** (-0.5)
    place = lax.axis_index("seq")
    first = place * block

    dp_count = lax.axis_size("dp")
    size = w_query.shape[1]
    square = [signs_and_scale(w) for w in (w_query, w_key, w_value, w_out)]
    up_signs, up_scale = signs_and_scale(w_up)
    down = w_down.reshape(dp_count, 4, size, size)
    down_signs = jnp.sign(down).astype(BF16).transpose(1, 3, 0, 2).reshape(4, size, width)
    down_scale = jnp.mean(jnp.abs(w_down), axis=0).astype(BF16)
    pairs = jnp.stack([up_signs.reshape(4, size, width), down_signs], axis=1).reshape(8, size, width)
    own = jnp.concatenate([jnp.stack([s for s, _ in square]), pairs])
    own_vectors = jnp.concatenate(
        [jnp.stack([*(a for _, a in square), down_scale, b_query, b_value, b_out, b_down, norm1_gain, norm1_bias,
                    norm2_gain, norm2_bias, clip_in, clip_ctx, clip_mid]),
         up_scale.reshape(4, size), b_up.reshape(4, size), clip_hid.reshape(4, size)]
    )
    own_vectors = jnp.pad(own_vectors.T, ((0, 0), (0, PAIR - own_vectors.shape[0])))

    positions = jnp.arange(seq_len, dtype=jnp.int32)
    live = positions[None, :] < row_lengths[:, None]
    key_seg = jnp.stack([segment_ids, jnp.where(live, segment_ids, -1)], axis=1)
    own_seg = lax.dynamic_slice_in_dim(segment_ids, first, block, 1)
    query_live = lax.dynamic_slice_in_dim(live, first, block, 1)
    query_seg = jnp.stack([own_seg, jnp.where(query_live, own_seg, -2)], axis=2)

    def row_spec(*shape):
        return pl.BlockSpec((1,) + shape, lambda i: (i,) + (0,) * len(shape))

    def whole(array):
        return pl.BlockSpec(array.shape, lambda i: (0,) * array.ndim, pipeline_mode=pl.Buffered(1))

    three = pl.BlockSpec((3, width, width), lambda i: (0, 0, 0), pipeline_mode=pl.Buffered(1))
    attend_specs = [row_spec(block, width), row_spec(seq_len, width), row_spec(seq_len, width), row_spec(block, width),
                    row_spec(block, width), row_spec(heads, block, seq_len), row_spec(heads, block, seq_len),
                    pl.BlockSpec((8, seq_len), lambda i: (0, 0))]
    attend_shapes = [jax.ShapeDtypeStruct((rows, block, width), F32),
                     jax.ShapeDtypeStruct((rows, seq_len, width), BF16),
                     jax.ShapeDtypeStruct((rows, seq_len, width), BF16),
                     jax.ShapeDtypeStruct((rows, block, width), F32),
                     jax.ShapeDtypeStruct((rows, block, width), F32),
                     jax.ShapeDtypeStruct((rows, heads, block, seq_len), BF16),
                     jax.ShapeDtypeStruct((rows, heads, block, seq_len), BF16),
                     jax.ShapeDtypeStruct((8, seq_len), F32)]
    masks_specs = [row_spec(block, 2), row_spec(2, seq_len), row_spec(heads, block, seq_len)]
    anywhere = pl.BlockSpec(memory_space=pl.ANY)
    lines = dp_count // 2
    sems = pltpu.SemaphoreType.DMA
    if size % 32 == 0:
        full, table, s_query, s_key, s_value, s_context, spread, probs, gaps, distill = pl.pallas_call(
            functools.partial(first_kernel, scale, dp_count),
            grid=(rows,),
            in_specs=[anywhere, whole(own_vectors), anywhere, row_spec(block, width)] + masks_specs,
            out_specs=[anywhere, pl.BlockSpec((VECTORS, width), lambda i: (0, 0))] + attend_specs,
            out_shape=[jax.ShapeDtypeStruct((UNITS, width, width), BF16), jax.ShapeDtypeStruct((VECTORS, width), F32)]
            + attend_shapes,
            scratch_shapes=[
                pltpu.VMEM((rows, seq_len, width), BF16), pltpu.VMEM((width, PAIR), BF16), pltpu.VMEM((3, width, width), BF16),
                sems((2, UNITS, lines * lines)), sems((2, UNITS, lines)), sems((2, UNITS, dp_count)),
                sems((2, UNITS, dp_count)), sems((UNITS,)), sems((2, 3, rows)), sems((rows,)), sems((2, dp_count)), sems((3,)),
                pltpu.VMEM((block, seq_len), F32), pltpu.VMEM((block, seq_len), F32),
            ],
            compiler_params=pltpu.CompilerParams(collective_id=0, has_side_effects=True, vmem_limit_bytes=60 * 2**20),
        )(own, own_vectors, hidden_in, hidden_in, query_seg, key_seg, teacher_scores)
    else:
        full = lax.all_gather(own, "dp", axis=1, tiled=True)
        table = lax.all_gather(own_vectors, "dp", axis=0, tiled=True).astype(F32).T[:VECTORS]
        hidden_full = lax.all_gather(hidden_in, "seq", axis=1, tiled=True)
        s_query, s_key, s_value, s_context, spread, probs, gaps, distill = pl.pallas_call(
            functools.partial(plain_kernel, scale),
            grid=(rows,),
            in_specs=[row_spec(seq_len, width), row_spec(block, width), three, whole(table)] + masks_specs,
            out_specs=attend_specs,
            out_shape=attend_shapes,
            scratch_shapes=[pltpu.VMEM((block, seq_len), F32), pltpu.VMEM((block, seq_len), F32)],
            compiler_params=pltpu.CompilerParams(vmem_limit_bytes=60 * 2**20),
        )(hidden_full, hidden_in, full, table, query_seg, key_seg, teacher_scores)

    group = 2
    def group_spec(*shape):
        return pl.BlockSpec((group,) + shape, lambda i: (i,) + (0,) * len(shape))
    flat_spec = pl.BlockSpec((group * block, width), lambda i: (i, 0))
    live_column = query_live.astype(F32)[..., None]
    final, grad_first, grad_ctx, sums = pl.pallas_call(
        chain_kernel,
        grid=(rows // group,),
        in_specs=[whole(full), whole(table),
                  group_spec(block, width), group_spec(block, width), group_spec(block, 1), group_spec(block, width)],
        out_specs=[flat_spec, flat_spec, flat_spec,
                   pl.BlockSpec((SUMS, 8, width), lambda i: (0, 0, 0))],
        out_shape=[jax.ShapeDtypeStruct((tokens, width), BF16),
                   jax.ShapeDtypeStruct((tokens, width), F32),
                   jax.ShapeDtypeStruct((tokens, width), F32),
                   jax.ShapeDtypeStruct((SUMS, 8, width), F32)],
        scratch_shapes=[pltpu.VMEM((SUMS, 8, width), F32)]
        + [pltpu.VMEM((4, group * block, width), F32)] * 3,
        compiler_params=pltpu.CompilerParams(vmem_limit_bytes=60 * 2**20),
    )(full, table, hidden_in, teacher_hidden, live_column, s_context)
    one_spec = pl.BlockSpec((block, width), lambda i: (i, 0))
    if size % 32 == 0:
        def now_spec(*shape):
            return pl.BlockSpec((1,) + shape, lambda i: (jnp.minimum(i, rows - 1),) + (0,) * len(shape))

        def then_spec(*shape):
            return pl.BlockSpec((1,) + shape, lambda i: (jnp.maximum(i - 2, 0),) + (0,) * len(shape))

        grad_input, early, late = pl.pallas_call(
            functools.partial(last_kernel, scale, dp_count),
            grid=(rows + 2,),
            in_specs=[three, whole(table), now_spec(block, width), now_spec(seq_len, width), now_spec(seq_len, width),
                      now_spec(block, width), now_spec(block, width), now_spec(heads, block, seq_len),
                      now_spec(heads, block, seq_len), pl.BlockSpec((block, width), lambda i: (jnp.minimum(i, rows - 1), 0)),
                      then_spec(block, width), pl.BlockSpec((block, width), lambda i: (jnp.maximum(i - 2, 0), 0)),
                      whole(sums), whole(distill)],
            out_specs=[then_spec(block, width)] + [pl.BlockSpec((size, PAIR), lambda i: (0, 0))] * 2,
            out_shape=[jax.ShapeDtypeStruct((rows, block, width), F32)] + [jax.ShapeDtypeStruct((size, PAIR), F32)] * 2,
            scratch_shapes=[
                pltpu.VMEM((seq_len, width), BF16), pltpu.VMEM((seq_len, width), BF16), pltpu.VMEM((block, width), F32),
                pltpu.VMEM((rows, seq_len, width), BF16), pltpu.VMEM((rows, block, width), F32),
                pltpu.VMEM((rows, 2, block, width), BF16), pltpu.VMEM((rows, block, width), BF16),
                pltpu.VMEM((rows, block, width), BF16), pltpu.VMEM((4, 8, width), F32),
                pltpu.VMEM((width, PAIR), F32), pltpu.VMEM((dp_count, size, PAIR), F32),
                pltpu.VMEM((width, PAIR), F32), pltpu.VMEM((dp_count, size, PAIR), F32),
                pltpu.VMEM((2, 4, size, PAIR), F32),
                sems((2, rows, 2)), sems((2, rows)), sems((2, dp_count + 3)), sems((2, dp_count + 3)),
            ],
            compiler_params=pltpu.CompilerParams(collective_id=1, has_side_effects=True, vmem_limit_bytes=60 * 2**20),
        )(full, table, s_query, s_key, s_value, s_context, spread, probs, gaps, grad_ctx, hidden_in, grad_first, sums, distill)
        early, late = early.T, late.T
        objective = early[LOSS, 0]
        sums = early[:16].at[G_K].set(late[0]).at[G_Q].set(late[1]).at[G_BQ].set(late[2]).at[G_CIN].set(late[3])
        wide_sums = early[16:28].reshape(3, 4 * size)
    else:
        pulled_in, own_in, more = pl.pallas_call(
            functools.partial(back_kernel, scale),
            grid=(rows,),
            in_specs=[three, whole(table),
                      row_spec(block, width), row_spec(seq_len, width), row_spec(seq_len, width), row_spec(block, width),
                      row_spec(block, width), row_spec(heads, block, seq_len), row_spec(heads, block, seq_len), one_spec],
            out_specs=[row_spec(seq_len, width), one_spec, pl.BlockSpec((3, 8, width), lambda i: (0, 0, 0))],
            out_shape=[jax.ShapeDtypeStruct((rows, seq_len, width), BF16),
                       jax.ShapeDtypeStruct((tokens, width), F32),
                       jax.ShapeDtypeStruct((3, 8, width), F32)],
            scratch_shapes=[pltpu.VMEM((seq_len, width), BF16), pltpu.VMEM((seq_len, width), BF16),
                            pltpu.VMEM((block, width), F32)],
            compiler_params=pltpu.CompilerParams(vmem_limit_bytes=60 * 2**20),
        )(full, table, s_query, s_key, s_value, s_context, spread, probs, gaps, grad_ctx)
        sums = sums.at[G_K].set(more[0]).at[G_Q].set(more[1]).at[G_BQ].set(more[2])
        objective = 0.5 * jnp.sum(sums[LOSS]) + 0.5 * SCORE_WEIGHT * jnp.sum(distill)

        crossed = lax.psum_scatter(pulled_in, "seq", scatter_dimension=1, tiled=True).astype(F32)
        grad_low = own_in + crossed.reshape(tokens, width)
        inputs = hidden_in.astype(F32).reshape(tokens, width)
        unused, in_slope, in_bound = clip_parts(inputs, table[C_IN : C_IN + 1])
        grad_input = grad_first + grad_low * in_slope
        sums = jnp.sum(sums, axis=1)
        wide_sums = sums[16:28]
        sums = sums[:16].at[G_CIN].set(columns(grad_low * in_bound)[0])
        sums, wide_sums, objective = lax.psum((sums, wide_sums, objective), ("dp", "seq"))
        at = lax.axis_index("dp")
        sums = lax.dynamic_slice_in_dim(sums, at * size, size, 1)
        wide_sums = lax.dynamic_slice_in_dim(wide_sums, at * size, size, 1).reshape(3, 4 * size)
    loss = objective / (lax.axis_size("dp") * rows * seq_len)
    grads = [
        jnp.sign(w) * (s / w.shape[0])
        for w, s in zip(
            (w_query, w_key, w_value, w_out, w_up, w_down),
            (sums[0], sums[1], sums[2], sums[3], wide_sums[0], sums[4]),
        )
    ]
    return (
        final.reshape(rows, block, width).astype(BF16),
        loss,
        grad_input.reshape(rows, block, width),
        *grads,
        sums[5],
        sums[6],
        sums[7],
        wide_sums[1],
        sums[8],
        sums[9],
        sums[10],
        sums[11],
        sums[12],
        sums[13],
        sums[14],
        sums[15],
        wide_sums[2],
    )


def solution(mesh):
    rows = P("dp", "seq", None)
    cols = P(None, "dp")
    vec = P("dp")
    return jax.shard_map(
        body,
        mesh=mesh,
        in_specs=(rows, P("dp", None), vec, P("dp", None, "seq", None), rows)
        + (cols,) * 6
        + (vec,) * 13,
        out_specs=(rows, P(), rows) + (cols,) * 6 + (vec,) * 13,
        check_vma=False,
    )
```

```python
import functools

import jax
import jax.numpy as jnp
from jax import lax
from jax.experimental import pallas as pl
from jax.experimental.pallas import tpu as pltpu
from jax.sharding import PartitionSpec as P

EPS = 1e-05
SCORE_WEIGHT = 0.0625
NEGATIVE = -1e30
F32 = jnp.float32
BF16 = jnp.bfloat16
PAIR = 128
HEAD = 64
GROUP = 256
A_Q, A_K, A_V, A_O, A_D, B_Q, B_V, B_O, B_D, G1, S1, G2, S2, C_IN, C_CTX, C_MID = range(16)
A_U, B_U, C_HID, VECTORS = 16, 20, 24, 32
G_Q, G_K, G_V, G_O, G_D, G_BQ, G_BV, G_BO, G_BD, G_G1, G_S1, G_G2, G_S2, G_CIN, G_CCTX, G_CMID = range(16)
G_U, G_BU, G_CHID, LOSS, SUMS = 16, 20, 24, 28, 29


def dot_nt(left, right):
    return lax.dot_general(left, right, (((1,), (1,)), ((), ())), preferred_element_type=F32)


def dot_nn(left, right):
    return lax.dot_general(left, right, (((1,), (0,)), ((), ())), preferred_element_type=F32)


def dot_tn(left, right):
    return lax.dot_general(left, right, (((0,), (0,)), ((), ())), preferred_element_type=F32)


def columns(value):
    return jnp.sum(value, axis=0, keepdims=True)


def clip_parts(value, bound):
    ratio = value / bound
    bent = jnp.tanh(ratio)
    slope = 1.0 - bent * bent
    return bound * bent, slope, bent - ratio * slope


def norm_parts(value, gain, shift):
    centre = value - jnp.mean(value, axis=-1, keepdims=True)
    inverse = lax.rsqrt(jnp.mean(centre * centre, axis=-1, keepdims=True) + EPS)
    unit = centre * inverse
    return unit * gain + shift, unit, inverse


def norm_back(grad, unit, inverse, gain):
    scaled = grad * gain
    return inverse * (
        scaled
        - jnp.mean(scaled, axis=-1, keepdims=True)
        - unit * jnp.mean(scaled * unit, axis=-1, keepdims=True)
    )


def stacked(value):
    lane = lax.broadcasted_iota(jnp.int32, value.shape, 1)
    zero = jnp.zeros_like(value)
    return jnp.concatenate([jnp.where(lane // HEAD == i, value, zero) for i in range(GROUP // HEAD)], axis=0)


def by_head(parts):
    shape = jnp.broadcast_shapes(parts[0].shape, (1, GROUP))
    lane = lax.broadcasted_iota(jnp.int32, shape, 1)
    result = parts[-1]
    for i in range(len(parts) - 2, -1, -1):
        result = jnp.where(lane < (i + 1) * HEAD, parts[i], result)
    return result


def folded(value):
    return jnp.sum(value.reshape(value.shape[0] // 8, 8, value.shape[1]), axis=0)


def mask_row(segments, lengths, row, start, bias, counted):
    block, seq_len = bias.shape
    keys = segments[pl.ds(row, 1), :].astype(F32)
    mine = keys[:, :block]
    for i in range(1, seq_len // block):
        mine = jnp.where(start == i * block, keys[:, i * block : (i + 1) * block], mine)
    queries = jnp.transpose(jnp.broadcast_to(mine, (block, block)))
    same = jnp.concatenate([queries] * (seq_len // block), axis=1) == keys
    length = lengths[row]
    query_at = start + lax.broadcasted_iota(jnp.int32, (block, seq_len), 0)
    key_at = lax.broadcasted_iota(jnp.int32, (block, seq_len), 1)
    bias[...] = jnp.where(same, 0.0, NEGATIVE)
    counted[...] = jnp.where(same & (query_at < length) & (key_at < length), 1.0, 0.0)


def signed(value):
    return jnp.where(value > 0, 1.0, jnp.where(value < 0, -1.0, 0.0))


def pack(squares, up, down, vectors_in, own, own_vectors, which):
    size = own.shape[1]
    width = own.shape[2]
    lane = lax.broadcasted_iota(jnp.int32, own_vectors.shape, 1)

    def put(unit, turned, kind):
        own[unit] = signed(turned).astype(BF16)
        scale = jnp.sum(jnp.abs(turned), axis=1, keepdims=True) / width
        own_vectors[...] = jnp.where(lane == kind, scale.astype(BF16).astype(F32), own_vectors[...])

    if which == 0:
        size = own.shape[1]
        zeros = functools.partial(jnp.zeros, dtype=F32)
        columns = jnp.transpose(
            jnp.concatenate([zeros((5, size)), vectors_in[0][...].astype(F32), zeros((PAIR - 16, size))], axis=0)
        )
        wide = jnp.transpose(
            jnp.concatenate([vectors_in[1][...].astype(F32), zeros((PAIR - 2, 4 * size))], axis=0)
        )
        for kind in range(2):
            for i in range(4):
                columns = jnp.where(lane == B_U + 4 * kind + i, wide[i * size : (i + 1) * size, kind : kind + 1], columns)
        own_vectors[...] = columns
        for unit in range(3):
            put(unit, squares[unit][...], A_Q + unit)
        return
    put(3, squares[3][...], A_O)
    turned = jnp.transpose(up[...])
    for i in range(4):
        part = turned[i * size : (i + 1) * size]
        own[4 + 2 * i] = signed(part).astype(BF16)
        scale = jnp.sum(jnp.abs(part), axis=1, keepdims=True) / width
        own_vectors[...] = jnp.where(lane == A_U + i, scale.astype(BF16).astype(F32), own_vectors[...])
    groups = down.shape[1] // (4 * size)
    scale = jnp.sum(jnp.abs(down[...]), axis=1, keepdims=True) / down.shape[1]
    own_vectors[...] = jnp.where(lane == A_D, scale.astype(BF16).astype(F32), own_vectors[...])
    straight = jnp.transpose(signed(down[...]))
    for i in range(4):
        part = jnp.concatenate([straight[(4 * j + i) * size : (4 * j + i + 1) * size] for j in range(groups)], axis=0)
        own[5 + 2 * i] = jnp.transpose(part).astype(BF16)


def project_row(hidden, own_hidden, sq, sk, sv, small, s_query, s_key, s_value, bounds_in, own_bounds):
    c_in = small[C_IN : C_IN + 1]
    inverse_in = 1.0 / c_in
    ratio = hidden[...].astype(F32) * inverse_in
    bent = jnp.tanh(ratio)
    bounds_in[...] = (bent - ratio * (1.0 - bent * bent)).astype(BF16)
    low = (c_in * bent).astype(BF16)
    s_key[...] = dot_nt(low, sk[...]).astype(BF16)
    s_value[...] = dot_nt(low, sv[...]).astype(BF16)
    ratio = own_hidden[...].astype(F32) * inverse_in
    bent = jnp.tanh(ratio)
    own_bounds[...] = (bent - ratio * (1.0 - bent * bent)).astype(BF16)
    low = (c_in * bent).astype(BF16)
    s_query[...] = dot_nt(low, sq[...])


def attend_row(
    scale, small, teacher, s_query, s_key, s_value, s_context, spread, probs, gaps, distill, bias, counted,
    first, last,
):
    block, width = s_query.shape

    def some(index, carry):
        at = pl.ds(pl.multiple_of(index * GROUP, GROUP), GROUP)
        query = (
            (small[A_Q : A_Q + 1, at] * s_query[:, at] + small[B_Q : B_Q + 1, at])
            * (small[A_K : A_K + 1, at] * scale)
        ).astype(BF16)
        scores = dot_nt(stacked(query), s_key[:, at])
        expos, inverses = [], []
        sums = jnp.zeros((8, scores.shape[1]), F32)
        for head in range(GROUP // HEAD):
            mine = scores[head * block : (head + 1) * block]
            gap = (mine - teacher[GROUP // HEAD * index + head].astype(F32)) * counted[...]
            sums = sums + folded(gap * gap)
            gaps[GROUP // HEAD * index + head] = (gap * SCORE_WEIGHT).astype(BF16)
            masked = mine + bias[...]
            expo = jnp.exp(masked - jnp.max(masked, axis=-1, keepdims=True))
            inverses.append(1.0 / jnp.sum(expo, axis=-1, keepdims=True))
            expo = expo.astype(BF16)
            probs[GROUP // HEAD * index + head] = expo
            expos.append(expo)
        distill[...] += sums
        both = dot_nn(jnp.concatenate(expos, axis=0), s_value[:, at])
        inverse = by_head(inverses)
        s_context[:, at] = by_head([both[h * block : (h + 1) * block] for h in range(GROUP // HEAD)]) * inverse
        spread[:, at] = inverse
        return carry

    lax.fori_loop(first, last, some, 0)


MESH = pl.DeviceIdType.MESH
UNITS = 12
STEPS = 10
SHARED = (6, 7)

def remote(source, target, send, recv, dp, seq):
    return pltpu.make_async_remote_copy(
        src_ref=source, dst_ref=target, send_sem=send, recv_sem=recv, device_id=(dp, seq), device_id_type=MESH
    )

class Streams:
    def __init__(self, lines, own, full, z_sems, x_sems, y_sems, c_sems, l_sems):
        self.lines, self.own, self.full = lines, own, full
        self.z_sems, self.x_sems, self.y_sems, self.c_sems, self.l_sems = z_sems, x_sems, y_sems, c_sems, l_sems
        self.dp, self.seq = lax.axis_index("dp"), lax.axis_index("seq")
        self.zi, self.xi = self.dp // 2, self.dp % 2
        self.yi, self.ci = self.seq // 2, self.seq % 2
        self.size = own.shape[1]
        self.half = self.size // 2

    def unit(self, t, partner=False):
        if t in SHARED:
            return SHARED[0] + 2 * (t - SHARED[0]) + (1 - self.yi if partner else self.yi)
        return t if t < SHARED[0] else t + 2

    def piece(self, u, dp):
        start = pl.multiple_of(dp * self.size + self.ci * self.half, self.half)
        return self.full.at[u, pl.ds(start, self.half)]

    def own_piece(self, u):
        return self.own.at[u, pl.ds(pl.multiple_of(self.ci * self.half, self.half), self.half)]

    def z_copy(self, u, src, to):
        place = self.piece(u, src * 2 + self.xi)
        return remote(self.own_piece(u) if src is self.zi else place, place,
                      self.z_sems.at[0, u, to + self.lines * src], self.z_sems.at[1, u, src], to * 2 + self.xi, self.seq)

    def x_copy(self, u, src):
        place = self.piece(u, src * 2 + self.xi)
        return remote(self.own_piece(u) if src is self.zi else place, place, self.x_sems.at[0, u, src], self.x_sems.at[1, u, src],
                      self.zi * 2 + 1 - self.xi, self.seq)

    def x_arrival(self, u, src):
        place = self.piece(u, src * 2 + 1 - self.xi)
        return remote(place, place, self.x_sems.at[0, u, src], self.x_sems.at[1, u, src], self.zi * 2 + 1 - self.xi, self.seq)

    def y_copy(self, u, dp):
        place = self.piece(u, dp)
        return remote(place, place, self.y_sems.at[0, u, dp], self.y_sems.at[1, u, dp], self.dp, (1 - self.yi) * 2 + self.ci)

    def c_copy(self, u, dp):
        place = self.piece(u, dp)
        return remote(place, place, self.c_sems.at[0, u, dp], self.c_sems.at[1, u, dp], self.dp, self.yi * 2 + 1 - self.ci)

    def local_copy(self, u):
        start = pl.multiple_of(self.dp * self.size, self.size)
        return pltpu.make_async_copy(self.own.at[u], self.full.at[u, pl.ds(start, self.size)], self.l_sems.at[u])

    def each_row(self, run):
        for k in range(1, self.lines):
            pl.when(self.zi >= k)(functools.partial(run, self.zi - k, True))
            pl.when(self.zi + k < self.lines)(functools.partial(run, self.zi + k, False))

    def neighbours(self, run):
        pl.when(self.zi > 0)(lambda: run(self.zi - 1))
        pl.when(self.zi < self.lines - 1)(lambda: run(self.zi + 1))

    def relay(self, src, below, run):
        if below:
            pl.when(self.zi < self.lines - 1)(lambda: run(self.zi + 1))
        else:
            pl.when(self.zi > 0)(lambda: run(self.zi - 1))

    def launch(self, t):
        u = self.unit(t)
        self.x_copy(u, self.zi).start()
        self.neighbours(lambda to: self.z_copy(u, self.zi, to).start())

    def at_distance(self, k, run):
        if k == 0:
            run(self.zi, None)
        else:
            pl.when(self.zi >= k)(functools.partial(run, self.zi - k, True))
            pl.when(self.zi + k < self.lines)(functools.partial(run, self.zi + k, False))

    def along_z(self, t, k):
        u = self.unit(t)
        def run(src, below):
            self.z_copy(u, src, self.zi).wait_recv()
            self.relay(src, below, lambda to: self.z_copy(u, src, to).start())
            self.x_copy(u, src).start()
            self.spread(t, u, src * 2 + self.xi)
        self.at_distance(k, run)

    def over_x(self, t, k):
        u = self.unit(t)
        def run(src, below):
            self.x_arrival(u, src).wait_recv()
            self.spread(t, u, src * 2 + 1 - self.xi)
        self.at_distance(k, run)

    def spread(self, t, u, dp):
        if t in SHARED:
            self.y_copy(u, dp).start()
        self.c_copy(u, dp).start()

    def others(self, run):
        self.each_row(lambda src, below: run(src * 2 + self.xi))
        run(self.zi * 2 + 1 - self.xi)
        self.each_row(lambda src, below: run(src * 2 + 1 - self.xi))

    def over_y(self, t):
        u = self.unit(t, True)
        def run(dp):
            self.y_copy(u, dp).wait_recv()
            self.c_copy(u, dp).start()
        self.others(run)

    def arrived(self, u):
        self.others(lambda dp: self.c_copy(u, dp).wait_recv())
        self.local_copy(u).wait()

    def finish(self):
        for t in range(STEPS):
            u = self.unit(t)
            self.x_copy(u, self.zi).wait_send()
            self.neighbours(lambda to: self.z_copy(u, self.zi, to).wait_send())
            def run(src, below):
                self.relay(src, below, lambda to: self.z_copy(u, src, to).wait_send())
                self.x_copy(u, src).wait_send()
            self.each_row(run)
            if t in SHARED:
                self.others(lambda dp: self.y_copy(u, dp).wait_send())
        for u in range(UNITS):
            self.others(lambda dp: self.c_copy(u, dp).wait_send())


def greet(dp_count):
    dp, seq = lax.axis_index("dp"), lax.axis_index("seq")
    barrier = pltpu.get_barrier_semaphore()
    for k in range(1, dp_count):
        pl.semaphore_signal(barrier, inc=1, device_id=(lax.rem(dp + k, dp_count), seq), device_id_type=MESH)
    pl.semaphore_signal(barrier, inc=1, device_id=(dp, seq // 2 * 2 + 1 - seq % 2), device_id_type=MESH)
    pl.semaphore_signal(barrier, inc=1, device_id=(dp, (1 - seq // 2) * 2 + seq % 2), device_id_type=MESH)
    pl.semaphore_wait(barrier, dp_count + 1)

NEAR = 3


def first_kernel(
    scale, dp_count, lengths, segments, w_query, w_key, w_value, w_out, w_up, w_down, vectors_in, wide_in,
    hidden, own_hidden, teacher,
    full, table, s_query, s_key, s_value, s_context, spread, probs, gaps, bounds_in, own_bounds, distill,
    own, own_columns, own_vectors, whole, vectors, weights, z_sems, x_sems, y_sems, c_sems, l_sems, h_sems, o_sems, v_sems, w_sems, bias, counted,
):
    step = pl.program_id(0)
    rows, block = hidden.shape[0], hidden.shape[1]
    s = Streams(dp_count // 2, own, full, z_sems, x_sems, y_sems, c_sems, l_sems)
    across, beside = (1 - s.yi) * 2 + s.ci, s.yi * 2 + 1 - s.ci

    def place(r, seq):
        return whole.at[r, pl.ds(pl.multiple_of(seq * block, block), block)]

    def to_chip(r):
        return remote(hidden.at[r], place(r, s.seq), h_sems.at[0, 0, r], h_sems.at[1, 0, r], s.dp, across)

    def to_core(r):
        return remote(hidden.at[r], place(r, s.seq), h_sems.at[0, 1, r], h_sems.at[1, 1, r], s.dp, beside)

    def passed_on(r):
        return remote(place(r, across), place(r, across), h_sems.at[0, 2, r], h_sems.at[1, 2, r], s.dp, beside)

    def kept(r):
        return pltpu.make_async_copy(hidden.at[r], place(r, s.seq), o_sems.at[r])

    def hidden_pump(r):
        to_chip(r).wait_recv()
        passed_on(r).start()
        if r + NEAR < rows:
            to_chip(r + NEAR).start()

    def vector_copy(k):
        mine = vectors.at[pl.ds(pl.multiple_of(s.dp * s.size, s.size), s.size)]
        return remote(own_vectors, mine, v_sems.at[0, k], v_sems.at[1, k], lax.rem(s.dp + k, dp_count), s.seq)

    def fetch(u):
        return pltpu.make_async_copy(full.at[u], weights.at[u], w_sems.at[u])

    def point(r, j):
        if j == 0 and r + 3 < rows:
            hidden_pump(r + 3)
        for t in range(3, STEPS):
            at = 4 * r + j - 3 * (t - 3)
            if at == 0 and t + 2 < STEPS:
                s.launch(t + 2)
            if at in (0, 3, 6):
                s.along_z(t, at // 3 + 1)
            if at in (1, 4, 7, 10):
                s.over_x(t, at // 3)
            if t in SHARED and at == 13:
                s.over_y(t)

    def points(j):
        for r in range(rows):
            pl.when(step == r)(functools.partial(point, r, j))

    @pl.when(step == 0)
    def _():
        distill[...] = jnp.zeros_like(distill)
        latents = (w_query, w_key, w_value, w_out), w_up, w_down
        pack(*latents, (vectors_in, wide_in), own, own_columns, 0)
        greet(dp_count)
        for r in range(NEAR):
            to_chip(r).start()
        for t in range(3):
            s.launch(t)
        pack(*latents, (vectors_in, wide_in), own, own_columns, 1)
        own_vectors[...] = own_columns[...].astype(BF16)
        for k in range(1, dp_count):
            vector_copy(k).start()
        for u in range(UNITS):
            s.local_copy(u).start()
        for r in range(rows):
            to_core(r).start()
            kept(r).start()
        mine = pl.ds(pl.multiple_of(s.dp * s.size, s.size), s.size)
        vectors[mine] = own_vectors[...]
        for k in range(1, s.lines):
            for t in range(3):
                s.along_z(t, k)
                s.over_x(t, k - 1)
            hidden_pump(k - 1)
        s.launch(3)
        for t in range(3):
            s.over_x(t, s.lines - 1)
        s.launch(4)
        for k in range(1, dp_count):
            vector_copy(k).wait()
        table[...] = jnp.transpose(vectors[...].astype(F32))[: table.shape[0]]
        for u in range(3):
            s.arrived(u)
            fetch(u).start()
        for u in range(3):
            fetch(u).wait()

    points(0)
    for r in range(rows):
        @pl.when(step == r)
        def _(r=r):
            kept(r).wait()
            to_core(r).wait_recv()
            passed_on(r).wait_recv()

    project_row(whole.at[step], own_hidden.at[0], weights.at[0], weights.at[1], weights.at[2], table,
                s_query.at[0], s_key.at[0], s_value.at[0], bounds_in.at[0], own_bounds.at[0])
    mask_row(segments, lengths, step, s.seq * block, bias, counted)
    count = s_query.shape[2] // GROUP
    for j in range(3):
        points(j + 1)
        attend_row(scale, table, teacher.at[0], s_query.at[0], s_key.at[0], s_value.at[0],
                   s_context.at[0], spread.at[0], probs.at[0], gaps.at[0], distill, bias, counted,
                   count * j // 3, count * (j + 1) // 3)

    @pl.when(step == rows - 1)
    def _():
        for u in range(3, UNITS):
            s.arrived(u)
        s.finish()
        for r in range(rows):
            to_chip(r).wait_send()
            to_core(r).wait_send()
            passed_on(r).wait_send()


def plain_kernel(
    scale, lengths, segments, whole, own_hidden, weights, table, teacher,
    s_query, s_key, s_value, s_context, spread, probs, gaps, bounds_in, own_bounds, distill, bias, counted,
):
    @pl.when(pl.program_id(0) == 0)
    def _():
        distill[...] = jnp.zeros_like(distill)

    project_row(whole.at[0], own_hidden.at[0], weights.at[0], weights.at[1], weights.at[2], table,
                s_query.at[0], s_key.at[0], s_value.at[0], bounds_in.at[0], own_bounds.at[0])
    mask_row(segments, lengths, pl.program_id(0), lax.axis_index("seq") * own_hidden.shape[1], bias, counted)
    attend_row(scale, table, teacher.at[0], s_query.at[0], s_key.at[0], s_value.at[0],
               s_context.at[0], spread.at[0], probs.at[0], gaps.at[0], distill, bias, counted, 0, s_query.shape[2] // GROUP)


def chain(stored, weights, arrivals, small, hidden, teacher, live, s_context, sums, final_out, grad_first_out,
          grad_ctx_out, pres, slopes, bounds):
    def vec(i):
        return small[i : i + 1]

    step = pl.program_id(0)

    def fetch(unit):
        return pltpu.make_async_copy(stored.at[3 + unit], weights.at[unit], arrivals.at[unit])

    def needed(unit):
        pass

    @pl.when(step == 0)
    def _():
        for unit in range(UNITS - 3):
            fetch(unit).start()
        for unit in range(UNITS - 3):
            fetch(unit).wait()

    def add(i, value):
        sums[i] += folded(value)

    width = hidden.shape[1]
    inputs = hidden[...].astype(F32)
    context = vec(A_V) * s_context[...] + vec(B_V)
    context_low = clip_parts(context, vec(C_CTX))[0]
    needed(0)
    s_out = dot_nt(context_low.astype(BF16), weights[0])
    normed, unit1, inverse1 = norm_parts(inputs + vec(A_O) * s_out + vec(B_O), vec(G1), vec(S1))
    normed_low, mid_slope, mid_bound = clip_parts(normed, vec(C_MID))
    normed_low = normed_low.astype(BF16)
    s_down = 0.0
    for i in range(4):
        needed(1 + 2 * i)
        s_up = dot_nt(normed_low, weights[1 + 2 * i])
        pres[i] = s_up
        pre = vec(A_U + i) * s_up + vec(B_U + i)
        phi = 0.5 + 0.5 * lax.erf(pre * (0.5**0.5))
        act_slope = phi + pre * (jnp.exp(-0.5 * pre * pre) * 0.3989422804014327)
        hidden_low, slope, bound = clip_parts(pre * phi, vec(C_HID + i))
        slopes[i] = (slope * act_slope)
        bounds[i] = bound
        needed(2 + 2 * i)
        s_down = s_down + dot_nt(hidden_low.astype(BF16), weights[2 + 2 * i])
    final, unit2, inverse2 = norm_parts(normed + vec(A_D) * s_down + vec(B_D), vec(G2), vec(S2))
    final_out[...] = final.astype(BF16)
    errors = jnp.where(live, final - teacher[...].astype(F32), 0.0)
    add(LOSS, errors * errors)
    add(G_G2, errors * unit2)
    add(G_S2, errors)
    grad_second = norm_back(errors, unit2, inverse2, vec(G2))
    add(G_D, grad_second * s_down)
    add(G_BD, grad_second)
    branch = (grad_second * vec(A_D)).astype(BF16)
    grad_mid = 0.0
    for i in range(4):
        grad_hid = dot_nn(branch, weights[2 + 2 * i])
        add(G_CHID + i, grad_hid * bounds[i])
        up_grad = grad_hid * slopes[i]
        add(G_BU + i, up_grad)
        add(G_U + i, up_grad * pres[i])
        grad_mid = grad_mid + dot_nn((up_grad * vec(A_U + i)).astype(BF16), weights[1 + 2 * i])
    add(G_CMID, grad_mid * mid_bound)
    grad_normed = grad_second + grad_mid * mid_slope
    add(G_G1, grad_normed * unit1)
    add(G_S1, grad_normed)
    grad_first = norm_back(grad_normed, unit1, inverse1, vec(G1))
    grad_first_out[...] = grad_first
    add(G_O, grad_first * s_out)
    add(G_BO, grad_first)
    grad_ctx_low = dot_nn((grad_first * vec(A_O)).astype(BF16), weights[0])
    unused, ctx_slope, ctx_bound = clip_parts(vec(A_V) * s_context[...] + vec(B_V), vec(C_CTX))
    add(G_CCTX, grad_ctx_low * ctx_bound)
    grad_ctx = grad_ctx_low * ctx_slope
    add(G_V, grad_ctx * s_context[...])
    add(G_BV, grad_ctx)
    grad_ctx_out[...] = grad_ctx


def attend_back_row(scale, small, s_query, s_key, s_value, s_context, spread, probs, gaps,
                    grad_ctx, key_grads, value_grads, query_grads):
    block, width = s_query.shape

    def some(index, carry):
        at = pl.ds(pl.multiple_of(index * GROUP, GROUP), GROUP)
        raw = small[A_Q : A_Q + 1, at] * s_query[:, at] + small[B_Q : B_Q + 1, at]
        query = stacked((raw * (small[A_K : A_K + 1, at] * scale)).astype(BF16))
        pulled = grad_ctx[:, at] * small[A_V : A_V + 1, at] * spread[:, at]
        product = pulled * s_context[:, at]
        lane = lax.broadcasted_iota(jnp.int32, product.shape, 1)
        deltas = [
            jnp.sum(jnp.where(lane // HEAD == h, product, 0.0), axis=-1, keepdims=True) for h in range(GROUP // HEAD)
        ]
        accum_grad = stacked(pulled.astype(BF16))
        prob_grad = dot_nt(accum_grad, s_value[:, at])
        score_grads, expos = [], []
        for head, delta in enumerate(deltas):
            expo = probs[GROUP // HEAD * index + head]
            expos.append(expo)
            mine = prob_grad[head * block : (head + 1) * block]
            score_grads.append(
                (expo.astype(F32) * (mine - delta) + gaps[GROUP // HEAD * index + head].astype(F32)).astype(BF16)
            )
        score_grad = jnp.concatenate(score_grads, axis=0)
        both = dot_nn(score_grad, s_key[:, at])
        query_grads[:, at] = (
            by_head([both[h * block : (h + 1) * block] for h in range(GROUP // HEAD)]) * scale
        )
        key_grads[:, at] = dot_tn(score_grad, query).astype(BF16)
        value_grads[:, at] = dot_tn(jnp.concatenate(expos, axis=0), accum_grad).astype(BF16)
        return carry

    lax.fori_loop(0, width // GROUP, some, 0, unroll=width // GROUP)


def chain_kernel(row_count, lengths, stored, small, hidden, teacher, s_context, final, grad_first, grad_ctx, sums_out,
                 weights, arrivals, sums, pres, slopes, bounds):
    step = pl.program_id(0)

    @pl.when(step == 0)
    def _():
        sums[...] = jnp.zeros_like(sums)

    flat = hidden.shape
    rows, block = row_count, flat[0] // row_count
    at = lax.broadcasted_iota(jnp.int32, flat, 0)
    limit = jnp.full(flat, lengths[step * rows], jnp.int32)
    for r in range(1, rows):
        limit = jnp.where(at < r * block, limit, lengths[step * rows + r])
    live = lax.axis_index("seq") * block + lax.rem(at, block) < limit
    chain(stored, weights, arrivals, small, hidden, teacher, live, s_context, sums, final, grad_first,
          grad_ctx, pres, slopes, bounds)

    @pl.when(step == pl.num_programs(0) - 1)
    def _():
        sums_out[...] = sums[...]


def back_kernel(scale, weights, small, s_query, s_key, s_value, s_context, spread, probs, gaps, grad_ctx,
                pulled_in, own_in, sums, key_grads, value_grads, query_grads):
    step = pl.program_id(0)

    @pl.when(step == 0)
    def _():
        sums[...] = jnp.zeros_like(sums)

    attend_back_row(scale, small, s_query.at[0], s_key.at[0], s_value.at[0],
                    s_context.at[0], spread.at[0], probs.at[0], gaps.at[0],
                    grad_ctx, key_grads, value_grads, query_grads)
    back = query_grads[...]
    raw = small[A_Q : A_Q + 1] * s_query[0] + small[B_Q : B_Q + 1]
    sums[0] += folded(raw * back)
    query_grad = back * small[A_K : A_K + 1]
    sums[1] += folded(query_grad * s_query[0])
    sums[2] += folded(query_grad)
    own_in[...] = dot_nn((query_grad * small[A_Q : A_Q + 1]).astype(BF16), weights[0])
    pulled_in[0] = (dot_nn(key_grads[...], weights[1]) + dot_nn(value_grads[...], weights[2])).astype(BF16)


def last_kernel(
    scale, dp_count, weights, table, s_query, s_key, s_value, s_context, spread, probs, gaps, grad_ctx,
    hidden, grad_first, bounds_in, own_bounds, chain_sums, distill,
    grad_input, early, late,
    query_grads, partial, kept, near, sent, far, sums,
    mine_a, slices_a, mine_b, slices_b, pieces, pieces_b,
    near_sems, far_sems, a_sems, b_sems,
):
    step = pl.program_id(0)
    rows = partial.shape[1]
    block, width = s_query.shape[1], s_query.shape[2]
    size = width // dp_count
    dp, seq = lax.axis_index("dp"), lax.axis_index("seq")
    yi, ci = seq // 2, seq % 2
    across, beside = (1 - yi) * 2 + ci, yi * 2 + 1 - ci
    corner = (1 - yi) * 2 + 1 - ci
    peers = (across, beside, corner)

    def positions(place):
        return pl.ds(pl.multiple_of(place * block, block), block)

    def near_copy(r, kind, which):
        place = beside if which == 0 else corner
        return remote(partial.at[kind, r, positions(place)], near.at[kind, r, which], near_sems.at[0, kind, r, which],
                      near_sems.at[1, kind, r, which], dp, beside)

    def far_copy(r):
        return remote(sent.at[r], far.at[r], far_sems.at[0, r], far_sems.at[1, r], dp, across)

    def scatter(mine, slices, sems, k):
        to = lax.rem(dp + k, dp_count)
        return remote(mine.at[to], slices.at[k], sems.at[0, k], sems.at[1, k], to, seq)

    def scatter_done(mine, slices, sems):
        total = mine[dp]
        for k in range(1, dp_count):
            scatter(mine, slices, sems, k).wait()
            total = total + slices[k]
        return total

    def swap(pieces, sems, k):
        return remote(pieces.at[0], pieces.at[k], sems.at[0, dp_count + k - 1], sems.at[1, dp_count + k - 1], dp, peers[k - 1])

    def swap_done(pieces, sems):
        total = pieces[0]
        for k in range(1, 4):
            swap(pieces, sems, k).wait()
            total = total + pieces[k]
        return total

    @pl.when(step == 0)
    def _():
        sums[...] = jnp.zeros_like(sums)
        barrier = pltpu.get_barrier_semaphore()
        for k in range(1, dp_count):
            pl.semaphore_signal(barrier, inc=1, device_id=(lax.rem(dp + k, dp_count), seq), device_id_type=MESH)
        for peer in peers:
            pl.semaphore_signal(barrier, inc=1, device_id=(dp, peer), device_id_type=MESH)
        pl.semaphore_wait(barrier, dp_count + 2)
        columns_of = [jnp.sum(chain_sums[i], axis=0, keepdims=True) for i in range(LOSS)]
        objective = 0.5 * jnp.sum(chain_sums[LOSS]) + 0.5 * SCORE_WEIGHT * jnp.sum(distill[...])
        columns_of.append(jnp.full((1, width), objective, F32))
        columns_of.append(jnp.zeros((PAIR - len(columns_of), width), F32))
        mine_a[...] = jnp.transpose(jnp.concatenate(columns_of, axis=0)).reshape(mine_a.shape)
        for k in range(1, dp_count):
            scatter(mine_a, slices_a, a_sems, k).start()

    @pl.when(step == 2)
    def _():
        pieces[0] = scatter_done(mine_a, slices_a, a_sems)
        for k in range(1, 4):
            swap(pieces, a_sems, k).start()

    @pl.when(step == 4)
    def _():
        early[...] = swap_done(pieces, a_sems)

    def joined(kind, r, which, place):
        near_copy(r, kind, which).wait_recv()
        return (partial[kind, r, positions(place)].astype(F32) + near[kind, r, which].astype(F32)).astype(BF16)

    def hand_over(r):
        low = None
        for kind in range(2):
            both = jnp.concatenate([joined(kind, r, 1, across), joined(kind, r, 0, seq)], axis=0)
            part = dot_nn(both, weights[1 + kind])
            low = part if low is None else low + part
        sent[r] = low[:block].astype(BF16)
        far_copy(r).start()
        kept[r] = kept[r] + low[block:]
        sums[3] += folded(low[:block] * bounds_in[0, positions(across)].astype(F32))
        sums[3] += folded(low[block:] * bounds_in[0, positions(seq)].astype(F32))

    def settle(r):
        far_copy(r).wait_recv()
        grad_low = kept[r] + far[r].astype(F32)
        unused, slope, bound = clip_parts(hidden[0].astype(F32), table[C_IN : C_IN + 1])
        grad_input[0] = grad_first[...] + grad_low * slope

    @pl.when(step < rows)
    def _():
        attend_back_row(scale, table, s_query.at[0], s_key.at[0], s_value.at[0],
                        s_context.at[0], spread.at[0], probs.at[0], gaps.at[0],
                        grad_ctx, partial.at[0, step], partial.at[1, step], query_grads)
        for kind in range(2):
            near_copy(step, kind, 1).start()
        for kind in range(2):
            near_copy(step, kind, 0).start()
        back = query_grads[...]
        raw = table[A_Q : A_Q + 1] * s_query[0] + table[B_Q : B_Q + 1]
        sums[0] += folded(raw * back)
        query_grad = back * table[A_K : A_K + 1]
        sums[1] += folded(query_grad * s_query[0])
        sums[2] += folded(query_grad)
        kept[step] = dot_nn((query_grad * table[A_Q : A_Q + 1]).astype(BF16), weights[0])
        sums[3] += folded(kept[step] * own_bounds[0].astype(F32))

    @pl.when((step > 0) & (step <= rows))
    def _():
        hand_over(step - 1)

    @pl.when(step == rows)
    def _():
        columns_of = [jnp.sum(sums[i], axis=0, keepdims=True) for i in range(4)]
        columns_of.append(jnp.zeros((PAIR - len(columns_of), width), F32))
        turned = jnp.transpose(jnp.concatenate(columns_of, axis=0))
        for k in range(dp_count):
            part = jnp.transpose(turned[k * size : (k + 1) * size])[:8]
            mine_b[k] = jnp.concatenate([part, jnp.zeros((8, PAIR - size), F32)], axis=1)
        for k in range(1, dp_count):
            scatter(mine_b, slices_b, b_sems, k).start()

    @pl.when(step > 1)
    def _():
        settle(step - 2)

    @pl.when(step == rows)
    def _():
        pieces_b[0] = scatter_done(mine_b, slices_b, b_sems)
        for k in range(1, 4):
            swap(pieces_b, b_sems, k).start()

    @pl.when(step == pl.num_programs(0) - 1)
    def _():
        for r in range(rows):
            for kind in range(2):
                near_copy(r, kind, 0).wait_send()
                near_copy(r, kind, 1).wait_send()
            far_copy(r).wait_send()
        late[...] = swap_done(pieces_b, b_sems)


def finish_kernel(early, late, *refs):
    latents, grads, vectors = refs[:6], refs[6:12], refs[12:]
    size = early.shape[0]
    first, second = jnp.transpose(early[...]), late[...]
    turned = jnp.transpose(jnp.concatenate([second] * (PAIR // 8), axis=0))[:size]

    def row(value, i):
        return value[i : i + 1, :size]

    sums = [turned[:, 1:2], turned[:, 0:1], early[:, G_V : G_V + 1], early[:, G_O : G_O + 1], None, early[:, G_D : G_D + 1]]
    lane = lax.broadcasted_iota(jnp.int32, (4 * size, PAIR), 1)
    wide = jnp.zeros((4 * size, PAIR), F32)
    for m in range(3):
        column = jnp.concatenate([early[:, G_U + 4 * m + i : G_U + 4 * m + i + 1] for i in range(4)], axis=0)
        wide = jnp.where(lane == m, column, wide)
    wide = jnp.transpose(wide)
    sums[4] = wide[0:1]
    for i, (latent, grad, total) in enumerate(zip(latents, grads, sums)):
        grad[...] = signed(latent[...]) * (total / latent.shape[0 if i == 4 else 1])
    loss, given = vectors[-1], vectors[:-1]
    loss[...] = jnp.broadcast_to(row(first, LOSS), loss.shape)
    parts = [row(second, 2), row(first, G_BV), row(first, G_BO), wide[1:2], row(first, G_BD), row(first, G_G1),
             row(first, G_S1), row(first, G_G2), row(first, G_S2), row(second, 3), row(first, G_CCTX), row(first, G_CMID),
             wide[2:3]]
    for ref, part in zip(given, parts):
        ref[...] = part


def signs_and_scale(latent):
    scale = jnp.mean(jnp.abs(latent), axis=0).astype(BF16)
    return jnp.sign(latent).astype(BF16).T, scale


def body(
    hidden_in,
    segment_ids,
    row_lengths,
    teacher_scores,
    teacher_hidden,
    w_query,
    w_key,
    w_value,
    w_out,
    w_up,
    w_down,
    b_query,
    b_value,
    b_out,
    b_up,
    b_down,
    norm1_gain,
    norm1_bias,
    norm2_gain,
    norm2_bias,
    clip_in,
    clip_ctx,
    clip_mid,
    clip_hid,
):
    rows, block, width = hidden_in.shape
    heads = teacher_scores.shape[1]
    head_dim = width // heads
    seq_len = segment_ids.shape[1]
    tokens = rows * block
    scale = head_dim ** (-0.5)
    place = lax.axis_index("seq")
    first = place * block

    dp_count = lax.axis_size("dp")
    size = w_query.shape[1]
    tuned = dp_count == 8 and rows == 8 and size % 32 == 0 and lax.axis_size("seq") == 4
    given = jnp.stack([b_query, b_value, b_out, b_down, norm1_gain, norm1_bias, norm2_gain, norm2_bias, clip_in, clip_ctx, clip_mid])
    given_wide = jnp.stack([b_up, clip_hid])

    def row_spec(*shape):
        return pl.BlockSpec((1,) + shape, lambda i: (i,) + (0,) * len(shape))

    def whole(array):
        return pl.BlockSpec(array.shape, lambda i: (0,) * array.ndim, pipeline_mode=pl.Buffered(1))

    three = pl.BlockSpec((3, width, width), lambda i: (0, 0, 0), pipeline_mode=pl.Buffered(1))
    attend_specs = [row_spec(block, width), row_spec(seq_len, width), row_spec(seq_len, width), row_spec(block, width),
                    row_spec(block, width), row_spec(heads, block, seq_len), row_spec(heads, block, seq_len),
                    row_spec(seq_len, width), row_spec(block, width), pl.BlockSpec((8, seq_len), lambda i: (0, 0))]
    attend_shapes = [jax.ShapeDtypeStruct((rows, block, width), F32),
                     jax.ShapeDtypeStruct((rows, seq_len, width), BF16),
                     jax.ShapeDtypeStruct((rows, seq_len, width), BF16),
                     jax.ShapeDtypeStruct((rows, block, width), F32),
                     jax.ShapeDtypeStruct((rows, block, width), F32),
                     jax.ShapeDtypeStruct((rows, heads, block, seq_len), BF16),
                     jax.ShapeDtypeStruct((rows, heads, block, seq_len), BF16),
                     jax.ShapeDtypeStruct((rows, seq_len, width), BF16),
                     jax.ShapeDtypeStruct((rows, block, width), BF16),
                     jax.ShapeDtypeStruct((8, seq_len), F32)]
    teacher_spec = row_spec(heads, block, seq_len)
    scalars = pl.BlockSpec(memory_space=pltpu.SMEM)
    latents = (w_query.T, w_key.T, w_value.T, w_out.T, w_up, w_down.T)
    anywhere = pl.BlockSpec(memory_space=pl.ANY)
    lines = dp_count // 2
    sems = pltpu.SemaphoreType.DMA
    if tuned:
        full, table, s_query, s_key, s_value, s_context, spread, probs, gaps, bounds_in, own_bounds, distill = pl.pallas_call(
            functools.partial(first_kernel, scale, dp_count),
            grid=(rows,),
            in_specs=[scalars, whole(segment_ids)] + [whole(w) for w in latents] + [whole(given), whole(given_wide), anywhere,
                      row_spec(block, width), teacher_spec],
            out_specs=[anywhere, pl.BlockSpec((VECTORS, width), lambda i: (0, 0))] + attend_specs,
            out_shape=[jax.ShapeDtypeStruct((UNITS, width, width), BF16), jax.ShapeDtypeStruct((VECTORS, width), F32)]
            + attend_shapes,
            scratch_shapes=[
                pltpu.VMEM((UNITS, size, width), BF16), pltpu.VMEM((size, PAIR), F32), pltpu.VMEM((size, PAIR), BF16),
                pltpu.VMEM((rows, seq_len, width), BF16), pltpu.VMEM((width, PAIR), BF16), pltpu.VMEM((3, width, width), BF16),
                sems((2, UNITS, lines * lines)), sems((2, UNITS, lines)), sems((2, UNITS, dp_count)),
                sems((2, UNITS, dp_count)), sems((UNITS,)), sems((2, 3, rows)), sems((rows,)), sems((2, dp_count)), sems((3,)),
                pltpu.VMEM((block, seq_len), F32), pltpu.VMEM((block, seq_len), F32),
            ],
            compiler_params=pltpu.CompilerParams(collective_id=0, has_side_effects=True, vmem_limit_bytes=60 * 2**20),
        )(row_lengths, segment_ids, *latents, given, given_wide, hidden_in, hidden_in, teacher_scores)
    else:
        square = [signs_and_scale(w) for w in (w_query, w_key, w_value, w_out)]
        up_signs, up_scale = signs_and_scale(w_up)
        down = w_down.reshape(dp_count, 4, size, size)
        down_signs = jnp.sign(down).astype(BF16).transpose(1, 3, 0, 2).reshape(4, size, width)
        down_scale = jnp.mean(jnp.abs(w_down), axis=0).astype(BF16)
        pairs = jnp.stack([up_signs.reshape(4, size, width), down_signs], axis=1).reshape(8, size, width)
        own = jnp.concatenate([jnp.stack([s for s, _ in square]), pairs])
        own_vectors = jnp.concatenate(
            [jnp.stack([*(a for _, a in square), down_scale, b_query, b_value, b_out, b_down, norm1_gain, norm1_bias,
                        norm2_gain, norm2_bias, clip_in, clip_ctx, clip_mid]),
             up_scale.reshape(4, size), b_up.reshape(4, size), clip_hid.reshape(4, size)]
        )
        own_vectors = jnp.pad(own_vectors.T, ((0, 0), (0, PAIR - own_vectors.shape[0])))

        full = lax.all_gather(own, "dp", axis=1, tiled=True)
        table = lax.all_gather(own_vectors, "dp", axis=0, tiled=True).astype(F32).T[:VECTORS]
        hidden_full = lax.all_gather(hidden_in, "seq", axis=1, tiled=True)
        s_query, s_key, s_value, s_context, spread, probs, gaps, bounds_in, own_bounds, distill = pl.pallas_call(
            functools.partial(plain_kernel, scale),
            grid=(rows,),
            in_specs=[scalars, whole(segment_ids), row_spec(seq_len, width), row_spec(block, width), three, whole(table),
                      teacher_spec],
            out_specs=attend_specs,
            out_shape=attend_shapes,
            scratch_shapes=[pltpu.VMEM((block, seq_len), F32), pltpu.VMEM((block, seq_len), F32)],
            compiler_params=pltpu.CompilerParams(vmem_limit_bytes=60 * 2**20),
        )(row_lengths, segment_ids, hidden_full, hidden_in, full, table, teacher_scores)

    group = 2
    def group_spec(*shape):
        return pl.BlockSpec((group,) + shape, lambda i: (i,) + (0,) * len(shape))
    flat_spec = pl.BlockSpec((group * block, width), lambda i: (i, 0))
    def flat_spec(buffers):
        return pl.BlockSpec((group * block, width), lambda i: (i, 0), pipeline_mode=pl.Buffered(buffers))

    final, grad_first, grad_ctx, sums = pl.pallas_call(
        functools.partial(chain_kernel, group),
        grid=(rows // group,),
        in_specs=[scalars, pl.BlockSpec(memory_space=pl.ANY), whole(table), flat_spec(2), flat_spec(2), flat_spec(2)],
        out_specs=[flat_spec(2), flat_spec(2), flat_spec(2),
                   pl.BlockSpec((SUMS, 8, width), lambda i: (0, 0, 0))],
        out_shape=[jax.ShapeDtypeStruct((tokens, width), BF16),
                   jax.ShapeDtypeStruct((tokens, width), F32),
                   jax.ShapeDtypeStruct((tokens, width), F32),
                   jax.ShapeDtypeStruct((SUMS, 8, width), F32)],
        scratch_shapes=[pltpu.VMEM((UNITS - 3, width, width), BF16), pltpu.SemaphoreType.DMA((UNITS - 3,)),
                        pltpu.VMEM((SUMS, 8, width), F32)]
        + [pltpu.VMEM((4, group * block, width), F32)] * 3,
        compiler_params=pltpu.CompilerParams(vmem_limit_bytes=63 * 2**20),
    )(row_lengths, full, table, hidden_in.reshape(tokens, width), teacher_hidden.reshape(tokens, width),
      s_context.reshape(tokens, width))
    if tuned:
        def now_spec(*shape):
            return pl.BlockSpec((1,) + shape, lambda i: (jnp.minimum(i, rows - 1),) + (0,) * len(shape))

        def then_spec(*shape):
            return pl.BlockSpec((1,) + shape, lambda i: (jnp.maximum(i - 2, 0),) + (0,) * len(shape))

        own_spec = now_spec(block, width)
        grad_input, early, late = pl.pallas_call(
            functools.partial(last_kernel, scale, dp_count),
            grid=(rows + 2,),
            in_specs=[three, whole(table), now_spec(block, width), now_spec(seq_len, width), now_spec(seq_len, width),
                      now_spec(block, width), now_spec(block, width), now_spec(heads, block, seq_len),
                      now_spec(heads, block, seq_len), pl.BlockSpec((block, width), lambda i: (jnp.minimum(i, rows - 1), 0)),
                      then_spec(block, width), pl.BlockSpec((block, width), lambda i: (jnp.maximum(i - 2, 0), 0)),
                      pl.BlockSpec((1, seq_len, width), lambda i: (jnp.clip(i - 1, 0, rows - 1), 0, 0)),
                      own_spec, whole(sums), whole(distill)],
            out_specs=[then_spec(block, width), pl.BlockSpec((size, PAIR), lambda i: (0, 0)), pl.BlockSpec((8, PAIR), lambda i: (0, 0))],
            out_shape=[jax.ShapeDtypeStruct((rows, block, width), F32), jax.ShapeDtypeStruct((size, PAIR), F32),
                       jax.ShapeDtypeStruct((8, PAIR), F32)],
            scratch_shapes=[
                pltpu.VMEM((block, width), F32),
                pltpu.VMEM((2, rows, seq_len, width), BF16), pltpu.VMEM((rows, block, width), F32),
                pltpu.VMEM((2, rows, 2, block, width), BF16), pltpu.VMEM((rows, block, width), BF16),
                pltpu.VMEM((rows, block, width), BF16), pltpu.VMEM((4, 8, width), F32),
                pltpu.VMEM((dp_count, size, PAIR), F32), pltpu.VMEM((dp_count, size, PAIR), F32),
                pltpu.VMEM((dp_count, 8, PAIR), F32), pltpu.VMEM((dp_count, 8, PAIR), F32),
                pltpu.VMEM((4, size, PAIR), F32), pltpu.VMEM((4, 8, PAIR), F32),
                sems((2, 2, rows, 2)), sems((2, rows)), sems((2, dp_count + 3)), sems((2, dp_count + 3)),
            ],
            compiler_params=pltpu.CompilerParams(collective_id=1, has_side_effects=True, vmem_limit_bytes=60 * 2**20),
        )(full, table, s_query, s_key, s_value, s_context, spread, probs, gaps, grad_ctx, hidden_in, grad_first, bounds_in, own_bounds, sums, distill)
        def one_block(shape):
            return pl.BlockSpec(shape, lambda: (0,) * len(shape))

        small_shapes = [(1, w.shape[0]) for w in (b_query, b_value, b_out, b_up, b_down, norm1_gain, norm1_bias, norm2_gain,
                                                  norm2_bias, clip_in, clip_ctx, clip_mid, clip_hid)]
        results = pl.pallas_call(
            finish_kernel,
            in_specs=[one_block(early.shape), one_block(late.shape)] + [one_block(w.shape) for w in latents],
            out_specs=[one_block(w.shape) for w in latents] + [one_block(shape) for shape in small_shapes] + [one_block((1, size))],
            out_shape=[jax.ShapeDtypeStruct(w.shape, F32) for w in latents]
            + [jax.ShapeDtypeStruct(shape, F32) for shape in small_shapes]
            + [jax.ShapeDtypeStruct((1, size), F32)],
            compiler_params=pltpu.CompilerParams(vmem_limit_bytes=60 * 2**20),
        )(early, late, *latents)
        loss = results[-1][0, 0] / (dp_count * rows * seq_len)
        return (
            (final.reshape(rows, block, width), loss, grad_input.reshape(rows, block, width))
            + tuple(grad if i == 4 else grad.T for i, grad in enumerate(results[:6]))
            + tuple(part.reshape(-1) for part in results[6:-1])
        )
    else:
        one_spec = pl.BlockSpec((block, width), lambda i: (i, 0))
        pulled_in, own_in, more = pl.pallas_call(
            functools.partial(back_kernel, scale),
            grid=(rows,),
            in_specs=[three, whole(table),
                      row_spec(block, width), row_spec(seq_len, width), row_spec(seq_len, width), row_spec(block, width),
                      row_spec(block, width), row_spec(heads, block, seq_len), row_spec(heads, block, seq_len), one_spec],
            out_specs=[row_spec(seq_len, width), one_spec, pl.BlockSpec((3, 8, width), lambda i: (0, 0, 0))],
            out_shape=[jax.ShapeDtypeStruct((rows, seq_len, width), BF16),
                       jax.ShapeDtypeStruct((tokens, width), F32),
                       jax.ShapeDtypeStruct((3, 8, width), F32)],
            scratch_shapes=[pltpu.VMEM((seq_len, width), BF16), pltpu.VMEM((seq_len, width), BF16),
                            pltpu.VMEM((block, width), F32)],
            compiler_params=pltpu.CompilerParams(vmem_limit_bytes=60 * 2**20),
        )(full, table, s_query, s_key, s_value, s_context, spread, probs, gaps, grad_ctx)
        sums = sums.at[G_K].set(more[0]).at[G_Q].set(more[1]).at[G_BQ].set(more[2])
        objective = 0.5 * jnp.sum(sums[LOSS]) + 0.5 * SCORE_WEIGHT * jnp.sum(distill)

        crossed = lax.psum_scatter(pulled_in, "seq", scatter_dimension=1, tiled=True).astype(F32)
        grad_low = own_in + crossed.reshape(tokens, width)
        inputs = hidden_in.astype(F32).reshape(tokens, width)
        unused, in_slope, in_bound = clip_parts(inputs, table[C_IN : C_IN + 1])
        grad_input = grad_first + grad_low * in_slope
        sums = jnp.sum(sums, axis=1)
        wide_sums = sums[16:28]
        sums = sums[:16].at[G_CIN].set(columns(grad_low * in_bound)[0])
        sums, wide_sums, objective = lax.psum((sums, wide_sums, objective), ("dp", "seq"))
        at = lax.axis_index("dp")
        sums = lax.dynamic_slice_in_dim(sums, at * size, size, 1)
        wide_sums = lax.dynamic_slice_in_dim(wide_sums, at * size, size, 1).reshape(3, 4 * size)
    loss = objective / (lax.axis_size("dp") * rows * seq_len)
    grads = [
        jnp.sign(w) * (s / w.shape[0])
        for w, s in zip(
            (w_query, w_key, w_value, w_out, w_up, w_down),
            (sums[0], sums[1], sums[2], sums[3], wide_sums[0], sums[4]),
        )
    ]
    return (
        final.reshape(rows, block, width).astype(BF16),
        loss,
        grad_input.reshape(rows, block, width),
        *grads,
        sums[5],
        sums[6],
        sums[7],
        wide_sums[1],
        sums[8],
        sums[9],
        sums[10],
        sums[11],
        sums[12],
        sums[13],
        sums[14],
        sums[15],
        wide_sums[2],
    )


def solution(mesh):
    rows = P("dp", "seq", None)
    cols = P(None, "dp")
    vec = P("dp")
    return jax.shard_map(
        body,
        mesh=mesh,
        in_specs=(rows, P("dp", None), vec, P("dp", None, "seq", None), rows)
        + (cols,) * 6
        + (vec,) * 13,
        out_specs=(rows, P(), rows) + (cols,) * 6 + (vec,) * 13,
        check_vma=False,
    )
```

```python
import functools

import jax
import jax.numpy as jnp
from jax import lax
from jax.experimental import pallas as pl
from jax.experimental.pallas import tpu as pltpu
from jax.sharding import PartitionSpec as P

EPS = 1e-05
SCORE_WEIGHT = 0.0625
NEGATIVE = -1e30
F32 = jnp.float32
BF16 = jnp.bfloat16
PAIR = 128
HEAD = 64
GROUP = 256
A_Q, A_K, A_V, A_O, A_D, B_Q, B_V, B_O, B_D, G1, S1, G2, S2, C_IN, C_CTX, C_MID = range(16)
A_U, B_U, C_HID, VECTORS = 16, 20, 24, 32
G_Q, G_K, G_V, G_O, G_D, G_BQ, G_BV, G_BO, G_BD, G_G1, G_S1, G_G2, G_S2, G_CIN, G_CCTX, G_CMID = range(16)
G_U, G_BU, G_CHID, LOSS, SUMS = 16, 20, 24, 28, 29


def dot_nt(left, right):
    return lax.dot_general(left, right, (((1,), (1,)), ((), ())), preferred_element_type=F32)


def dot_nn(left, right):
    return lax.dot_general(left, right, (((1,), (0,)), ((), ())), preferred_element_type=F32)


def dot_tn(left, right):
    return lax.dot_general(left, right, (((0,), (0,)), ((), ())), preferred_element_type=F32)


def columns(value):
    return jnp.sum(value, axis=0, keepdims=True)


def clip_parts(value, bound):
    ratio = value / bound
    bent = jnp.tanh(ratio)
    slope = 1.0 - bent * bent
    return bound * bent, slope, bent - ratio * slope


def norm_parts(value, gain, shift):
    centre = value - jnp.mean(value, axis=-1, keepdims=True)
    inverse = lax.rsqrt(jnp.mean(centre * centre, axis=-1, keepdims=True) + EPS)
    unit = centre * inverse
    return unit * gain + shift, unit, inverse


def norm_back(grad, unit, inverse, gain):
    scaled = grad * gain
    return inverse * (
        scaled
        - jnp.mean(scaled, axis=-1, keepdims=True)
        - unit * jnp.mean(scaled * unit, axis=-1, keepdims=True)
    )


def stacked(value):
    lane = lax.broadcasted_iota(jnp.int32, value.shape, 1)
    zero = jnp.zeros_like(value)
    return jnp.concatenate([jnp.where(lane // HEAD == i, value, zero) for i in range(GROUP // HEAD)], axis=0)


def by_head(parts):
    shape = jnp.broadcast_shapes(parts[0].shape, (1, GROUP))
    lane = lax.broadcasted_iota(jnp.int32, shape, 1)
    result = parts[-1]
    for i in range(len(parts) - 2, -1, -1):
        result = jnp.where(lane < (i + 1) * HEAD, parts[i], result)
    return result


def folded(value):
    return jnp.sum(value.reshape(value.shape[0] // 8, 8, value.shape[1]), axis=0)


def mask_row(segments, lengths, row, start, bias, counted):
    block, seq_len = bias.shape
    keys = segments[pl.ds(row, 1), :].astype(F32)
    mine = keys[:, :block]
    for i in range(1, seq_len // block):
        mine = jnp.where(start == i * block, keys[:, i * block : (i + 1) * block], mine)
    queries = jnp.transpose(jnp.broadcast_to(mine, (block, block)))
    same = jnp.concatenate([queries] * (seq_len // block), axis=1) == keys
    length = lengths[row]
    query_at = start + lax.broadcasted_iota(jnp.int32, (block, seq_len), 0)
    key_at = lax.broadcasted_iota(jnp.int32, (block, seq_len), 1)
    bias[...] = jnp.where(same, 0.0, NEGATIVE)
    counted[...] = jnp.where(same & (query_at < length) & (key_at < length), 1.0, 0.0)


def signed(value):
    return jnp.where(value > 0, 1.0, jnp.where(value < 0, -1.0, 0.0))


def pack(squares, up, down, vectors_in, own, own_vectors, which):
    size = own.shape[1]
    width = own.shape[2]
    lane = lax.broadcasted_iota(jnp.int32, own_vectors.shape, 1)

    def put(unit, turned, kind):
        own[unit] = signed(turned).astype(BF16)
        scale = jnp.sum(jnp.abs(turned), axis=1, keepdims=True) / width
        own_vectors[...] = jnp.where(lane == kind, scale.astype(BF16).astype(F32), own_vectors[...])

    if which == 0:
        size = own.shape[1]
        zeros = functools.partial(jnp.zeros, dtype=F32)
        columns = jnp.transpose(
            jnp.concatenate([zeros((5, size)), vectors_in[0][...].astype(F32), zeros((PAIR - 16, size))], axis=0)
        )
        wide = jnp.transpose(
            jnp.concatenate([vectors_in[1][...].astype(F32), zeros((PAIR - 2, 4 * size))], axis=0)
        )
        for kind in range(2):
            for i in range(4):
                columns = jnp.where(lane == B_U + 4 * kind + i, wide[i * size : (i + 1) * size, kind : kind + 1], columns)
        own_vectors[...] = columns
        for unit in range(3):
            put(unit, squares[unit][...], A_Q + unit)
        return
    put(3, squares[3][...], A_O)
    turned = jnp.transpose(up[...])
    for i in range(4):
        part = turned[i * size : (i + 1) * size]
        own[4 + 2 * i] = signed(part).astype(BF16)
        scale = jnp.sum(jnp.abs(part), axis=1, keepdims=True) / width
        own_vectors[...] = jnp.where(lane == A_U + i, scale.astype(BF16).astype(F32), own_vectors[...])
    groups = down.shape[1] // (4 * size)
    scale = jnp.sum(jnp.abs(down[...]), axis=1, keepdims=True) / down.shape[1]
    own_vectors[...] = jnp.where(lane == A_D, scale.astype(BF16).astype(F32), own_vectors[...])
    straight = jnp.transpose(signed(down[...]))
    for i in range(4):
        part = jnp.concatenate([straight[(4 * j + i) * size : (4 * j + i + 1) * size] for j in range(groups)], axis=0)
        own[5 + 2 * i] = jnp.transpose(part).astype(BF16)


def project_row(hidden, own_hidden, sq, sk, sv, small, s_query, s_key, s_value, bounds_in, own_bounds):
    c_in = small[C_IN : C_IN + 1]
    inverse_in = 1.0 / c_in
    ratio = hidden[...].astype(F32) * inverse_in
    bent = jnp.tanh(ratio)
    bounds_in[...] = (bent - ratio * (1.0 - bent * bent)).astype(BF16)
    low = (c_in * bent).astype(BF16)
    s_key[...] = dot_nt(low, sk[...]).astype(BF16)
    s_value[...] = dot_nt(low, sv[...]).astype(BF16)
    ratio = own_hidden[...].astype(F32) * inverse_in
    bent = jnp.tanh(ratio)
    own_bounds[...] = (bent - ratio * (1.0 - bent * bent)).astype(BF16)
    low = (c_in * bent).astype(BF16)
    s_query[...] = dot_nt(low, sq[...])


def attend_row(
    scale, small, teacher, s_query, s_key, s_value, s_context, spread, probs, gaps, distill, bias, counted,
    first, last,
):
    block, width = s_query.shape

    def some(index, carry):
        at = pl.ds(pl.multiple_of(index * GROUP, GROUP), GROUP)
        query = (
            (small[A_Q : A_Q + 1, at] * s_query[:, at] + small[B_Q : B_Q + 1, at])
            * (small[A_K : A_K + 1, at] * scale)
        ).astype(BF16)
        scores = dot_nt(stacked(query), s_key[:, at])
        expos, inverses = [], []
        sums = jnp.zeros((8, scores.shape[1]), F32)
        for head in range(GROUP // HEAD):
            mine = scores[head * block : (head + 1) * block]
            gap = (mine - teacher[GROUP // HEAD * index + head].astype(F32)) * counted[...]
            sums = sums + folded(gap * gap)
            gaps[GROUP // HEAD * index + head] = (gap * SCORE_WEIGHT).astype(BF16)
            masked = mine + bias[...]
            expo = jnp.exp(masked - jnp.max(masked, axis=-1, keepdims=True))
            inverses.append(1.0 / jnp.sum(expo, axis=-1, keepdims=True))
            expo = expo.astype(BF16)
            probs[GROUP // HEAD * index + head] = expo
            expos.append(expo)
        distill[...] += sums
        both = dot_nn(jnp.concatenate(expos, axis=0), s_value[:, at])
        inverse = by_head(inverses)
        s_context[:, at] = by_head([both[h * block : (h + 1) * block] for h in range(GROUP // HEAD)]) * inverse
        spread[:, at] = inverse
        return carry

    lax.fori_loop(first, last, some, 0)


MESH = pl.DeviceIdType.MESH
UNITS = 12
STEPS = 10
SHARED = (6, 7)

def remote(source, target, send, recv, dp, seq):
    return pltpu.make_async_remote_copy(
        src_ref=source, dst_ref=target, send_sem=send, recv_sem=recv, device_id=(dp, seq), device_id_type=MESH
    )

class Streams:
    def __init__(self, lines, own, full, s_sems, z_sems, x_sems, y_sems, c_sems, l_sems):
        self.lines, self.own, self.full = lines, own, full
        self.s_sems, self.z_sems, self.x_sems, self.y_sems, self.c_sems, self.l_sems = s_sems, z_sems, x_sems, y_sems, c_sems, l_sems
        self.dp, self.seq = lax.axis_index("dp"), lax.axis_index("seq")
        self.zi, self.xi = self.dp // 2, self.dp % 2
        self.yi, self.ci = self.seq // 2, self.seq % 2
        self.size = own.shape[1]
        self.half = self.size // 2

    def unit(self, t, partner=False):
        if t in SHARED:
            return SHARED[0] + 2 * (t - SHARED[0]) + (1 - self.yi if partner else self.yi)
        return t if t < SHARED[0] else t + 2

    def piece(self, u, dp):
        start = pl.multiple_of(dp * self.size + self.ci * self.half, self.half)
        return self.full.at[u, pl.ds(start, self.half)]

    def own_piece(self, u):
        return self.own.at[u, pl.ds(pl.multiple_of(self.ci * self.half, self.half), self.half)]

    def z_copy(self, u, src, to):
        place = self.piece(u, src * 2 + self.xi)
        return remote(self.own_piece(u) if src is self.zi else place, place,
                      self.s_sems.at[0, u], self.z_sems.at[u, src], to * 2 + self.xi, self.seq)

    def x_copy(self, u, src):
        place = self.piece(u, src * 2 + self.xi)
        return remote(self.own_piece(u) if src is self.zi else place, place, self.s_sems.at[1, u], self.x_sems.at[u, src],
                      self.zi * 2 + 1 - self.xi, self.seq)

    def x_arrival(self, u, src):
        place = self.piece(u, src * 2 + 1 - self.xi)
        return remote(place, place, self.s_sems.at[1, u], self.x_sems.at[u, src], self.zi * 2 + 1 - self.xi, self.seq)

    def y_copy(self, u, dp):
        place = self.piece(u, dp)
        return remote(place, place, self.y_sems.at[0, u - SHARED[0]], self.y_sems.at[1, u - SHARED[0]], self.dp, (1 - self.yi) * 2 + self.ci)

    def c_copy(self, u, dp):
        place = self.piece(u, dp)
        return remote(place, place, self.c_sems.at[0, u], self.c_sems.at[1, u], self.dp, self.yi * 2 + 1 - self.ci)

    def local_copy(self, u):
        start = pl.multiple_of(self.dp * self.size, self.size)
        return pltpu.make_async_copy(self.own.at[u], self.full.at[u, pl.ds(start, self.size)], self.l_sems.at[u])

    def each_row(self, run):
        for k in range(1, self.lines):
            pl.when(self.zi >= k)(functools.partial(run, self.zi - k, True))
            pl.when(self.zi + k < self.lines)(functools.partial(run, self.zi + k, False))

    def neighbours(self, run):
        pl.when(self.zi > 0)(lambda: run(self.zi - 1))
        pl.when(self.zi < self.lines - 1)(lambda: run(self.zi + 1))

    def relay(self, src, below, run):
        if below:
            pl.when(self.zi < self.lines - 1)(lambda: run(self.zi + 1))
        else:
            pl.when(self.zi > 0)(lambda: run(self.zi - 1))

    def launch(self, t):
        u = self.unit(t)
        self.x_copy(u, self.zi).start()
        self.neighbours(lambda to: self.z_copy(u, self.zi, to).start())

    def at_distance(self, k, run):
        if k == 0:
            run(self.zi, None)
        else:
            pl.when(self.zi >= k)(functools.partial(run, self.zi - k, True))
            pl.when(self.zi + k < self.lines)(functools.partial(run, self.zi + k, False))

    def along_z(self, t, k):
        u = self.unit(t)
        def run(src, below):
            self.z_copy(u, src, self.zi).wait_recv()
            self.relay(src, below, lambda to: self.z_copy(u, src, to).start())
            self.x_copy(u, src).start()
            self.spread(t, u, src * 2 + self.xi)
        self.at_distance(k, run)

    def over_x(self, t, k):
        u = self.unit(t)
        def run(src, below):
            self.x_arrival(u, src).wait_recv()
            self.spread(t, u, src * 2 + 1 - self.xi)
        self.at_distance(k, run)

    def spread(self, t, u, dp):
        if t in SHARED:
            self.y_copy(u, dp).start()
        self.c_copy(u, dp).start()

    def others(self, run):
        self.each_row(lambda src, below: run(src * 2 + self.xi))
        run(self.zi * 2 + 1 - self.xi)
        self.each_row(lambda src, below: run(src * 2 + 1 - self.xi))

    def over_y(self, t):
        u = self.unit(t, True)
        self.bulk(u, 2 * self.lines - 1, self.y_sems.at[1, u - SHARED[0]])
        self.others(lambda dp: self.c_copy(u, dp).start())

    def arrived(self, u):
        self.bulk(u, 2 * self.lines - 1, self.c_sems.at[1, u])
        self.local_copy(u).wait()

    def bulk(self, u, pieces, sem):
        part = self.full.at[u, pl.ds(0, pieces * self.half)]
        pltpu.make_async_copy(part, part, sem).wait()

    def finish(self):
        inner = (self.zi > 0) & (self.zi < self.lines - 1)
        for t in range(STEPS):
            u = self.unit(t)
            pl.when(inner)(functools.partial(self.bulk, u, self.lines + 1, self.s_sems.at[0, u]))
            pl.when(jnp.logical_not(inner))(functools.partial(self.bulk, u, 1, self.s_sems.at[0, u]))
            self.bulk(u, self.lines, self.s_sems.at[1, u])
            if t in SHARED:
                self.bulk(u, 2 * self.lines - 1, self.y_sems.at[0, u - SHARED[0]])
        for u in range(UNITS):
            self.bulk(u, 2 * self.lines - 1, self.c_sems.at[0, u])


def greet(dp_count):
    dp, seq = lax.axis_index("dp"), lax.axis_index("seq")
    barrier = pltpu.get_barrier_semaphore()
    for k in range(1, dp_count):
        pl.semaphore_signal(barrier, inc=1, device_id=(lax.rem(dp + k, dp_count), seq), device_id_type=MESH)
    pl.semaphore_signal(barrier, inc=1, device_id=(dp, seq // 2 * 2 + 1 - seq % 2), device_id_type=MESH)
    pl.semaphore_signal(barrier, inc=1, device_id=(dp, (1 - seq // 2) * 2 + seq % 2), device_id_type=MESH)
    pl.semaphore_wait(barrier, dp_count + 1)

NEAR = 3


def first_kernel(
    scale, dp_count, lengths, segments, w_query, w_key, w_value, w_out, w_up, w_down, vectors_in, wide_in,
    hidden, own_hidden, teacher,
    full, table, s_query, s_key, s_value, s_context, spread, probs, gaps, bounds_in, own_bounds, distill,
    own, own_columns, own_vectors, whole, vectors, weights, s_sems, z_sems, x_sems, y_sems, c_sems, l_sems, h_sems, o_sems, v_sems, w_sems, bias, counted,
):
    step = pl.program_id(0)
    rows, block = hidden.shape[0], hidden.shape[1]
    s = Streams(dp_count // 2, own, full, s_sems, z_sems, x_sems, y_sems, c_sems, l_sems)
    across, beside = (1 - s.yi) * 2 + s.ci, s.yi * 2 + 1 - s.ci

    def place(r, seq):
        return whole.at[r, pl.ds(pl.multiple_of(seq * block, block), block)]

    def to_chip(r):
        return remote(hidden.at[r], place(r, s.seq), h_sems.at[0, 0, r], h_sems.at[1, 0, r], s.dp, across)

    def to_core(r):
        return remote(hidden.at[r], place(r, s.seq), h_sems.at[0, 1, r], h_sems.at[1, 1, r], s.dp, beside)

    def passed_on(r):
        return remote(place(r, across), place(r, across), h_sems.at[0, 2, r], h_sems.at[1, 2, r], s.dp, beside)

    def kept(r):
        return pltpu.make_async_copy(hidden.at[r], place(r, s.seq), o_sems.at[r])

    def hidden_pump(r):
        to_chip(r).wait_recv()
        passed_on(r).start()
        if r + NEAR < rows:
            to_chip(r + NEAR).start()

    def vector_copy(k):
        mine = vectors.at[pl.ds(pl.multiple_of(s.dp * s.size, s.size), s.size)]
        return remote(own_vectors, mine, v_sems.at[0, k], v_sems.at[1, k], lax.rem(s.dp + k, dp_count), s.seq)

    def fetch(u):
        return pltpu.make_async_copy(full.at[u], weights.at[u], w_sems.at[u])

    def point(r, j):
        if j == 0 and r + 3 < rows:
            hidden_pump(r + 3)
        for t in range(3, STEPS):
            at = 4 * r + j - 3 * (t - 3)
            if at == 0 and t + 2 < STEPS:
                s.launch(t + 2)
            if at in (0, 3, 6):
                s.along_z(t, at // 3 + 1)
            if at in (1, 4, 7, 10):
                s.over_x(t, at // 3)
            if t in SHARED and at == 13:
                s.over_y(t)

    def points(j):
        for r in range(rows):
            pl.when(step == r)(functools.partial(point, r, j))

    @pl.when(step == 0)
    def _():
        distill[...] = jnp.zeros_like(distill)
        latents = (w_query, w_key, w_value, w_out), w_up, w_down
        pack(*latents, (vectors_in, wide_in), own, own_columns, 0)
        greet(dp_count)
        for r in range(NEAR):
            to_chip(r).start()
        for t in range(3):
            s.launch(t)
        pack(*latents, (vectors_in, wide_in), own, own_columns, 1)
        own_vectors[...] = own_columns[...].astype(BF16)
        for k in range(1, dp_count):
            vector_copy(k).start()
        for u in range(UNITS):
            s.local_copy(u).start()
        for r in range(rows):
            to_core(r).start()
            kept(r).start()
        mine = pl.ds(pl.multiple_of(s.dp * s.size, s.size), s.size)
        vectors[mine] = own_vectors[...]
        for k in range(1, s.lines):
            for t in range(3):
                s.along_z(t, k)
                s.over_x(t, k - 1)
            hidden_pump(k - 1)
        s.launch(3)
        for t in range(3):
            s.over_x(t, s.lines - 1)
        s.launch(4)
        for k in range(1, dp_count):
            vector_copy(k).wait()
        table[...] = jnp.transpose(vectors[...].astype(F32))[: table.shape[0]]
        for u in range(3):
            s.arrived(u)
            fetch(u).start()
        for u in range(3):
            fetch(u).wait()

    points(0)
    for r in range(rows):
        @pl.when(step == r)
        def _(r=r):
            kept(r).wait()
            to_core(r).wait_recv()
            passed_on(r).wait_recv()

    project_row(whole.at[step], own_hidden.at[0], weights.at[0], weights.at[1], weights.at[2], table,
                s_query.at[0], s_key.at[0], s_value.at[0], bounds_in.at[0], own_bounds.at[0])
    mask_row(segments, lengths, step, s.seq * block, bias, counted)
    count = s_query.shape[2] // GROUP
    for j in range(3):
        points(j + 1)
        attend_row(scale, table, teacher.at[0], s_query.at[0], s_key.at[0], s_value.at[0],
                   s_context.at[0], spread.at[0], probs.at[0], gaps.at[0], distill, bias, counted,
                   count * j // 3, count * (j + 1) // 3)

    @pl.when(step == rows - 1)
    def _():
        for u in range(3, UNITS):
            s.arrived(u)
        s.finish()
        for r in range(rows):
            to_chip(r).wait_send()
            to_core(r).wait_send()
            passed_on(r).wait_send()


def plain_kernel(
    scale, lengths, segments, whole, own_hidden, weights, table, teacher,
    s_query, s_key, s_value, s_context, spread, probs, gaps, bounds_in, own_bounds, distill, bias, counted,
):
    @pl.when(pl.program_id(0) == 0)
    def _():
        distill[...] = jnp.zeros_like(distill)

    project_row(whole.at[0], own_hidden.at[0], weights.at[0], weights.at[1], weights.at[2], table,
                s_query.at[0], s_key.at[0], s_value.at[0], bounds_in.at[0], own_bounds.at[0])
    mask_row(segments, lengths, pl.program_id(0), lax.axis_index("seq") * own_hidden.shape[1], bias, counted)
    attend_row(scale, table, teacher.at[0], s_query.at[0], s_key.at[0], s_value.at[0],
               s_context.at[0], spread.at[0], probs.at[0], gaps.at[0], distill, bias, counted, 0, s_query.shape[2] // GROUP)


def chain(stored, weights, arrivals, small, hidden, teacher, live, s_context, sums, final_out, grad_first_out,
          grad_ctx_out, pres, slopes, bounds):
    def vec(i):
        return small[i : i + 1]

    step = pl.program_id(0)

    def fetch(unit):
        return pltpu.make_async_copy(stored.at[3 + unit], weights.at[unit], arrivals.at[unit])

    def needed(unit):
        pass

    @pl.when(step == 0)
    def _():
        for unit in range(UNITS - 3):
            fetch(unit).start()
        for unit in range(UNITS - 3):
            fetch(unit).wait()

    def add(i, value):
        sums[i] += folded(value)

    width = hidden.shape[1]
    inputs = hidden[...].astype(F32)
    context = vec(A_V) * s_context[...] + vec(B_V)
    context_low = clip_parts(context, vec(C_CTX))[0]
    needed(0)
    s_out = dot_nt(context_low.astype(BF16), weights[0])
    normed, unit1, inverse1 = norm_parts(inputs + vec(A_O) * s_out + vec(B_O), vec(G1), vec(S1))
    normed_low, mid_slope, mid_bound = clip_parts(normed, vec(C_MID))
    normed_low = normed_low.astype(BF16)
    s_down = 0.0
    for i in range(4):
        needed(1 + 2 * i)
        s_up = dot_nt(normed_low, weights[1 + 2 * i])
        pres[i] = s_up
        pre = vec(A_U + i) * s_up + vec(B_U + i)
        phi = 0.5 + 0.5 * lax.erf(pre * (0.5**0.5))
        act_slope = phi + pre * (jnp.exp(-0.5 * pre * pre) * 0.3989422804014327)
        hidden_low, slope, bound = clip_parts(pre * phi, vec(C_HID + i))
        slopes[i] = (slope * act_slope)
        bounds[i] = bound
        needed(2 + 2 * i)
        s_down = s_down + dot_nt(hidden_low.astype(BF16), weights[2 + 2 * i])
    final, unit2, inverse2 = norm_parts(normed + vec(A_D) * s_down + vec(B_D), vec(G2), vec(S2))
    final_out[...] = final.astype(BF16)
    errors = jnp.where(live, final - teacher[...].astype(F32), 0.0)
    add(LOSS, errors * errors)
    add(G_G2, errors * unit2)
    add(G_S2, errors)
    grad_second = norm_back(errors, unit2, inverse2, vec(G2))
    add(G_D, grad_second * s_down)
    add(G_BD, grad_second)
    branch = (grad_second * vec(A_D)).astype(BF16)
    grad_mid = 0.0
    for i in range(4):
        grad_hid = dot_nn(branch, weights[2 + 2 * i])
        add(G_CHID + i, grad_hid * bounds[i])
        up_grad = grad_hid * slopes[i]
        add(G_BU + i, up_grad)
        add(G_U + i, up_grad * pres[i])
        grad_mid = grad_mid + dot_nn((up_grad * vec(A_U + i)).astype(BF16), weights[1 + 2 * i])
    add(G_CMID, grad_mid * mid_bound)
    grad_normed = grad_second + grad_mid * mid_slope
    add(G_G1, grad_normed * unit1)
    add(G_S1, grad_normed)
    grad_first = norm_back(grad_normed, unit1, inverse1, vec(G1))
    grad_first_out[...] = grad_first
    add(G_O, grad_first * s_out)
    add(G_BO, grad_first)
    grad_ctx_low = dot_nn((grad_first * vec(A_O)).astype(BF16), weights[0])
    unused, ctx_slope, ctx_bound = clip_parts(vec(A_V) * s_context[...] + vec(B_V), vec(C_CTX))
    add(G_CCTX, grad_ctx_low * ctx_bound)
    grad_ctx = grad_ctx_low * ctx_slope
    add(G_V, grad_ctx * s_context[...])
    add(G_BV, grad_ctx)
    grad_ctx_out[...] = grad_ctx


def attend_back_row(scale, small, s_query, s_key, s_value, s_context, spread, probs, gaps,
                    grad_ctx, key_grads, value_grads, query_grads):
    block, width = s_query.shape

    def some(index, carry):
        at = pl.ds(pl.multiple_of(index * GROUP, GROUP), GROUP)
        raw = small[A_Q : A_Q + 1, at] * s_query[:, at] + small[B_Q : B_Q + 1, at]
        query = stacked((raw * (small[A_K : A_K + 1, at] * scale)).astype(BF16))
        pulled = grad_ctx[:, at] * small[A_V : A_V + 1, at] * spread[:, at]
        product = pulled * s_context[:, at]
        lane = lax.broadcasted_iota(jnp.int32, product.shape, 1)
        deltas = [
            jnp.sum(jnp.where(lane // HEAD == h, product, 0.0), axis=-1, keepdims=True) for h in range(GROUP // HEAD)
        ]
        accum_grad = stacked(pulled.astype(BF16))
        prob_grad = dot_nt(accum_grad, s_value[:, at])
        score_grads, expos = [], []
        for head, delta in enumerate(deltas):
            expo = probs[GROUP // HEAD * index + head]
            expos.append(expo)
            mine = prob_grad[head * block : (head + 1) * block]
            score_grads.append(
                (expo.astype(F32) * (mine - delta) + gaps[GROUP // HEAD * index + head].astype(F32)).astype(BF16)
            )
        score_grad = jnp.concatenate(score_grads, axis=0)
        both = dot_nn(score_grad, s_key[:, at])
        query_grads[:, at] = (
            by_head([both[h * block : (h + 1) * block] for h in range(GROUP // HEAD)]) * scale
        )
        key_grads[:, at] = dot_tn(score_grad, query).astype(BF16)
        value_grads[:, at] = dot_tn(jnp.concatenate(expos, axis=0), accum_grad).astype(BF16)
        return carry

    lax.fori_loop(0, width // GROUP, some, 0, unroll=width // GROUP)


def chain_kernel(row_count, lengths, stored, small, hidden, teacher, s_context, final, grad_first, grad_ctx, sums_out,
                 weights, arrivals, sums, pres, slopes, bounds):
    step = pl.program_id(0)

    @pl.when(step == 0)
    def _():
        sums[...] = jnp.zeros_like(sums)

    flat = hidden.shape
    rows, block = row_count, flat[0] // row_count
    at = lax.broadcasted_iota(jnp.int32, flat, 0)
    limit = jnp.full(flat, lengths[step * rows], jnp.int32)
    for r in range(1, rows):
        limit = jnp.where(at < r * block, limit, lengths[step * rows + r])
    live = lax.axis_index("seq") * block + lax.rem(at, block) < limit
    chain(stored, weights, arrivals, small, hidden, teacher, live, s_context, sums, final, grad_first,
          grad_ctx, pres, slopes, bounds)

    @pl.when(step == pl.num_programs(0) - 1)
    def _():
        sums_out[...] = sums[...]


def back_kernel(scale, weights, small, s_query, s_key, s_value, s_context, spread, probs, gaps, grad_ctx,
                pulled_in, own_in, sums, key_grads, value_grads, query_grads):
    step = pl.program_id(0)

    @pl.when(step == 0)
    def _():
        sums[...] = jnp.zeros_like(sums)

    attend_back_row(scale, small, s_query.at[0], s_key.at[0], s_value.at[0],
                    s_context.at[0], spread.at[0], probs.at[0], gaps.at[0],
                    grad_ctx, key_grads, value_grads, query_grads)
    back = query_grads[...]
    raw = small[A_Q : A_Q + 1] * s_query[0] + small[B_Q : B_Q + 1]
    sums[0] += folded(raw * back)
    query_grad = back * small[A_K : A_K + 1]
    sums[1] += folded(query_grad * s_query[0])
    sums[2] += folded(query_grad)
    own_in[...] = dot_nn((query_grad * small[A_Q : A_Q + 1]).astype(BF16), weights[0])
    pulled_in[0] = (dot_nn(key_grads[...], weights[1]) + dot_nn(value_grads[...], weights[2])).astype(BF16)


def last_kernel(
    scale, dp_count, weights, table, s_query, s_key, s_value, s_context, spread, probs, gaps, grad_ctx,
    hidden, grad_first, bounds_in, own_bounds, chain_sums, distill,
    grad_input, early, late,
    query_grads, partial, kept, near, sent, far, sums,
    mine_a, slices_a, mine_b, slices_b, pieces, pieces_b,
    near_sems, far_sems, a_sems, b_sems,
):
    step = pl.program_id(0)
    rows = partial.shape[1]
    block, width = s_query.shape[1], s_query.shape[2]
    size = width // dp_count
    dp, seq = lax.axis_index("dp"), lax.axis_index("seq")
    yi, ci = seq // 2, seq % 2
    across, beside = (1 - yi) * 2 + ci, yi * 2 + 1 - ci
    corner = (1 - yi) * 2 + 1 - ci
    peers = (across, beside, corner)

    def positions(place):
        return pl.ds(pl.multiple_of(place * block, block), block)

    def near_copy(r, kind, which):
        place = beside if which == 0 else corner
        return remote(partial.at[kind, r, positions(place)], near.at[kind, r, which], near_sems.at[0, kind, r, which],
                      near_sems.at[1, kind, r, which], dp, beside)

    def far_copy(r):
        return remote(sent.at[r], far.at[r], far_sems.at[0, r], far_sems.at[1, r], dp, across)

    def scatter(mine, slices, sems, k):
        to = lax.rem(dp + k, dp_count)
        return remote(mine.at[to], slices.at[k], sems.at[0, k], sems.at[1, k], to, seq)

    def scatter_done(mine, slices, sems):
        total = mine[dp]
        for k in range(1, dp_count):
            scatter(mine, slices, sems, k).wait()
            total = total + slices[k]
        return total

    def swap(pieces, sems, k):
        return remote(pieces.at[0], pieces.at[k], sems.at[0, dp_count + k - 1], sems.at[1, dp_count + k - 1], dp, peers[k - 1])

    def swap_done(pieces, sems):
        total = pieces[0]
        for k in range(1, 4):
            swap(pieces, sems, k).wait()
            total = total + pieces[k]
        return total

    @pl.when(step == 0)
    def _():
        sums[...] = jnp.zeros_like(sums)
        barrier = pltpu.get_barrier_semaphore()
        for k in range(1, dp_count):
            pl.semaphore_signal(barrier, inc=1, device_id=(lax.rem(dp + k, dp_count), seq), device_id_type=MESH)
        for peer in peers:
            pl.semaphore_signal(barrier, inc=1, device_id=(dp, peer), device_id_type=MESH)
        pl.semaphore_wait(barrier, dp_count + 2)
        columns_of = [jnp.sum(chain_sums[i], axis=0, keepdims=True) for i in range(LOSS)]
        objective = 0.5 * jnp.sum(chain_sums[LOSS]) + 0.5 * SCORE_WEIGHT * jnp.sum(distill[...])
        columns_of.append(jnp.full((1, width), objective, F32))
        columns_of.append(jnp.zeros((PAIR - len(columns_of), width), F32))
        mine_a[...] = jnp.transpose(jnp.concatenate(columns_of, axis=0)).reshape(mine_a.shape)
        for k in range(1, dp_count):
            scatter(mine_a, slices_a, a_sems, k).start()

    @pl.when(step == 2)
    def _():
        pieces[0] = scatter_done(mine_a, slices_a, a_sems)
        for k in range(1, 4):
            swap(pieces, a_sems, k).start()

    @pl.when(step == 4)
    def _():
        early[...] = swap_done(pieces, a_sems)

    def joined(kind, r, which, place):
        near_copy(r, kind, which).wait_recv()
        return (partial[kind, r, positions(place)].astype(F32) + near[kind, r, which].astype(F32)).astype(BF16)

    def hand_over(r):
        low = None
        for kind in range(2):
            both = jnp.concatenate([joined(kind, r, 1, across), joined(kind, r, 0, seq)], axis=0)
            part = dot_nn(both, weights[1 + kind])
            low = part if low is None else low + part
        sent[r] = low[:block].astype(BF16)
        far_copy(r).start()
        kept[r] = kept[r] + low[block:]
        sums[3] += folded(low[:block] * bounds_in[0, positions(across)].astype(F32))
        sums[3] += folded(low[block:] * bounds_in[0, positions(seq)].astype(F32))

    def settle(r):
        far_copy(r).wait_recv()
        grad_low = kept[r] + far[r].astype(F32)
        unused, slope, bound = clip_parts(hidden[0].astype(F32), table[C_IN : C_IN + 1])
        grad_input[0] = grad_first[...] + grad_low * slope

    @pl.when(step < rows)
    def _():
        attend_back_row(scale, table, s_query.at[0], s_key.at[0], s_value.at[0],
                        s_context.at[0], spread.at[0], probs.at[0], gaps.at[0],
                        grad_ctx, partial.at[0, step], partial.at[1, step], query_grads)
        for kind in range(2):
            near_copy(step, kind, 1).start()
        for kind in range(2):
            near_copy(step, kind, 0).start()
        back = query_grads[...]
        raw = table[A_Q : A_Q + 1] * s_query[0] + table[B_Q : B_Q + 1]
        sums[0] += folded(raw * back)
        query_grad = back * table[A_K : A_K + 1]
        sums[1] += folded(query_grad * s_query[0])
        sums[2] += folded(query_grad)
        kept[step] = dot_nn((query_grad * table[A_Q : A_Q + 1]).astype(BF16), weights[0])
        sums[3] += folded(kept[step] * own_bounds[0].astype(F32))

    @pl.when((step > 0) & (step <= rows))
    def _():
        hand_over(step - 1)

    @pl.when(step == rows)
    def _():
        columns_of = [jnp.sum(sums[i], axis=0, keepdims=True) for i in range(4)]
        columns_of.append(jnp.zeros((PAIR - len(columns_of), width), F32))
        turned = jnp.transpose(jnp.concatenate(columns_of, axis=0))
        for k in range(dp_count):
            part = jnp.transpose(turned[k * size : (k + 1) * size])[:8]
            mine_b[k] = jnp.concatenate([part, jnp.zeros((8, PAIR - size), F32)], axis=1)
        for k in range(1, dp_count):
            scatter(mine_b, slices_b, b_sems, k).start()

    @pl.when(step > 2)
    def _():
        settle(step - 3)

    @pl.when(step == rows)
    def _():
        pieces_b[0] = scatter_done(mine_b, slices_b, b_sems)
        for k in range(1, 4):
            swap(pieces_b, b_sems, k).start()

    @pl.when(step == pl.num_programs(0) - 1)
    def _():
        for r in range(rows):
            for kind in range(2):
                near_copy(r, kind, 0).wait_send()
                near_copy(r, kind, 1).wait_send()
            far_copy(r).wait_send()
        late[...] = swap_done(pieces_b, b_sems)


def finish_kernel(early, late, *refs):
    latents, grads, vectors = refs[:6], refs[6:12], refs[12:]
    size = early.shape[0]
    first, second = jnp.transpose(early[...]), late[...]
    turned = jnp.transpose(jnp.concatenate([second] * (PAIR // 8), axis=0))[:size]

    def row(value, i):
        return value[i : i + 1, :size]

    sums = [turned[:, 1:2], turned[:, 0:1], early[:, G_V : G_V + 1], early[:, G_O : G_O + 1], None, early[:, G_D : G_D + 1]]
    lane = lax.broadcasted_iota(jnp.int32, (4 * size, PAIR), 1)
    wide = jnp.zeros((4 * size, PAIR), F32)
    for m in range(3):
        column = jnp.concatenate([early[:, G_U + 4 * m + i : G_U + 4 * m + i + 1] for i in range(4)], axis=0)
        wide = jnp.where(lane == m, column, wide)
    wide = jnp.transpose(wide)
    sums[4] = wide[0:1]
    for i, (latent, grad, total) in enumerate(zip(latents, grads, sums)):
        grad[...] = signed(latent[...]) * (total / latent.shape[0 if i == 4 else 1])
    loss, given = vectors[-1], vectors[:-1]
    loss[...] = jnp.broadcast_to(row(first, LOSS), loss.shape)
    parts = [row(second, 2), row(first, G_BV), row(first, G_BO), wide[1:2], row(first, G_BD), row(first, G_G1),
             row(first, G_S1), row(first, G_G2), row(first, G_S2), row(second, 3), row(first, G_CCTX), row(first, G_CMID),
             wide[2:3]]
    for ref, part in zip(given, parts):
        ref[...] = part[0]


def signs_and_scale(latent):
    scale = jnp.mean(jnp.abs(latent), axis=0).astype(BF16)
    return jnp.sign(latent).astype(BF16).T, scale


def body(
    hidden_in,
    segment_ids,
    row_lengths,
    teacher_scores,
    teacher_hidden,
    w_query,
    w_key,
    w_value,
    w_out,
    w_up,
    w_down,
    b_query,
    b_value,
    b_out,
    b_up,
    b_down,
    norm1_gain,
    norm1_bias,
    norm2_gain,
    norm2_bias,
    clip_in,
    clip_ctx,
    clip_mid,
    clip_hid,
):
    rows, block, width = hidden_in.shape
    heads = teacher_scores.shape[1]
    head_dim = width // heads
    seq_len = segment_ids.shape[1]
    tokens = rows * block
    scale = head_dim ** (-0.5)
    place = lax.axis_index("seq")
    first = place * block

    dp_count = lax.axis_size("dp")
    size = w_query.shape[1]
    tuned = dp_count == 8 and rows == 8 and size % 32 == 0 and lax.axis_size("seq") == 4
    given = jnp.stack([b_query, b_value, b_out, b_down, norm1_gain, norm1_bias, norm2_gain, norm2_bias, clip_in, clip_ctx, clip_mid])
    given_wide = jnp.stack([b_up, clip_hid])

    def row_spec(*shape):
        return pl.BlockSpec((1,) + shape, lambda i: (i,) + (0,) * len(shape))

    def whole(array):
        return pl.BlockSpec(array.shape, lambda i: (0,) * array.ndim, pipeline_mode=pl.Buffered(1))

    three = pl.BlockSpec((3, width, width), lambda i: (0, 0, 0), pipeline_mode=pl.Buffered(1))
    attend_specs = [row_spec(block, width), row_spec(seq_len, width), row_spec(seq_len, width), row_spec(block, width),
                    row_spec(block, width), row_spec(heads, block, seq_len), row_spec(heads, block, seq_len),
                    row_spec(seq_len, width), row_spec(block, width), pl.BlockSpec((8, seq_len), lambda i: (0, 0))]
    attend_shapes = [jax.ShapeDtypeStruct((rows, block, width), F32),
                     jax.ShapeDtypeStruct((rows, seq_len, width), BF16),
                     jax.ShapeDtypeStruct((rows, seq_len, width), BF16),
                     jax.ShapeDtypeStruct((rows, block, width), F32),
                     jax.ShapeDtypeStruct((rows, block, width), F32),
                     jax.ShapeDtypeStruct((rows, heads, block, seq_len), BF16),
                     jax.ShapeDtypeStruct((rows, heads, block, seq_len), BF16),
                     jax.ShapeDtypeStruct((rows, seq_len, width), BF16),
                     jax.ShapeDtypeStruct((rows, block, width), BF16),
                     jax.ShapeDtypeStruct((8, seq_len), F32)]
    teacher_spec = row_spec(heads, block, seq_len)
    scalars = pl.BlockSpec(memory_space=pltpu.SMEM)
    latents = (w_query.T, w_key.T, w_value.T, w_out.T, w_up, w_down.T)
    anywhere = pl.BlockSpec(memory_space=pl.ANY)
    lines = dp_count // 2
    sems = pltpu.SemaphoreType.DMA
    if tuned:
        full, table, s_query, s_key, s_value, s_context, spread, probs, gaps, bounds_in, own_bounds, distill = pl.pallas_call(
            functools.partial(first_kernel, scale, dp_count),
            grid=(rows,),
            in_specs=[scalars, whole(segment_ids)] + [whole(w) for w in latents] + [whole(given), whole(given_wide), anywhere,
                      row_spec(block, width), teacher_spec],
            out_specs=[anywhere, pl.BlockSpec((VECTORS, width), lambda i: (0, 0))] + attend_specs,
            out_shape=[jax.ShapeDtypeStruct((UNITS, width, width), BF16), jax.ShapeDtypeStruct((VECTORS, width), F32)]
            + attend_shapes,
            scratch_shapes=[
                pltpu.VMEM((UNITS, size, width), BF16), pltpu.VMEM((size, PAIR), F32), pltpu.VMEM((size, PAIR), BF16),
                pltpu.VMEM((rows, seq_len, width), BF16), pltpu.VMEM((width, PAIR), BF16), pltpu.VMEM((3, width, width), BF16),
                sems((2, UNITS)), sems((UNITS, lines)), sems((UNITS, lines)), sems((2, 2 * len(SHARED))),
                sems((2, UNITS)), sems((UNITS,)), sems((2, 3, rows)), sems((rows,)), sems((2, dp_count)), sems((3,)),
                pltpu.VMEM((block, seq_len), F32), pltpu.VMEM((block, seq_len), F32),
            ],
            compiler_params=pltpu.CompilerParams(collective_id=0, has_side_effects=True, vmem_limit_bytes=60 * 2**20),
        )(row_lengths, segment_ids, *latents, given, given_wide, hidden_in, hidden_in, teacher_scores)
    else:
        square = [signs_and_scale(w) for w in (w_query, w_key, w_value, w_out)]
        up_signs, up_scale = signs_and_scale(w_up)
        down = w_down.reshape(dp_count, 4, size, size)
        down_signs = jnp.sign(down).astype(BF16).transpose(1, 3, 0, 2).reshape(4, size, width)
        down_scale = jnp.mean(jnp.abs(w_down), axis=0).astype(BF16)
        pairs = jnp.stack([up_signs.reshape(4, size, width), down_signs], axis=1).reshape(8, size, width)
        own = jnp.concatenate([jnp.stack([s for s, _ in square]), pairs])
        own_vectors = jnp.concatenate(
            [jnp.stack([*(a for _, a in square), down_scale, b_query, b_value, b_out, b_down, norm1_gain, norm1_bias,
                        norm2_gain, norm2_bias, clip_in, clip_ctx, clip_mid]),
             up_scale.reshape(4, size), b_up.reshape(4, size), clip_hid.reshape(4, size)]
        )
        own_vectors = jnp.pad(own_vectors.T, ((0, 0), (0, PAIR - own_vectors.shape[0])))

        full = lax.all_gather(own, "dp", axis=1, tiled=True)
        table = lax.all_gather(own_vectors, "dp", axis=0, tiled=True).astype(F32).T[:VECTORS]
        hidden_full = lax.all_gather(hidden_in, "seq", axis=1, tiled=True)
        s_query, s_key, s_value, s_context, spread, probs, gaps, bounds_in, own_bounds, distill = pl.pallas_call(
            functools.partial(plain_kernel, scale),
            grid=(rows,),
            in_specs=[scalars, whole(segment_ids), row_spec(seq_len, width), row_spec(block, width), three, whole(table),
                      teacher_spec],
            out_specs=attend_specs,
            out_shape=attend_shapes,
            scratch_shapes=[pltpu.VMEM((block, seq_len), F32), pltpu.VMEM((block, seq_len), F32)],
            compiler_params=pltpu.CompilerParams(vmem_limit_bytes=60 * 2**20),
        )(row_lengths, segment_ids, hidden_full, hidden_in, full, table, teacher_scores)

    group = 2
    def group_spec(*shape):
        return pl.BlockSpec((group,) + shape, lambda i: (i,) + (0,) * len(shape))
    flat_spec = pl.BlockSpec((group * block, width), lambda i: (i, 0))
    def flat_spec(buffers):
        return pl.BlockSpec((group * block, width), lambda i: (i, 0), pipeline_mode=pl.Buffered(buffers))

    final, grad_first, grad_ctx, sums = pl.pallas_call(
        functools.partial(chain_kernel, group),
        grid=(rows // group,),
        in_specs=[scalars, pl.BlockSpec(memory_space=pl.ANY), whole(table), flat_spec(2), flat_spec(2), flat_spec(2)],
        out_specs=[flat_spec(2), flat_spec(2), flat_spec(2),
                   pl.BlockSpec((SUMS, 8, width), lambda i: (0, 0, 0))],
        out_shape=[jax.ShapeDtypeStruct((tokens, width), BF16),
                   jax.ShapeDtypeStruct((tokens, width), F32),
                   jax.ShapeDtypeStruct((tokens, width), F32),
                   jax.ShapeDtypeStruct((SUMS, 8, width), F32)],
        scratch_shapes=[pltpu.VMEM((UNITS - 3, width, width), BF16), pltpu.SemaphoreType.DMA((UNITS - 3,)),
                        pltpu.VMEM((SUMS, 8, width), F32)]
        + [pltpu.VMEM((4, group * block, width), F32)] * 3,
        compiler_params=pltpu.CompilerParams(vmem_limit_bytes=63 * 2**20),
    )(row_lengths, full, table, hidden_in.reshape(tokens, width), teacher_hidden.reshape(tokens, width),
      s_context.reshape(tokens, width))
    if tuned:
        def now_spec(*shape):
            return pl.BlockSpec((1,) + shape, lambda i: (jnp.minimum(i, rows - 1),) + (0,) * len(shape))

        def then_spec(*shape):
            return pl.BlockSpec((1,) + shape, lambda i: (jnp.maximum(i - 3, 0),) + (0,) * len(shape))

        own_spec = now_spec(block, width)
        grad_input, early, late = pl.pallas_call(
            functools.partial(last_kernel, scale, dp_count),
            grid=(rows + 3,),
            in_specs=[three, whole(table), now_spec(block, width), now_spec(seq_len, width), now_spec(seq_len, width),
                      now_spec(block, width), now_spec(block, width), now_spec(heads, block, seq_len),
                      now_spec(heads, block, seq_len), pl.BlockSpec((block, width), lambda i: (jnp.minimum(i, rows - 1), 0)),
                      then_spec(block, width), pl.BlockSpec((block, width), lambda i: (jnp.maximum(i - 3, 0), 0)),
                      pl.BlockSpec((1, seq_len, width), lambda i: (jnp.clip(i - 1, 0, rows - 1), 0, 0)),
                      own_spec, whole(sums), whole(distill)],
            out_specs=[then_spec(block, width), pl.BlockSpec((size, PAIR), lambda i: (0, 0)), pl.BlockSpec((8, PAIR), lambda i: (0, 0))],
            out_shape=[jax.ShapeDtypeStruct((rows, block, width), F32), jax.ShapeDtypeStruct((size, PAIR), F32),
                       jax.ShapeDtypeStruct((8, PAIR), F32)],
            scratch_shapes=[
                pltpu.VMEM((block, width), F32),
                pltpu.VMEM((2, rows, seq_len, width), BF16), pltpu.VMEM((rows, block, width), F32),
                pltpu.VMEM((2, rows, 2, block, width), BF16), pltpu.VMEM((rows, block, width), BF16),
                pltpu.VMEM((rows, block, width), BF16), pltpu.VMEM((4, 8, width), F32),
                pltpu.VMEM((dp_count, size, PAIR), F32), pltpu.VMEM((dp_count, size, PAIR), F32),
                pltpu.VMEM((dp_count, 8, PAIR), F32), pltpu.VMEM((dp_count, 8, PAIR), F32),
                pltpu.VMEM((4, size, PAIR), F32), pltpu.VMEM((4, 8, PAIR), F32),
                sems((2, 2, rows, 2)), sems((2, rows)), sems((2, dp_count + 3)), sems((2, dp_count + 3)),
            ],
            compiler_params=pltpu.CompilerParams(collective_id=1, has_side_effects=True, vmem_limit_bytes=60 * 2**20),
        )(full, table, s_query, s_key, s_value, s_context, spread, probs, gaps, grad_ctx, hidden_in, grad_first, bounds_in, own_bounds, sums, distill)
        def one_block(shape):
            return pl.BlockSpec(shape, lambda: (0,) * len(shape))

        small_shapes = [w.shape for w in (b_query, b_value, b_out, b_up, b_down, norm1_gain, norm1_bias, norm2_gain,
                                                  norm2_bias, clip_in, clip_ctx, clip_mid, clip_hid)]
        results = pl.pallas_call(
            finish_kernel,
            in_specs=[one_block(early.shape), one_block(late.shape)] + [one_block(w.shape) for w in latents],
            out_specs=[one_block(w.shape) for w in latents] + [one_block(shape) for shape in small_shapes] + [one_block((1, size))],
            out_shape=[jax.ShapeDtypeStruct(w.shape, F32) for w in latents]
            + [jax.ShapeDtypeStruct(shape, F32) for shape in small_shapes]
            + [jax.ShapeDtypeStruct((1, size), F32)],
            compiler_params=pltpu.CompilerParams(vmem_limit_bytes=60 * 2**20),
        )(early, late, *latents)
        loss = results[-1][0, 0] / (dp_count * rows * seq_len)
        return (
            (final.reshape(rows, block, width), loss, grad_input.reshape(rows, block, width))
            + tuple(grad if i == 4 else grad.T for i, grad in enumerate(results[:6]))
            + tuple(results[6:-1])
        )
    else:
        one_spec = pl.BlockSpec((block, width), lambda i: (i, 0))
        pulled_in, own_in, more = pl.pallas_call(
            functools.partial(back_kernel, scale),
            grid=(rows,),
            in_specs=[three, whole(table),
                      row_spec(block, width), row_spec(seq_len, width), row_spec(seq_len, width), row_spec(block, width),
                      row_spec(block, width), row_spec(heads, block, seq_len), row_spec(heads, block, seq_len), one_spec],
            out_specs=[row_spec(seq_len, width), one_spec, pl.BlockSpec((3, 8, width), lambda i: (0, 0, 0))],
            out_shape=[jax.ShapeDtypeStruct((rows, seq_len, width), BF16),
                       jax.ShapeDtypeStruct((tokens, width), F32),
                       jax.ShapeDtypeStruct((3, 8, width), F32)],
            scratch_shapes=[pltpu.VMEM((seq_len, width), BF16), pltpu.VMEM((seq_len, width), BF16),
                            pltpu.VMEM((block, width), F32)],
            compiler_params=pltpu.CompilerParams(vmem_limit_bytes=60 * 2**20),
        )(full, table, s_query, s_key, s_value, s_context, spread, probs, gaps, grad_ctx)
        sums = sums.at[G_K].set(more[0]).at[G_Q].set(more[1]).at[G_BQ].set(more[2])
        objective = 0.5 * jnp.sum(sums[LOSS]) + 0.5 * SCORE_WEIGHT * jnp.sum(distill)

        crossed = lax.psum_scatter(pulled_in, "seq", scatter_dimension=1, tiled=True).astype(F32)
        grad_low = own_in + crossed.reshape(tokens, width)
        inputs = hidden_in.astype(F32).reshape(tokens, width)
        unused, in_slope, in_bound = clip_parts(inputs, table[C_IN : C_IN + 1])
        grad_input = grad_first + grad_low * in_slope
        sums = jnp.sum(sums, axis=1)
        wide_sums = sums[16:28]
        sums = sums[:16].at[G_CIN].set(columns(grad_low * in_bound)[0])
        sums, wide_sums, objective = lax.psum((sums, wide_sums, objective), ("dp", "seq"))
        at = lax.axis_index("dp")
        sums = lax.dynamic_slice_in_dim(sums, at * size, size, 1)
        wide_sums = lax.dynamic_slice_in_dim(wide_sums, at * size, size, 1).reshape(3, 4 * size)
    loss = objective / (lax.axis_size("dp") * rows * seq_len)
    grads = [
        jnp.sign(w) * (s / w.shape[0])
        for w, s in zip(
            (w_query, w_key, w_value, w_out, w_up, w_down),
            (sums[0], sums[1], sums[2], sums[3], wide_sums[0], sums[4]),
        )
    ]
    return (
        final.reshape(rows, block, width).astype(BF16),
        loss,
        grad_input.reshape(rows, block, width),
        *grads,
        sums[5],
        sums[6],
        sums[7],
        wide_sums[1],
        sums[8],
        sums[9],
        sums[10],
        sums[11],
        sums[12],
        sums[13],
        sums[14],
        sums[15],
        wide_sums[2],
    )


def solution(mesh):
    rows = P("dp", "seq", None)
    cols = P(None, "dp")
    vec = P("dp")
    return jax.shard_map(
        body,
        mesh=mesh,
        in_specs=(rows, P("dp", None), vec, P("dp", None, "seq", None), rows)
        + (cols,) * 6
        + (vec,) * 13,
        out_specs=(rows, P(), rows) + (cols,) * 6 + (vec,) * 13,
        check_vma=False,
    )
```

```python
import functools

import jax
import jax.numpy as jnp
from jax import lax
from jax.experimental import pallas as pl
from jax.experimental.pallas import tpu as pltpu
from jax.sharding import PartitionSpec as P

EPS = 1e-05
SCORE_WEIGHT = 0.0625
NEGATIVE = -1e30
F32 = jnp.float32
BF16 = jnp.bfloat16
PAIR = 128
HEAD = 64
GROUP = 256
A_Q, A_K, A_V, A_O, A_D, B_Q, B_V, B_O, B_D, G1, S1, G2, S2, C_IN, C_CTX, C_MID = range(16)
A_U, B_U, C_HID, VECTORS = 16, 20, 24, 32
G_Q, G_K, G_V, G_O, G_D, G_BQ, G_BV, G_BO, G_BD, G_G1, G_S1, G_G2, G_S2, G_CIN, G_CCTX, G_CMID = range(16)
G_U, G_BU, G_CHID, LOSS, SUMS = 16, 20, 24, 28, 29


def dot_nt(left, right):
    return lax.dot_general(left, right, (((1,), (1,)), ((), ())), preferred_element_type=F32)


def dot_nn(left, right):
    return lax.dot_general(left, right, (((1,), (0,)), ((), ())), preferred_element_type=F32)


def dot_tn(left, right):
    return lax.dot_general(left, right, (((0,), (0,)), ((), ())), preferred_element_type=F32)


def columns(value):
    return jnp.sum(value, axis=0, keepdims=True)


def clip_parts(value, bound):
    ratio = value / bound
    bent = jnp.tanh(ratio)
    slope = 1.0 - bent * bent
    return bound * bent, slope, bent - ratio * slope


def norm_parts(value, gain, shift):
    centre = value - jnp.mean(value, axis=-1, keepdims=True)
    inverse = lax.rsqrt(jnp.mean(centre * centre, axis=-1, keepdims=True) + EPS)
    unit = centre * inverse
    return unit * gain + shift, unit, inverse


def norm_back(grad, unit, inverse, gain):
    scaled = grad * gain
    return inverse * (
        scaled
        - jnp.mean(scaled, axis=-1, keepdims=True)
        - unit * jnp.mean(scaled * unit, axis=-1, keepdims=True)
    )


def stacked(value):
    lane = lax.broadcasted_iota(jnp.int32, value.shape, 1)
    zero = jnp.zeros_like(value)
    return jnp.concatenate([jnp.where(lane // HEAD == i, value, zero) for i in range(GROUP // HEAD)], axis=0)


def by_head(parts):
    shape = jnp.broadcast_shapes(parts[0].shape, (1, GROUP))
    lane = lax.broadcasted_iota(jnp.int32, shape, 1)
    result = parts[-1]
    for i in range(len(parts) - 2, -1, -1):
        result = jnp.where(lane < (i + 1) * HEAD, parts[i], result)
    return result


def folded(value):
    return jnp.sum(value.reshape(value.shape[0] // 8, 8, value.shape[1]), axis=0)


def mask_row(segments, lengths, row, start, bias, counted):
    block, seq_len = bias.shape
    keys = segments[pl.ds(row, 1), :].astype(F32)
    mine = keys[:, :block]
    for i in range(1, seq_len // block):
        mine = jnp.where(start == i * block, keys[:, i * block : (i + 1) * block], mine)
    queries = jnp.transpose(jnp.broadcast_to(mine, (block, block)))
    same = jnp.concatenate([queries] * (seq_len // block), axis=1) == keys
    length = lengths[row]
    query_at = start + lax.broadcasted_iota(jnp.int32, (block, seq_len), 0)
    key_at = lax.broadcasted_iota(jnp.int32, (block, seq_len), 1)
    bias[...] = jnp.where(same, 0.0, NEGATIVE)
    counted[...] = jnp.where(same & (query_at < length) & (key_at < length), 1.0, 0.0)


def signed(value):
    return jnp.where(value > 0, 1.0, jnp.where(value < 0, -1.0, 0.0))


def pack(squares, up, down, vectors_in, own, own_vectors, which):
    size = own.shape[1]
    width = own.shape[2]
    lane = lax.broadcasted_iota(jnp.int32, own_vectors.shape, 1)

    def put(unit, turned, kind):
        own[unit] = signed(turned).astype(BF16)
        scale = jnp.sum(jnp.abs(turned), axis=1, keepdims=True) / width
        own_vectors[...] = jnp.where(lane == kind, scale.astype(BF16).astype(F32), own_vectors[...])

    if which == 0:
        size = own.shape[1]
        zeros = functools.partial(jnp.zeros, dtype=F32)
        columns = jnp.transpose(
            jnp.concatenate([zeros((5, size)), vectors_in[0][...].astype(F32), zeros((PAIR - 16, size))], axis=0)
        )
        wide = jnp.transpose(
            jnp.concatenate([vectors_in[1][...].astype(F32), zeros((PAIR - 2, 4 * size))], axis=0)
        )
        for kind in range(2):
            for i in range(4):
                columns = jnp.where(lane == B_U + 4 * kind + i, wide[i * size : (i + 1) * size, kind : kind + 1], columns)
        own_vectors[...] = columns
        for unit in range(3):
            put(unit, squares[unit][...], A_Q + unit)
        return
    put(3, squares[3][...], A_O)
    turned = jnp.transpose(up[...])
    for i in range(4):
        part = turned[i * size : (i + 1) * size]
        own[4 + 2 * i] = signed(part).astype(BF16)
        scale = jnp.sum(jnp.abs(part), axis=1, keepdims=True) / width
        own_vectors[...] = jnp.where(lane == A_U + i, scale.astype(BF16).astype(F32), own_vectors[...])
    groups = down.shape[1] // (4 * size)
    scale = jnp.sum(jnp.abs(down[...]), axis=1, keepdims=True) / down.shape[1]
    own_vectors[...] = jnp.where(lane == A_D, scale.astype(BF16).astype(F32), own_vectors[...])
    straight = jnp.transpose(signed(down[...]))
    for i in range(4):
        part = jnp.concatenate([straight[(4 * j + i) * size : (4 * j + i + 1) * size] for j in range(groups)], axis=0)
        own[5 + 2 * i] = jnp.transpose(part).astype(BF16)


def project_row(hidden, own_hidden, sq, sk, sv, small, s_query, s_key, s_value, bounds_in, own_bounds):
    c_in = small[C_IN : C_IN + 1]
    inverse_in = 1.0 / c_in
    ratio = hidden[...].astype(F32) * inverse_in
    bent = jnp.tanh(ratio)
    bounds_in[...] = (bent - ratio * (1.0 - bent * bent)).astype(BF16)
    low = (c_in * bent).astype(BF16)
    s_key[...] = dot_nt(low, sk[...]).astype(BF16)
    s_value[...] = dot_nt(low, sv[...]).astype(BF16)
    ratio = own_hidden[...].astype(F32) * inverse_in
    bent = jnp.tanh(ratio)
    own_bounds[...] = (bent - ratio * (1.0 - bent * bent)).astype(BF16)
    low = (c_in * bent).astype(BF16)
    s_query[...] = dot_nt(low, sq[...])


def attend_row(
    scale, small, teacher, s_query, s_key, s_value, s_context, spread, probs, gaps, distill, bias, counted,
    first, last,
):
    block, width = s_query.shape

    def some(index, carry):
        at = pl.ds(pl.multiple_of(index * GROUP, GROUP), GROUP)
        query = (
            (small[A_Q : A_Q + 1, at] * s_query[:, at] + small[B_Q : B_Q + 1, at])
            * (small[A_K : A_K + 1, at] * scale)
        ).astype(BF16)
        scores = dot_nt(stacked(query), s_key[:, at])
        expos, inverses = [], []
        sums = jnp.zeros((8, scores.shape[1]), F32)
        for head in range(GROUP // HEAD):
            mine = scores[head * block : (head + 1) * block]
            gap = (mine - teacher[GROUP // HEAD * index + head].astype(F32)) * counted[...]
            sums = sums + folded(gap * gap)
            gaps[GROUP // HEAD * index + head] = (gap * SCORE_WEIGHT).astype(BF16)
            masked = mine + bias[...]
            expo = jnp.exp(masked - jnp.max(masked, axis=-1, keepdims=True))
            inverses.append(1.0 / jnp.sum(expo, axis=-1, keepdims=True))
            expo = expo.astype(BF16)
            probs[GROUP // HEAD * index + head] = expo
            expos.append(expo)
        distill[...] += sums
        both = dot_nn(jnp.concatenate(expos, axis=0), s_value[:, at])
        inverse = by_head(inverses)
        s_context[:, at] = by_head([both[h * block : (h + 1) * block] for h in range(GROUP // HEAD)]) * inverse
        spread[:, at] = inverse
        return carry

    lax.fori_loop(first, last, some, 0)


MESH = pl.DeviceIdType.MESH
UNITS = 12
STEPS = 10
SHARED = (6, 7)

def remote(source, target, send, recv, dp, seq):
    return pltpu.make_async_remote_copy(
        src_ref=source, dst_ref=target, send_sem=send, recv_sem=recv, device_id=(dp, seq), device_id_type=MESH
    )

class Streams:
    def __init__(self, lines, own, full, s_sems, z_sems, x_sems, y_sems, c_sems, l_sems):
        self.lines, self.own, self.full = lines, own, full
        self.s_sems, self.z_sems, self.x_sems, self.y_sems, self.c_sems, self.l_sems = s_sems, z_sems, x_sems, y_sems, c_sems, l_sems
        self.dp, self.seq = lax.axis_index("dp"), lax.axis_index("seq")
        self.zi, self.xi = self.dp // 2, self.dp % 2
        self.yi, self.ci = self.seq // 2, self.seq % 2
        self.size = own.shape[1]
        self.half = self.size // 2

    def unit(self, t, partner=False):
        if t in SHARED:
            return SHARED[0] + 2 * (t - SHARED[0]) + (1 - self.yi if partner else self.yi)
        return t if t < SHARED[0] else t + 2

    def piece(self, u, dp):
        start = pl.multiple_of(dp * self.size + self.ci * self.half, self.half)
        return self.full.at[u, pl.ds(start, self.half)]

    def own_piece(self, u):
        return self.own.at[u, pl.ds(pl.multiple_of(self.ci * self.half, self.half), self.half)]

    def z_copy(self, u, src, to):
        place = self.piece(u, src * 2 + self.xi)
        return remote(self.own_piece(u) if src is self.zi else place, place,
                      self.s_sems.at[0, u], self.z_sems.at[u, src], to * 2 + self.xi, self.seq)

    def x_copy(self, u, src):
        place = self.piece(u, src * 2 + self.xi)
        return remote(self.own_piece(u) if src is self.zi else place, place, self.s_sems.at[1, u], self.x_sems.at[u, src],
                      self.zi * 2 + 1 - self.xi, self.seq)

    def x_arrival(self, u, src):
        place = self.piece(u, src * 2 + 1 - self.xi)
        return remote(place, place, self.s_sems.at[1, u], self.x_sems.at[u, src], self.zi * 2 + 1 - self.xi, self.seq)

    def y_copy(self, u, dp):
        place = self.piece(u, dp)
        return remote(place, place, self.y_sems.at[0, u - SHARED[0]], self.y_sems.at[1, u - SHARED[0]], self.dp, (1 - self.yi) * 2 + self.ci)

    def c_copy(self, u, dp):
        place = self.piece(u, dp)
        return remote(place, place, self.c_sems.at[0, u], self.c_sems.at[1, u], self.dp, self.yi * 2 + 1 - self.ci)

    def local_copy(self, u):
        start = pl.multiple_of(self.dp * self.size, self.size)
        return pltpu.make_async_copy(self.own.at[u], self.full.at[u, pl.ds(start, self.size)], self.l_sems.at[u])

    def each_row(self, run):
        for k in range(1, self.lines):
            pl.when(self.zi >= k)(functools.partial(run, self.zi - k, True))
            pl.when(self.zi + k < self.lines)(functools.partial(run, self.zi + k, False))

    def neighbours(self, run):
        pl.when(self.zi > 0)(lambda: run(self.zi - 1))
        pl.when(self.zi < self.lines - 1)(lambda: run(self.zi + 1))

    def relay(self, src, below, run):
        if below:
            pl.when(self.zi < self.lines - 1)(lambda: run(self.zi + 1))
        else:
            pl.when(self.zi > 0)(lambda: run(self.zi - 1))

    def launch(self, t):
        u = self.unit(t)
        self.x_copy(u, self.zi).start()
        self.neighbours(lambda to: self.z_copy(u, self.zi, to).start())

    def at_distance(self, k, run):
        if k == 0:
            run(self.zi, None)
        else:
            pl.when(self.zi >= k)(functools.partial(run, self.zi - k, True))
            pl.when(self.zi + k < self.lines)(functools.partial(run, self.zi + k, False))

    def along_z(self, t, k):
        u = self.unit(t)
        def run(src, below):
            self.z_copy(u, src, self.zi).wait_recv()
            self.relay(src, below, lambda to: self.z_copy(u, src, to).start())
            self.x_copy(u, src).start()
            self.spread(t, u, src * 2 + self.xi)
        self.at_distance(k, run)

    def over_x(self, t, k):
        u = self.unit(t)
        def run(src, below):
            self.x_arrival(u, src).wait_recv()
            self.spread(t, u, src * 2 + 1 - self.xi)
        self.at_distance(k, run)

    def spread(self, t, u, dp):
        if t in SHARED:
            self.y_copy(u, dp).start()
        self.c_copy(u, dp).start()

    def others(self, run):
        self.each_row(lambda src, below: run(src * 2 + self.xi))
        run(self.zi * 2 + 1 - self.xi)
        self.each_row(lambda src, below: run(src * 2 + 1 - self.xi))

    def over_y(self, t):
        u = self.unit(t, True)
        self.bulk(u, 2 * self.lines - 1, self.y_sems.at[1, u - SHARED[0]])
        self.others(lambda dp: self.c_copy(u, dp).start())

    def arrived(self, u):
        self.bulk(u, 2 * self.lines - 1, self.c_sems.at[1, u])
        self.local_copy(u).wait()

    def bulk(self, u, pieces, sem):
        part = self.full.at[u, pl.ds(0, pieces * self.half)]
        pltpu.make_async_copy(part, part, sem).wait()

    def finish(self):
        inner = (self.zi > 0) & (self.zi < self.lines - 1)
        for t in range(STEPS):
            u = self.unit(t)
            pl.when(inner)(functools.partial(self.bulk, u, self.lines + 1, self.s_sems.at[0, u]))
            pl.when(jnp.logical_not(inner))(functools.partial(self.bulk, u, 1, self.s_sems.at[0, u]))
            self.bulk(u, self.lines, self.s_sems.at[1, u])
            if t in SHARED:
                self.bulk(u, 2 * self.lines - 1, self.y_sems.at[0, u - SHARED[0]])
        for u in range(UNITS):
            self.bulk(u, 2 * self.lines - 1, self.c_sems.at[0, u])


def greet(dp_count):
    dp, seq = lax.axis_index("dp"), lax.axis_index("seq")
    barrier = pltpu.get_barrier_semaphore()
    for k in range(1, dp_count):
        pl.semaphore_signal(barrier, inc=1, device_id=(lax.rem(dp + k, dp_count), seq), device_id_type=MESH)
    pl.semaphore_signal(barrier, inc=1, device_id=(dp, seq // 2 * 2 + 1 - seq % 2), device_id_type=MESH)
    pl.semaphore_signal(barrier, inc=1, device_id=(dp, (1 - seq // 2) * 2 + seq % 2), device_id_type=MESH)
    pl.semaphore_wait(barrier, dp_count + 1)

NEAR = 3


def first_kernel(
    scale, dp_count, lengths, segments, w_query, w_key, w_value, w_out, w_up, w_down, vectors_in, wide_in,
    hidden, own_hidden, teacher,
    full, table, s_query, s_key, s_value, s_context, spread, probs, gaps, bounds_in, own_bounds, distill,
    own, own_columns, own_vectors, whole, vectors, weights, s_sems, z_sems, x_sems, y_sems, c_sems, l_sems, h_sems, o_sems, v_sems, w_sems, bias, counted,
):
    step = pl.program_id(0)
    rows, block = hidden.shape[0], hidden.shape[1]
    s = Streams(dp_count // 2, own, full, s_sems, z_sems, x_sems, y_sems, c_sems, l_sems)
    across, beside = (1 - s.yi) * 2 + s.ci, s.yi * 2 + 1 - s.ci

    def place(r, seq):
        return whole.at[r, pl.ds(pl.multiple_of(seq * block, block), block)]

    def to_chip(r):
        return remote(hidden.at[r], place(r, s.seq), h_sems.at[0, 0, r], h_sems.at[1, 0, r], s.dp, across)

    def to_core(r):
        return remote(hidden.at[r], place(r, s.seq), h_sems.at[0, 1, r], h_sems.at[1, 1, r], s.dp, beside)

    def passed_on(r):
        return remote(place(r, across), place(r, across), h_sems.at[0, 2, r], h_sems.at[1, 2, r], s.dp, beside)

    def kept(r):
        return pltpu.make_async_copy(hidden.at[r], place(r, s.seq), o_sems.at[r])

    def hidden_pump(r):
        to_chip(r).wait_recv()
        passed_on(r).start()
        if r + NEAR < rows:
            to_chip(r + NEAR).start()

    def vector_copy(k):
        mine = vectors.at[pl.ds(pl.multiple_of(s.dp * s.size, s.size), s.size)]
        return remote(own_vectors, mine, v_sems.at[0, k], v_sems.at[1, k], lax.rem(s.dp + k, dp_count), s.seq)

    def fetch(u):
        return pltpu.make_async_copy(full.at[u], weights.at[u], w_sems.at[u])

    def point(r, j):
        if j == 0 and r + 3 < rows:
            hidden_pump(r + 3)
        for t in range(3, STEPS):
            at = 4 * r + j - 3 * (t - 3)
            if at == 0 and t + 2 < STEPS:
                s.launch(t + 2)
            if at in (0, 3, 6):
                s.along_z(t, at // 3 + 1)
            if at in (2, 5, 8, 11):
                s.over_x(t, at // 3)
            if t in SHARED and at == 16:
                s.over_y(t)

    def points(j):
        for r in range(rows):
            pl.when(step == r)(functools.partial(point, r, j))

    @pl.when(step == 0)
    def _():
        distill[...] = jnp.zeros_like(distill)
        latents = (w_query, w_key, w_value, w_out), w_up, w_down
        pack(*latents, (vectors_in, wide_in), own, own_columns, 0)
        greet(dp_count)
        for r in range(NEAR):
            to_chip(r).start()
        for t in range(3):
            s.launch(t)
        pack(*latents, (vectors_in, wide_in), own, own_columns, 1)
        own_vectors[...] = own_columns[...].astype(BF16)
        for k in range(1, dp_count):
            vector_copy(k).start()
        for u in range(UNITS):
            s.local_copy(u).start()
        for r in range(rows):
            to_core(r).start()
            kept(r).start()
        mine = pl.ds(pl.multiple_of(s.dp * s.size, s.size), s.size)
        vectors[mine] = own_vectors[...]
        for k in range(1, s.lines):
            for t in range(3):
                s.along_z(t, k)
                s.over_x(t, k - 1)
            hidden_pump(k - 1)
        s.launch(3)
        for t in range(3):
            s.over_x(t, s.lines - 1)
        s.launch(4)
        for k in range(1, dp_count):
            vector_copy(k).wait()
        table[...] = jnp.transpose(vectors[...].astype(F32))[: table.shape[0]]
        for u in range(3):
            s.arrived(u)
            fetch(u).start()
        for u in range(3):
            fetch(u).wait()

    points(0)
    for r in range(rows):
        @pl.when(step == r)
        def _(r=r):
            kept(r).wait()
            to_core(r).wait_recv()
            passed_on(r).wait_recv()

    project_row(whole.at[step], own_hidden.at[0], weights.at[0], weights.at[1], weights.at[2], table,
                s_query.at[0], s_key.at[0], s_value.at[0], bounds_in.at[0], own_bounds.at[0])
    mask_row(segments, lengths, step, s.seq * block, bias, counted)
    count = s_query.shape[2] // GROUP
    for j in range(3):
        points(j + 1)
        attend_row(scale, table, teacher.at[0], s_query.at[0], s_key.at[0], s_value.at[0],
                   s_context.at[0], spread.at[0], probs.at[0], gaps.at[0], distill, bias, counted,
                   count * j // 3, count * (j + 1) // 3)

    @pl.when(step == rows - 1)
    def _():
        for u in range(3, UNITS):
            s.arrived(u)
        s.finish()
        for r in range(rows):
            to_chip(r).wait_send()
            to_core(r).wait_send()
            passed_on(r).wait_send()


def plain_kernel(
    scale, lengths, segments, whole, own_hidden, weights, table, teacher,
    s_query, s_key, s_value, s_context, spread, probs, gaps, bounds_in, own_bounds, distill, bias, counted,
):
    @pl.when(pl.program_id(0) == 0)
    def _():
        distill[...] = jnp.zeros_like(distill)

    project_row(whole.at[0], own_hidden.at[0], weights.at[0], weights.at[1], weights.at[2], table,
                s_query.at[0], s_key.at[0], s_value.at[0], bounds_in.at[0], own_bounds.at[0])
    mask_row(segments, lengths, pl.program_id(0), lax.axis_index("seq") * own_hidden.shape[1], bias, counted)
    attend_row(scale, table, teacher.at[0], s_query.at[0], s_key.at[0], s_value.at[0],
               s_context.at[0], spread.at[0], probs.at[0], gaps.at[0], distill, bias, counted, 0, s_query.shape[2] // GROUP)


def chain(stored, weights, arrivals, small, hidden, teacher, live, s_context, sums, final_out, grad_first_out,
          grad_ctx_out, pres, slopes, bounds):
    def vec(i):
        return small[i : i + 1]

    step = pl.program_id(0)

    def fetch(unit):
        return pltpu.make_async_copy(stored.at[3 + unit], weights.at[unit], arrivals.at[unit])

    def needed(unit):
        pass

    @pl.when(step == 0)
    def _():
        for unit in range(UNITS - 3):
            fetch(unit).start()
        for unit in range(UNITS - 3):
            fetch(unit).wait()

    def add(i, value):
        sums[i] += folded(value)

    width = hidden.shape[1]
    inputs = hidden[...].astype(F32)
    context = vec(A_V) * s_context[...] + vec(B_V)
    context_low = clip_parts(context, vec(C_CTX))[0]
    needed(0)
    s_out = dot_nt(context_low.astype(BF16), weights[0])
    normed, unit1, inverse1 = norm_parts(inputs + vec(A_O) * s_out + vec(B_O), vec(G1), vec(S1))
    normed_low, mid_slope, mid_bound = clip_parts(normed, vec(C_MID))
    normed_low = normed_low.astype(BF16)
    s_down = 0.0
    for i in range(4):
        needed(1 + 2 * i)
        s_up = dot_nt(normed_low, weights[1 + 2 * i])
        pres[i] = s_up
        pre = vec(A_U + i) * s_up + vec(B_U + i)
        phi = 0.5 + 0.5 * lax.erf(pre * (0.5**0.5))
        act_slope = phi + pre * (jnp.exp(-0.5 * pre * pre) * 0.3989422804014327)
        hidden_low, slope, bound = clip_parts(pre * phi, vec(C_HID + i))
        slopes[i] = (slope * act_slope)
        bounds[i] = bound
        needed(2 + 2 * i)
        s_down = s_down + dot_nt(hidden_low.astype(BF16), weights[2 + 2 * i])
    final, unit2, inverse2 = norm_parts(normed + vec(A_D) * s_down + vec(B_D), vec(G2), vec(S2))
    final_out[...] = final.astype(BF16)
    errors = jnp.where(live, final - teacher[...].astype(F32), 0.0)
    add(LOSS, errors * errors)
    add(G_G2, errors * unit2)
    add(G_S2, errors)
    grad_second = norm_back(errors, unit2, inverse2, vec(G2))
    add(G_D, grad_second * s_down)
    add(G_BD, grad_second)
    branch = (grad_second * vec(A_D)).astype(BF16)
    grad_mid = 0.0
    for i in range(4):
        grad_hid = dot_nn(branch, weights[2 + 2 * i])
        add(G_CHID + i, grad_hid * bounds[i])
        up_grad = grad_hid * slopes[i]
        add(G_BU + i, up_grad)
        add(G_U + i, up_grad * pres[i])
        grad_mid = grad_mid + dot_nn((up_grad * vec(A_U + i)).astype(BF16), weights[1 + 2 * i])
    add(G_CMID, grad_mid * mid_bound)
    grad_normed = grad_second + grad_mid * mid_slope
    add(G_G1, grad_normed * unit1)
    add(G_S1, grad_normed)
    grad_first = norm_back(grad_normed, unit1, inverse1, vec(G1))
    grad_first_out[...] = grad_first
    add(G_O, grad_first * s_out)
    add(G_BO, grad_first)
    grad_ctx_low = dot_nn((grad_first * vec(A_O)).astype(BF16), weights[0])
    unused, ctx_slope, ctx_bound = clip_parts(vec(A_V) * s_context[...] + vec(B_V), vec(C_CTX))
    add(G_CCTX, grad_ctx_low * ctx_bound)
    grad_ctx = grad_ctx_low * ctx_slope
    add(G_V, grad_ctx * s_context[...])
    add(G_BV, grad_ctx)
    grad_ctx_out[...] = grad_ctx


def attend_back_row(scale, small, s_query, s_key, s_value, s_context, spread, probs, gaps,
                    grad_ctx, key_grads, value_grads, query_grads):
    block, width = s_query.shape

    def some(index, carry):
        at = pl.ds(pl.multiple_of(index * GROUP, GROUP), GROUP)
        raw = small[A_Q : A_Q + 1, at] * s_query[:, at] + small[B_Q : B_Q + 1, at]
        query = stacked((raw * (small[A_K : A_K + 1, at] * scale)).astype(BF16))
        pulled = grad_ctx[:, at] * small[A_V : A_V + 1, at] * spread[:, at]
        product = pulled * s_context[:, at]
        lane = lax.broadcasted_iota(jnp.int32, product.shape, 1)
        deltas = [
            jnp.sum(jnp.where(lane // HEAD == h, product, 0.0), axis=-1, keepdims=True) for h in range(GROUP // HEAD)
        ]
        accum_grad = stacked(pulled.astype(BF16))
        prob_grad = dot_nt(accum_grad, s_value[:, at])
        score_grads, expos = [], []
        for head, delta in enumerate(deltas):
            expo = probs[GROUP // HEAD * index + head]
            expos.append(expo)
            mine = prob_grad[head * block : (head + 1) * block]
            score_grads.append(
                (expo.astype(F32) * (mine - delta) + gaps[GROUP // HEAD * index + head].astype(F32)).astype(BF16)
            )
        score_grad = jnp.concatenate(score_grads, axis=0)
        both = dot_nn(score_grad, s_key[:, at])
        query_grads[:, at] = (
            by_head([both[h * block : (h + 1) * block] for h in range(GROUP // HEAD)]) * scale
        )
        key_grads[:, at] = dot_tn(score_grad, query).astype(BF16)
        value_grads[:, at] = dot_tn(jnp.concatenate(expos, axis=0), accum_grad).astype(BF16)
        return carry

    lax.fori_loop(0, width // GROUP, some, 0, unroll=width // GROUP)


def chain_kernel(row_count, lengths, stored, small, hidden, teacher, s_context, final, grad_first, grad_ctx, sums_out,
                 weights, arrivals, sums, pres, slopes, bounds):
    step = pl.program_id(0)

    @pl.when(step == 0)
    def _():
        sums[...] = jnp.zeros_like(sums)

    flat = hidden.shape
    rows, block = row_count, flat[0] // row_count
    at = lax.broadcasted_iota(jnp.int32, flat, 0)
    limit = jnp.full(flat, lengths[step * rows], jnp.int32)
    for r in range(1, rows):
        limit = jnp.where(at < r * block, limit, lengths[step * rows + r])
    live = lax.axis_index("seq") * block + lax.rem(at, block) < limit
    chain(stored, weights, arrivals, small, hidden, teacher, live, s_context, sums, final, grad_first,
          grad_ctx, pres, slopes, bounds)

    @pl.when(step == pl.num_programs(0) - 1)
    def _():
        sums_out[...] = sums[...]


def back_kernel(scale, weights, small, s_query, s_key, s_value, s_context, spread, probs, gaps, grad_ctx,
                pulled_in, own_in, sums, key_grads, value_grads, query_grads):
    step = pl.program_id(0)

    @pl.when(step == 0)
    def _():
        sums[...] = jnp.zeros_like(sums)

    attend_back_row(scale, small, s_query.at[0], s_key.at[0], s_value.at[0],
                    s_context.at[0], spread.at[0], probs.at[0], gaps.at[0],
                    grad_ctx, key_grads, value_grads, query_grads)
    back = query_grads[...]
    raw = small[A_Q : A_Q + 1] * s_query[0] + small[B_Q : B_Q + 1]
    sums[0] += folded(raw * back)
    query_grad = back * small[A_K : A_K + 1]
    sums[1] += folded(query_grad * s_query[0])
    sums[2] += folded(query_grad)
    own_in[...] = dot_nn((query_grad * small[A_Q : A_Q + 1]).astype(BF16), weights[0])
    pulled_in[0] = (dot_nn(key_grads[...], weights[1]) + dot_nn(value_grads[...], weights[2])).astype(BF16)


def last_kernel(
    scale, dp_count, weights, table, s_query, s_key, s_value, s_context, spread, probs, gaps, grad_ctx,
    hidden, grad_first, bounds_in, own_bounds, chain_sums, distill,
    grad_input, early, late,
    query_grads, partial, kept, near, sent, far, sums,
    mine_a, slices_a, mine_b, slices_b, pieces, pieces_b,
    near_sems, far_sems, a_sems, b_sems,
):
    step = pl.program_id(0)
    rows = partial.shape[1]
    block, width = s_query.shape[1], s_query.shape[2]
    size = width // dp_count
    dp, seq = lax.axis_index("dp"), lax.axis_index("seq")
    yi, ci = seq // 2, seq % 2
    across, beside = (1 - yi) * 2 + ci, yi * 2 + 1 - ci
    corner = (1 - yi) * 2 + 1 - ci
    peers = (across, beside, corner)

    def positions(place):
        return pl.ds(pl.multiple_of(place * block, block), block)

    def near_copy(r, kind, which):
        place = beside if which == 0 else corner
        return remote(partial.at[kind, r, positions(place)], near.at[kind, r, which], near_sems.at[0, kind, r, which],
                      near_sems.at[1, kind, r, which], dp, beside)

    def far_copy(r):
        return remote(sent.at[r], far.at[r], far_sems.at[0, r], far_sems.at[1, r], dp, across)

    def scatter(mine, slices, sems, k):
        to = lax.rem(dp + k, dp_count)
        return remote(mine.at[to], slices.at[k], sems.at[0, k], sems.at[1, k], to, seq)

    def scatter_done(mine, slices, sems):
        total = mine[dp]
        for k in range(1, dp_count):
            scatter(mine, slices, sems, k).wait()
            total = total + slices[k]
        return total

    def swap(pieces, sems, k):
        return remote(pieces.at[0], pieces.at[k], sems.at[0, dp_count + k - 1], sems.at[1, dp_count + k - 1], dp, peers[k - 1])

    def swap_done(pieces, sems):
        total = pieces[0]
        for k in range(1, 4):
            swap(pieces, sems, k).wait()
            total = total + pieces[k]
        return total

    @pl.when(step == 0)
    def _():
        sums[...] = jnp.zeros_like(sums)
        barrier = pltpu.get_barrier_semaphore()
        for k in range(1, dp_count):
            pl.semaphore_signal(barrier, inc=1, device_id=(lax.rem(dp + k, dp_count), seq), device_id_type=MESH)
        for peer in peers:
            pl.semaphore_signal(barrier, inc=1, device_id=(dp, peer), device_id_type=MESH)
        pl.semaphore_wait(barrier, dp_count + 2)
        columns_of = [jnp.sum(chain_sums[i], axis=0, keepdims=True) for i in range(LOSS)]
        objective = 0.5 * jnp.sum(chain_sums[LOSS]) + 0.5 * SCORE_WEIGHT * jnp.sum(distill[...])
        columns_of.append(jnp.full((1, width), objective, F32))
        columns_of.append(jnp.zeros((PAIR - len(columns_of), width), F32))
        mine_a[...] = jnp.transpose(jnp.concatenate(columns_of, axis=0)).reshape(mine_a.shape)
        for k in range(1, dp_count):
            scatter(mine_a, slices_a, a_sems, k).start()

    @pl.when(step == 2)
    def _():
        pieces[0] = scatter_done(mine_a, slices_a, a_sems)
        for k in range(1, 4):
            swap(pieces, a_sems, k).start()

    @pl.when(step == 4)
    def _():
        early[...] = swap_done(pieces, a_sems)

    def joined(kind, r, which, place):
        near_copy(r, kind, which).wait_recv()
        return (partial[kind, r, positions(place)].astype(F32) + near[kind, r, which].astype(F32)).astype(BF16)

    def hand_over(r):
        low = None
        for kind in range(2):
            both = jnp.concatenate([joined(kind, r, 1, across), joined(kind, r, 0, seq)], axis=0)
            part = dot_nn(both, weights[1 + kind])
            low = part if low is None else low + part
        sent[r] = low[:block].astype(BF16)
        far_copy(r).start()
        kept[r] = kept[r] + low[block:]
        sums[3] += folded(low[:block] * bounds_in[0, positions(across)].astype(F32))
        sums[3] += folded(low[block:] * bounds_in[0, positions(seq)].astype(F32))

    def settle(r):
        far_copy(r).wait_recv()
        grad_low = kept[r] + far[r].astype(F32)
        unused, slope, bound = clip_parts(hidden[0].astype(F32), table[C_IN : C_IN + 1])
        grad_input[0] = grad_first[...] + grad_low * slope

    @pl.when(step < rows)
    def _():
        attend_back_row(scale, table, s_query.at[0], s_key.at[0], s_value.at[0],
                        s_context.at[0], spread.at[0], probs.at[0], gaps.at[0],
                        grad_ctx, partial.at[0, step], partial.at[1, step], query_grads)
        for kind in range(2):
            near_copy(step, kind, 1).start()
        for kind in range(2):
            near_copy(step, kind, 0).start()
        back = query_grads[...]
        raw = table[A_Q : A_Q + 1] * s_query[0] + table[B_Q : B_Q + 1]
        sums[0] += folded(raw * back)
        query_grad = back * table[A_K : A_K + 1]
        sums[1] += folded(query_grad * s_query[0])
        sums[2] += folded(query_grad)
        kept[step] = dot_nn((query_grad * table[A_Q : A_Q + 1]).astype(BF16), weights[0])
        sums[3] += folded(kept[step] * own_bounds[0].astype(F32))

    @pl.when((step > 0) & (step <= rows))
    def _():
        hand_over(step - 1)

    @pl.when(step == rows)
    def _():
        columns_of = [jnp.sum(sums[i], axis=0, keepdims=True) for i in range(4)]
        columns_of.append(jnp.zeros((PAIR - len(columns_of), width), F32))
        turned = jnp.transpose(jnp.concatenate(columns_of, axis=0))
        for k in range(dp_count):
            part = jnp.transpose(turned[k * size : (k + 1) * size])[:8]
            mine_b[k] = jnp.concatenate([part, jnp.zeros((8, PAIR - size), F32)], axis=1)
        for k in range(1, dp_count):
            scatter(mine_b, slices_b, b_sems, k).start()

    @pl.when(step > 2)
    def _():
        settle(step - 3)

    @pl.when(step == rows)
    def _():
        pieces_b[0] = scatter_done(mine_b, slices_b, b_sems)
        for k in range(1, 4):
            swap(pieces_b, b_sems, k).start()

    @pl.when(step == pl.num_programs(0) - 1)
    def _():
        for r in range(rows):
            for kind in range(2):
                near_copy(r, kind, 0).wait_send()
                near_copy(r, kind, 1).wait_send()
            far_copy(r).wait_send()
        late[...] = swap_done(pieces_b, b_sems)


def finish_kernel(early, late, *refs):
    latents, grads, vectors = refs[:6], refs[6:12], refs[12:]
    size = early.shape[0]
    first, second = jnp.transpose(early[...]), late[...]
    turned = jnp.transpose(jnp.concatenate([second] * (PAIR // 8), axis=0))[:size]

    def row(value, i):
        return value[i : i + 1, :size]

    sums = [turned[:, 1:2], turned[:, 0:1], early[:, G_V : G_V + 1], early[:, G_O : G_O + 1], None, early[:, G_D : G_D + 1]]
    lane = lax.broadcasted_iota(jnp.int32, (4 * size, PAIR), 1)
    wide = jnp.zeros((4 * size, PAIR), F32)
    for m in range(3):
        column = jnp.concatenate([early[:, G_U + 4 * m + i : G_U + 4 * m + i + 1] for i in range(4)], axis=0)
        wide = jnp.where(lane == m, column, wide)
    wide = jnp.transpose(wide)
    sums[4] = wide[0:1]
    for i, (latent, grad, total) in enumerate(zip(latents, grads, sums)):
        grad[...] = signed(latent[...]) * (total / latent.shape[0 if i == 4 else 1])
    loss, given = vectors[-1], vectors[:-1]
    loss[...] = jnp.broadcast_to(row(first, LOSS), loss.shape)
    parts = [row(second, 2), row(first, G_BV), row(first, G_BO), wide[1:2], row(first, G_BD), row(first, G_G1),
             row(first, G_S1), row(first, G_G2), row(first, G_S2), row(second, 3), row(first, G_CCTX), row(first, G_CMID),
             wide[2:3]]
    for ref, part in zip(given, parts):
        ref[...] = part[0]


def signs_and_scale(latent):
    scale = jnp.mean(jnp.abs(latent), axis=0).astype(BF16)
    return jnp.sign(latent).astype(BF16).T, scale


def body(
    hidden_in,
    segment_ids,
    row_lengths,
    teacher_scores,
    teacher_hidden,
    w_query,
    w_key,
    w_value,
    w_out,
    w_up,
    w_down,
    b_query,
    b_value,
    b_out,
    b_up,
    b_down,
    norm1_gain,
    norm1_bias,
    norm2_gain,
    norm2_bias,
    clip_in,
    clip_ctx,
    clip_mid,
    clip_hid,
):
    rows, block, width = hidden_in.shape
    heads = teacher_scores.shape[1]
    head_dim = width // heads
    seq_len = segment_ids.shape[1]
    tokens = rows * block
    scale = head_dim ** (-0.5)
    place = lax.axis_index("seq")
    first = place * block

    dp_count = lax.axis_size("dp")
    size = w_query.shape[1]
    tuned = dp_count == 8 and rows == 8 and size % 32 == 0 and lax.axis_size("seq") == 4
    given = jnp.stack([b_query, b_value, b_out, b_down, norm1_gain, norm1_bias, norm2_gain, norm2_bias, clip_in, clip_ctx, clip_mid])
    given_wide = jnp.stack([b_up, clip_hid])

    def row_spec(*shape):
        return pl.BlockSpec((1,) + shape, lambda i: (i,) + (0,) * len(shape))

    def whole(array):
        return pl.BlockSpec(array.shape, lambda i: (0,) * array.ndim, pipeline_mode=pl.Buffered(1))

    three = pl.BlockSpec((3, width, width), lambda i: (0, 0, 0), pipeline_mode=pl.Buffered(1))
    attend_specs = [row_spec(block, width), row_spec(seq_len, width), row_spec(seq_len, width), row_spec(block, width),
                    row_spec(block, width), row_spec(heads, block, seq_len), row_spec(heads, block, seq_len),
                    row_spec(seq_len, width), row_spec(block, width), pl.BlockSpec((8, seq_len), lambda i: (0, 0))]
    attend_shapes = [jax.ShapeDtypeStruct((rows, block, width), F32),
                     jax.ShapeDtypeStruct((rows, seq_len, width), BF16),
                     jax.ShapeDtypeStruct((rows, seq_len, width), BF16),
                     jax.ShapeDtypeStruct((rows, block, width), F32),
                     jax.ShapeDtypeStruct((rows, block, width), F32),
                     jax.ShapeDtypeStruct((rows, heads, block, seq_len), BF16),
                     jax.ShapeDtypeStruct((rows, heads, block, seq_len), BF16),
                     jax.ShapeDtypeStruct((rows, seq_len, width), BF16),
                     jax.ShapeDtypeStruct((rows, block, width), BF16),
                     jax.ShapeDtypeStruct((8, seq_len), F32)]
    teacher_spec = row_spec(heads, block, seq_len)
    scalars = pl.BlockSpec(memory_space=pltpu.SMEM)
    latents = (w_query.T, w_key.T, w_value.T, w_out.T, w_up, w_down.T)
    anywhere = pl.BlockSpec(memory_space=pl.ANY)
    lines = dp_count // 2
    sems = pltpu.SemaphoreType.DMA
    if tuned:
        full, table, s_query, s_key, s_value, s_context, spread, probs, gaps, bounds_in, own_bounds, distill = pl.pallas_call(
            functools.partial(first_kernel, scale, dp_count),
            grid=(rows,),
            in_specs=[scalars, whole(segment_ids)] + [whole(w) for w in latents] + [whole(given), whole(given_wide), anywhere,
                      row_spec(block, width), teacher_spec],
            out_specs=[anywhere, pl.BlockSpec((VECTORS, width), lambda i: (0, 0))] + attend_specs,
            out_shape=[jax.ShapeDtypeStruct((UNITS, width, width), BF16), jax.ShapeDtypeStruct((VECTORS, width), F32)]
            + attend_shapes,
            scratch_shapes=[
                pltpu.VMEM((UNITS, size, width), BF16), pltpu.VMEM((size, PAIR), F32), pltpu.VMEM((size, PAIR), BF16),
                pltpu.VMEM((rows, seq_len, width), BF16), pltpu.VMEM((width, PAIR), BF16), pltpu.VMEM((3, width, width), BF16),
                sems((2, UNITS)), sems((UNITS, lines)), sems((UNITS, lines)), sems((2, 2 * len(SHARED))),
                sems((2, UNITS)), sems((UNITS,)), sems((2, 3, rows)), sems((rows,)), sems((2, dp_count)), sems((3,)),
                pltpu.VMEM((block, seq_len), F32), pltpu.VMEM((block, seq_len), F32),
            ],
            compiler_params=pltpu.CompilerParams(collective_id=0, has_side_effects=True, vmem_limit_bytes=60 * 2**20),
        )(row_lengths, segment_ids, *latents, given, given_wide, hidden_in, hidden_in, teacher_scores)
    else:
        square = [signs_and_scale(w) for w in (w_query, w_key, w_value, w_out)]
        up_signs, up_scale = signs_and_scale(w_up)
        down = w_down.reshape(dp_count, 4, size, size)
        down_signs = jnp.sign(down).astype(BF16).transpose(1, 3, 0, 2).reshape(4, size, width)
        down_scale = jnp.mean(jnp.abs(w_down), axis=0).astype(BF16)
        pairs = jnp.stack([up_signs.reshape(4, size, width), down_signs], axis=1).reshape(8, size, width)
        own = jnp.concatenate([jnp.stack([s for s, _ in square]), pairs])
        own_vectors = jnp.concatenate(
            [jnp.stack([*(a for _, a in square), down_scale, b_query, b_value, b_out, b_down, norm1_gain, norm1_bias,
                        norm2_gain, norm2_bias, clip_in, clip_ctx, clip_mid]),
             up_scale.reshape(4, size), b_up.reshape(4, size), clip_hid.reshape(4, size)]
        )
        own_vectors = jnp.pad(own_vectors.T, ((0, 0), (0, PAIR - own_vectors.shape[0])))

        full = lax.all_gather(own, "dp", axis=1, tiled=True)
        table = lax.all_gather(own_vectors, "dp", axis=0, tiled=True).astype(F32).T[:VECTORS]
        hidden_full = lax.all_gather(hidden_in, "seq", axis=1, tiled=True)
        s_query, s_key, s_value, s_context, spread, probs, gaps, bounds_in, own_bounds, distill = pl.pallas_call(
            functools.partial(plain_kernel, scale),
            grid=(rows,),
            in_specs=[scalars, whole(segment_ids), row_spec(seq_len, width), row_spec(block, width), three, whole(table),
                      teacher_spec],
            out_specs=attend_specs,
            out_shape=attend_shapes,
            scratch_shapes=[pltpu.VMEM((block, seq_len), F32), pltpu.VMEM((block, seq_len), F32)],
            compiler_params=pltpu.CompilerParams(vmem_limit_bytes=60 * 2**20),
        )(row_lengths, segment_ids, hidden_full, hidden_in, full, table, teacher_scores)

    group = 2
    def group_spec(*shape):
        return pl.BlockSpec((group,) + shape, lambda i: (i,) + (0,) * len(shape))
    flat_spec = pl.BlockSpec((group * block, width), lambda i: (i, 0))
    def flat_spec(buffers):
        return pl.BlockSpec((group * block, width), lambda i: (i, 0), pipeline_mode=pl.Buffered(buffers))

    final, grad_first, grad_ctx, sums = pl.pallas_call(
        functools.partial(chain_kernel, group),
        grid=(rows // group,),
        in_specs=[scalars, pl.BlockSpec(memory_space=pl.ANY), whole(table), flat_spec(2), flat_spec(2), flat_spec(2)],
        out_specs=[flat_spec(2), flat_spec(2), flat_spec(2),
                   pl.BlockSpec((SUMS, 8, width), lambda i: (0, 0, 0))],
        out_shape=[jax.ShapeDtypeStruct((tokens, width), BF16),
                   jax.ShapeDtypeStruct((tokens, width), F32),
                   jax.ShapeDtypeStruct((tokens, width), F32),
                   jax.ShapeDtypeStruct((SUMS, 8, width), F32)],
        scratch_shapes=[pltpu.VMEM((UNITS - 3, width, width), BF16), pltpu.SemaphoreType.DMA((UNITS - 3,)),
                        pltpu.VMEM((SUMS, 8, width), F32)]
        + [pltpu.VMEM((4, group * block, width), F32)] * 3,
        compiler_params=pltpu.CompilerParams(vmem_limit_bytes=63 * 2**20),
    )(row_lengths, full, table, hidden_in.reshape(tokens, width), teacher_hidden.reshape(tokens, width),
      s_context.reshape(tokens, width))
    if tuned:
        def now_spec(*shape):
            return pl.BlockSpec((1,) + shape, lambda i: (jnp.minimum(i, rows - 1),) + (0,) * len(shape))

        def then_spec(*shape):
            return pl.BlockSpec((1,) + shape, lambda i: (jnp.maximum(i - 3, 0),) + (0,) * len(shape))

        own_spec = now_spec(block, width)
        grad_input, early, late = pl.pallas_call(
            functools.partial(last_kernel, scale, dp_count),
            grid=(rows + 3,),
            in_specs=[three, whole(table), now_spec(block, width), now_spec(seq_len, width), now_spec(seq_len, width),
                      now_spec(block, width), now_spec(block, width), now_spec(heads, block, seq_len),
                      now_spec(heads, block, seq_len), pl.BlockSpec((block, width), lambda i: (jnp.minimum(i, rows - 1), 0)),
                      then_spec(block, width), pl.BlockSpec((block, width), lambda i: (jnp.maximum(i - 3, 0), 0)),
                      pl.BlockSpec((1, seq_len, width), lambda i: (jnp.clip(i - 1, 0, rows - 1), 0, 0)),
                      own_spec, whole(sums), whole(distill)],
            out_specs=[then_spec(block, width), pl.BlockSpec((size, PAIR), lambda i: (0, 0)), pl.BlockSpec((8, PAIR), lambda i: (0, 0))],
            out_shape=[jax.ShapeDtypeStruct((rows, block, width), F32), jax.ShapeDtypeStruct((size, PAIR), F32),
                       jax.ShapeDtypeStruct((8, PAIR), F32)],
            scratch_shapes=[
                pltpu.VMEM((block, width), F32),
                pltpu.VMEM((2, rows, seq_len, width), BF16), pltpu.VMEM((rows, block, width), F32),
                pltpu.VMEM((2, rows, 2, block, width), BF16), pltpu.VMEM((rows, block, width), BF16),
                pltpu.VMEM((rows, block, width), BF16), pltpu.VMEM((4, 8, width), F32),
                pltpu.VMEM((dp_count, size, PAIR), F32), pltpu.VMEM((dp_count, size, PAIR), F32),
                pltpu.VMEM((dp_count, 8, PAIR), F32), pltpu.VMEM((dp_count, 8, PAIR), F32),
                pltpu.VMEM((4, size, PAIR), F32), pltpu.VMEM((4, 8, PAIR), F32),
                sems((2, 2, rows, 2)), sems((2, rows)), sems((2, dp_count + 3)), sems((2, dp_count + 3)),
            ],
            compiler_params=pltpu.CompilerParams(collective_id=1, has_side_effects=True, vmem_limit_bytes=60 * 2**20),
        )(full, table, s_query, s_key, s_value, s_context, spread, probs, gaps, grad_ctx, hidden_in, grad_first, bounds_in, own_bounds, sums, distill)
        def one_block(shape):
            return pl.BlockSpec(shape, lambda: (0,) * len(shape))

        small_shapes = [w.shape for w in (b_query, b_value, b_out, b_up, b_down, norm1_gain, norm1_bias, norm2_gain,
                                                  norm2_bias, clip_in, clip_ctx, clip_mid, clip_hid)]
        results = pl.pallas_call(
            finish_kernel,
            in_specs=[one_block(early.shape), one_block(late.shape)] + [one_block(w.shape) for w in latents],
            out_specs=[one_block(w.shape) for w in latents] + [one_block(shape) for shape in small_shapes] + [one_block((1, size))],
            out_shape=[jax.ShapeDtypeStruct(w.shape, F32) for w in latents]
            + [jax.ShapeDtypeStruct(shape, F32) for shape in small_shapes]
            + [jax.ShapeDtypeStruct((1, size), F32)],
            compiler_params=pltpu.CompilerParams(vmem_limit_bytes=60 * 2**20),
        )(early, late, *latents)
        loss = results[-1][0, 0] / (dp_count * rows * seq_len)
        return (
            (final.reshape(rows, block, width), loss, grad_input.reshape(rows, block, width))
            + tuple(grad if i == 4 else grad.T for i, grad in enumerate(results[:6]))
            + tuple(results[6:-1])
        )
    else:
        one_spec = pl.BlockSpec((block, width), lambda i: (i, 0))
        pulled_in, own_in, more = pl.pallas_call(
            functools.partial(back_kernel, scale),
            grid=(rows,),
            in_specs=[three, whole(table),
                      row_spec(block, width), row_spec(seq_len, width), row_spec(seq_len, width), row_spec(block, width),
                      row_spec(block, width), row_spec(heads, block, seq_len), row_spec(heads, block, seq_len), one_spec],
            out_specs=[row_spec(seq_len, width), one_spec, pl.BlockSpec((3, 8, width), lambda i: (0, 0, 0))],
            out_shape=[jax.ShapeDtypeStruct((rows, seq_len, width), BF16),
                       jax.ShapeDtypeStruct((tokens, width), F32),
                       jax.ShapeDtypeStruct((3, 8, width), F32)],
            scratch_shapes=[pltpu.VMEM((seq_len, width), BF16), pltpu.VMEM((seq_len, width), BF16),
                            pltpu.VMEM((block, width), F32)],
            compiler_params=pltpu.CompilerParams(vmem_limit_bytes=60 * 2**20),
        )(full, table, s_query, s_key, s_value, s_context, spread, probs, gaps, grad_ctx)
        sums = sums.at[G_K].set(more[0]).at[G_Q].set(more[1]).at[G_BQ].set(more[2])
        objective = 0.5 * jnp.sum(sums[LOSS]) + 0.5 * SCORE_WEIGHT * jnp.sum(distill)

        crossed = lax.psum_scatter(pulled_in, "seq", scatter_dimension=1, tiled=True).astype(F32)
        grad_low = own_in + crossed.reshape(tokens, width)
        inputs = hidden_in.astype(F32).reshape(tokens, width)
        unused, in_slope, in_bound = clip_parts(inputs, table[C_IN : C_IN + 1])
        grad_input = grad_first + grad_low * in_slope
        sums = jnp.sum(sums, axis=1)
        wide_sums = sums[16:28]
        sums = sums[:16].at[G_CIN].set(columns(grad_low * in_bound)[0])
        sums, wide_sums, objective = lax.psum((sums, wide_sums, objective), ("dp", "seq"))
        at = lax.axis_index("dp")
        sums = lax.dynamic_slice_in_dim(sums, at * size, size, 1)
        wide_sums = lax.dynamic_slice_in_dim(wide_sums, at * size, size, 1).reshape(3, 4 * size)
    loss = objective / (lax.axis_size("dp") * rows * seq_len)
    grads = [
        jnp.sign(w) * (s / w.shape[0])
        for w, s in zip(
            (w_query, w_key, w_value, w_out, w_up, w_down),
            (sums[0], sums[1], sums[2], sums[3], wide_sums[0], sums[4]),
        )
    ]
    return (
        final.reshape(rows, block, width).astype(BF16),
        loss,
        grad_input.reshape(rows, block, width),
        *grads,
        sums[5],
        sums[6],
        sums[7],
        wide_sums[1],
        sums[8],
        sums[9],
        sums[10],
        sums[11],
        sums[12],
        sums[13],
        sums[14],
        sums[15],
        wide_sums[2],
    )


def solution(mesh):
    rows = P("dp", "seq", None)
    cols = P(None, "dp")
    vec = P("dp")
    return jax.shard_map(
        body,
        mesh=mesh,
        in_specs=(rows, P("dp", None), vec, P("dp", None, "seq", None), rows)
        + (cols,) * 6
        + (vec,) * 13,
        out_specs=(rows, P(), rows) + (cols,) * 6 + (vec,) * 13,
        check_vma=False,
    )
```
